128 devices in a mesh: gx: 32 (over z, x_hi, y), gy: 4 (over x_lo, core).
Axes of the slice: x: 4 (x_hi: 2, x_lo: 2; x = x_hi * 2 + x_lo), y: 4, z: 4, core: 2. Of those that a mesh axis runs over, the one named last changes fastest.
Arguments:
- temp_start: float32 [8, 2048, 4096], P(None, 'gx', 'gy'), may hold values from -6 to 6
- conduct: float32 [2048, 4096], P('gx', 'gy'), may hold values from 0.2 to 1
- adjoint_in: float32 [8, 2048, 4096], P(None, 'gx', 'gy'), may hold values from -6 to 6
- grad_in: float32 [2048, 4096], P('gx', 'gy'), may hold values from -6 to 6
- observed: float32 [4, 8192, 1024], P(None, ('gx', 'gy')), may hold values from -6 to 6
- frame_index: int32 [8192], P(('gx', 'gy')), may hold values from 0 to 3
- source_map: int32 [8192, 4], P(('gx', 'gy')), may hold values from 0 to 8191, as said below
- source_weight: float32 [8192, 4], P(('gx', 'gy')), may hold values from 0.2 to 0.6
Outputs:
- misfit: float32 [8192, 1024], P(('gx', 'gy'))
- adjoint_out: float32 [8, 2048, 4096], P(None, 'gx', 'gy')
- grad_out: float32 [2048, 4096], P('gx', 'gy')
The draws below stay inside these ranges and needn't reach their ends.
Inputs may be any that keep to these rules, and one draw needn't show every extreme that they name: `source_map`: each camera tile's blocks lie in plate tiles of devices with the same gy index as the device that holds the camera tile. Of the 256 blocks of one device's camera tiles, at most 16 lie on any one plate device, and exactly 16 on each of 8 of them.
All inputs are finite; a program needn't handle non-finite values.
Results may differ from the reference program's by a relative error of at most 0.00008.
Values sent between devices are 32-bit elements; how exact they have to be, the bound alone decides.
A program may use at most 64 MiB of HBM per device.

```python
import math
import jax
import jax.numpy as jnp
from jax import lax

CX = 64
CY = 1024
L = 8
TR = 8
TC = 128
K = 4
NF = 4
CT_DEV = 64
CAP = 16
NX = 2048
NY = 4096
NT = 8192
N_GX = 32
N_GY = 4


def draw_source_map(key, part):
    key = jax.random.fold_in(key, 11)
    request = jnp.arange(K * CT_DEV)
    half_count = K * CT_DEV // 2
    remaining = N_GX - N_GX // 4
    group_index = jnp.where(request < half_count, request // CAP, N_GX // 4 + (request - half_count) % remaining)

    def one_device(device):
        device_key = jax.random.fold_in(key, device)
        key_order = jax.random.fold_in(device_key, 1)
        key_slots = jax.random.fold_in(device_key, 2)
        key_tiles = jax.random.fold_in(device_key, 3)
        shuffled = jax.random.permutation(key_order, N_GX)
        target = shuffled[group_index]
        slot_order = jax.random.permutation(key_slots, K * CT_DEV)
        local_tile = jax.random.randint(key_tiles, (K * CT_DEV,), 0, CT_DEV)
        column = device % N_GY
        global_tile = ((target * N_GY + column) * CT_DEV + local_tile).astype(jnp.int32)
        return jnp.zeros((K * CT_DEV,), jnp.int32).at[slot_order].set(global_tile)
    full_table = jax.vmap(one_device)(jnp.arange(N_GX * N_GY))
    return full_table.reshape(N_GX * N_GY * CT_DEV, K)


def place_ends(result, stream_key, smallest, largest):
    spot = [jax.random.randint(jax.random.fold_in(stream_key, axis), (), 0, length) for axis, length in enumerate(result.shape)]
    main_axis = result.shape.index(max(result.shape))
    neighbour = spot[:main_axis] + [(spot[main_axis] + 1) % result.shape[main_axis]] + spot[main_axis + 1:]
    return result.at[tuple(spot)].set(smallest).at[tuple(neighbour)].set(largest)


def shard_levels(stream_key, extent, shards, smallest, high):
    def one(position, blocks):
        steps = jax.random.uniform(jax.random.fold_in(jax.random.fold_in(stream_key, 6), position), (blocks,), jnp.float32, smallest / len(shards), high / len(shards))
        return jnp.repeat(jnp.exp(steps), extent[position] // blocks).reshape((-1,) + (1,) * (len(extent) - position - 1))

    factor_of = one(*shards[0])
    for cut in shards[1:]:
        factor_of = factor_of * one(*cut)
    return factor_of


def gaussian(rng, extent, width, limit, cuts=(), held_as=jnp.bfloat16):
    gain = shard_levels(rng, extent, cuts, -0.22, 0.18) if cuts else 1.0
    values = jax.random.normal(rng, extent, jnp.float32) * width * gain
    return jnp.minimum(jnp.maximum(values, -limit), limit).astype(held_as)


def setup_inputs(seed: int = 0) -> dict:
    key_list = jax.random.split(jax.random.key(seed), 9)
    return {
        "temp_start": gaussian(key_list[0], (L, NX, NY), 1.0, 6.0, ((1, 32), (2, 4)), jnp.float32),
        "conduct": jnp.clip(jnp.exp(math.log(1.0) - 1.609438 * jax.random.uniform(key_list[1], (NX, NY), jnp.float32) ** shard_levels(key_list[1], (NX, NY), ((0, 32), (1, 4)), -0.2, 0.2)), 0.2, 1.0),
        "adjoint_in": gaussian(key_list[2], (L, NX, NY), 0.5, 6.0, ((1, 32), (2, 4)), jnp.float32),
        "grad_in": gaussian(key_list[3], (NX, NY), 0.5, 6.0, ((0, 32), (1, 4)), jnp.float32),
        "observed": gaussian(key_list[4], (NF, NT, TR * TC), 1.0, 6.0, ((1, 128),), jnp.float32),
        "frame_index": place_ends(jax.random.randint(key_list[5], (NT,), 0, NF), jax.random.fold_in(key_list[5], 1), 0, NF - 1).astype(jnp.int32),
        "source_map": draw_source_map(jax.random.fold_in(key_list[8], 71), 0),
        "source_weight": jnp.clip(0.2 + 0.400000021 * jax.random.uniform(key_list[7], (NT, K), jnp.float32) ** shard_levels(key_list[7], (NT, K), ((0, 128),), -0.2, 0.2), 0.2, 0.6),
    }


RATE_PLANE = 0.2
RATE_VERTICAL = 0.08

def plane_term(fpad, kpad):
    centre = fpad[..., 1:-1, 1:-1]
    kcentre = kpad[1:-1, 1:-1]
    total = jnp.zeros(centre.shape, jnp.float32)
    total = total + 0.5 * (kcentre + kpad[2:, 1:-1]) * (fpad[..., 2:, 1:-1] - centre)
    total = total + 0.5 * (kcentre + kpad[:-2, 1:-1]) * (fpad[..., :-2, 1:-1] - centre)
    total = total + 0.5 * (kcentre + kpad[1:-1, 2:]) * (fpad[..., 1:-1, 2:] - centre)
    total = total + 0.5 * (kcentre + kpad[1:-1, :-2]) * (fpad[..., 1:-1, :-2] - centre)
    return total

def vertical(field):
    zero_layer = jnp.zeros(field[:1].shape, jnp.float32)
    lower = jnp.concatenate([field[1:] - field[:-1], zero_layer], axis=0)
    upper = jnp.concatenate([zero_layer, field[:-1] - field[1:]], axis=0)
    return RATE_VERTICAL * (lower + upper)

def face_grad(tpad, lpad):
    tcen = tpad[:, 1:-1, 1:-1]
    lcen = lpad[:, 1:-1, 1:-1]
    total = jnp.zeros(tcen.shape, jnp.float32)
    total = total + 0.5 * (tpad[:, 2:, 1:-1] - tcen) * (lcen - lpad[:, 2:, 1:-1])
    total = total + 0.5 * (tpad[:, :-2, 1:-1] - tcen) * (lcen - lpad[:, :-2, 1:-1])
    total = total + 0.5 * (tpad[:, 1:-1, 2:] - tcen) * (lcen - lpad[:, 1:-1, 2:])
    total = total + 0.5 * (tpad[:, 1:-1, :-2] - tcen) * (lcen - lpad[:, 1:-1, :-2])
    return lax.optimization_barrier(jnp.sum(total, axis=0))

def pad_layers(field):
    return jnp.pad(field, ((0, 0), (1, 1), (1, 1)))

def to_tiles(plane):
    shaped = plane.reshape(N_GX, CX // TR, TR, N_GY, CY // TC, TC)
    return shaped.transpose(0, 3, 1, 4, 2, 5).reshape(NT, TR * TC)

def from_tiles(tiles):
    shaped = tiles.reshape(N_GX, N_GY, CX // TR, CY // TC, TR, TC)
    return shaped.transpose(0, 2, 4, 1, 3, 5).reshape(NX, NY)

def reference(temp_start, conduct, adjoint_in, grad_in, observed, frame_index, source_map, source_weight):
    kpad = jnp.pad(conduct, 1)
    top_now = temp_start[-1]
    top_next = top_now + RATE_PLANE * plane_term(jnp.pad(top_now, 1), kpad) + RATE_VERTICAL * (temp_start[-2] - top_now)
    tiles = to_tiles(top_next)
    seen = tiles[source_map]
    predicted = lax.optimization_barrier(jnp.sum(source_weight[:, :, None] * seen, axis=1))
    frame_obs = observed[frame_index, jnp.arange(NT, dtype=jnp.int32)]
    misfit = predicted - frame_obs
    contrib = source_weight[:, :, None] * misfit[:, None, :]
    added = jax.ops.segment_sum(contrib.reshape(NT * K, TR * TC), source_map.reshape(NT * K), num_segments=NT)
    adjoint_next = adjoint_in.at[-1].add(from_tiles(added))
    adj_pad = pad_layers(adjoint_next)
    adjoint_out = adjoint_next + RATE_PLANE * plane_term(adj_pad, kpad) + vertical(adjoint_next)
    grad_out = grad_in + RATE_PLANE * face_grad(pad_layers(temp_start), adj_pad)
    return (misfit, adjoint_out, grad_out)
```

```python
import jax
import jax.numpy as jnp
from jax import lax
from jax.experimental import pallas as pl
from jax.experimental.pallas import tpu as pltpu
from jax.sharding import PartitionSpec as P

TR = 8
TC = 128
CAP = 16
LANES = 128
RATE_PLANE = 0.2
RATE_VERTICAL = 0.08
MESH = pl.DeviceIdType.MESH
F32 = jnp.float32
BF16 = jnp.bfloat16


def iota(shape, dim):
    return lax.broadcasted_iota(jnp.int32, shape, dim)


def two_parts(x):
    hi = x.astype(BF16)
    lo = (x - hi.astype(F32)).astype(BF16)
    return hi, lo


def three_parts(x):
    hi = x.astype(BF16)
    rest = x - hi.astype(F32)
    mid = rest.astype(BF16)
    lo = (rest - mid.astype(F32)).astype(BF16)
    return hi, mid, lo


RING = 4
PLANE = RING * RING
ORDER = (
    ((2, 2), (2, 2)), ((2, 0), (0, 2)), ((0, 2), (2, 0)),
    ((2, 1), (2, 3)), ((1, 2), (3, 2)), ((2, 3), (2, 1)), ((3, 2), (1, 2)),
    ((1, 1), (3, 3)), ((1, 3), (3, 1)), ((3, 3), (1, 1)), ((3, 1), (1, 3)),
    ((0, 1), (0, 3)), ((1, 0), (3, 0)), ((0, 3), (0, 1)), ((3, 0), (1, 0)),
)


def make_kernel(n_gx, n_gy, layers, rows, cols, frames, k_blocks):
    tiles = (rows // TR) * (cols // TC)
    half = PLANE * CAP
    n_slots = 2 * half
    row0, col0 = TR, LANES
    row1, col1 = row0 + rows, col0 + cols
    strips = rows // TR
    tile_cols = cols // TC
    top = layers - 1
    per_group = LANES // CAP
    groups = PLANE // per_group
    order = [tuple(dz * RING + dy for dz, dy in pair) for pair in ORDER]
    others = range(1, PLANE)

    def kernel(
        temp, cond, adj, grad, obs, frame_ref, map_ref, weight_ref,
        misfit_out, adj_out, grad_out,
        tpad, apad, kpad, gin, obs_v, coef, gacc, outv, misv, gradv,
        ns0_send, ns0_recv, ew0_send, ew0_recv,
        ns_send, ns_recv, ew_send, ew_recv,
        ns2_send, ns2_recv, ew2_send, ew2_recv,
        req_send, req_recv, tiles3, wsel, onehot, lhs1, lhs2, rhs,
        x_send, x_recv, xa_send, xa_recv,
        send1, recv1, send2, recv2,
        in_sem, out_sem,
        rim0_ss, rim0_rs, rim_ss, rim_rs, rim2_ss, rim2_rs, x_ss, x_rs,
        req_ss, req_rs, a1_ss, a1_rs, a2_ss, a2_rs,
    ):
        gx = lax.axis_index("gx")
        gy = lax.axis_index("gy")
        gx_y = lax.rem(gx, RING)
        gx_x = lax.rem(gx // RING, 2)
        gx_z = gx // (2 * RING)
        north, south = lax.rem(gx + n_gx - 1, n_gx), lax.rem(gx + 1, n_gx)
        west, east = lax.rem(gy + n_gy - 1, n_gy), lax.rem(gy + 1, n_gy)
        sides = ({"gx": north}, {"gx": south}, {"gy": west}, {"gy": east})
        partner = {"gx": gx + RING - 2 * RING * gx_x}

        core = lax.rem(gy, 2)

        def peer(q, sign):
            dz, dy = q // RING, lax.rem(q, RING)
            if sign < 0:
                dz, dy = RING - dz, RING - dy
            z = lax.rem(gx_z + dz, RING)
            y = lax.rem(gx_y + dy, RING)
            return {"gx": z * (2 * RING) + gx_x * RING + y}

        barrier = pltpu.get_barrier_semaphore()
        greeted = [peer(q, 1) for q in others] + [partner] + list(sides)
        for device in greeted:
            pl.semaphore_signal(barrier, inc=1, device_id=device, device_id_type=MESH)

        body_at = (slice(row0, row1), slice(col0, col1))
        loads = [
            pltpu.make_async_copy(
                temp.at[top - 1 : layers],
                tpad.at[(slice(top - 1, layers), *body_at)],
                in_sem.at[0],
            ),
            pltpu.make_async_copy(cond, kpad.at[body_at], in_sem.at[1]),
            pltpu.make_async_copy(
                temp.at[0 : top - 1], tpad.at[(slice(0, top - 1), *body_at)], in_sem.at[2]
            ),
            pltpu.make_async_copy(adj, apad.at[(slice(None), *body_at)], in_sem.at[3]),
            pltpu.make_async_copy(grad, gin, in_sem.at[4]),
            pltpu.make_async_copy(obs, obs_v, in_sem.at[5]),
        ]
        for load in loads:
            load.start()

        eye = iota((tiles, tiles), 0) == iota((tiles, tiles), 1)

        def as_column(line):
            spread = jnp.where(eye, jnp.broadcast_to(line, (tiles, tiles)), 0)
            return jnp.sum(spread, axis=1, keepdims=True)

        lane = iota((tiles, LANES), 1)
        lane_slot = iota((tiles, n_slots), 1)
        below = jnp.where(iota((tiles, tiles), 0) > iota((tiles, tiles), 1), 1.0, 0.0)
        base = jnp.zeros((1, LANES), F32)
        weights = jnp.zeros((tiles, n_slots), F32)
        wanted = jnp.zeros((tiles, n_slots), F32)
        for k in range(k_blocks):
            code = as_column(map_ref[k : k + 1, :].astype(F32)).astype(jnp.int32)
            weight = as_column(weight_ref[k : k + 1, :])
            plate = code >> ((tiles * n_gy).bit_length() - 1)
            far = ((plate ^ gx) >> 2) & 1
            dz = ((plate >> 3) - gx_z) & 3
            dy = (plate - gx) & 3
            block = far * PLANE + dz * RING + dy
            local = code & (tiles - 1)
            hit = jnp.where(block == lane, 1.0, 0.0)
            before = jnp.dot(below, hit, preferred_element_type=F32) + base
            base = base + jnp.sum(hit, axis=0, keepdims=True)
            rank = jnp.sum(hit * before, axis=1, keepdims=True)
            here = block * CAP + rank.astype(jnp.int32) == lane_slot
            weights = weights + jnp.where(here, weight, 0.0)
            wanted = wanted + jnp.where(here, (local + 1).astype(F32), 0.0)
        wsel[...] = weights
        asked = jnp.sum(wanted, axis=0, keepdims=True)
        for g in range(groups):
            for f in range(2):
                at = f * half + g * LANES
                req_send[g, f : f + 1] = asked[:, at : at + LANES]

        for load in loads[:2]:
            load.wait()
        first, last = row0, row1 - 1
        rim_lane = iota((rows, LANES), 1)
        for side, row in ((0, first), (1, last)):
            ns0_send[side, 0:1] = tpad[top, row : row + 1, col0:col1]
            ns0_send[side, 1:2] = kpad[row : row + 1, col0:col1]
        for side, col in ((0, col0), (1, col1 - 1)):
            ew0_send[side] = jnp.where(
                rim_lane == 0,
                tpad[top, row0:row1, col : col + 1],
                kpad[row0:row1, col : col + 1],
            )

        pl.semaphore_wait(barrier, len(greeted))

        def rim_copies(ns_s, ns_r, ew_s, ew_r, ss, rs):
            copies = []
            for i in range(4):
                src, dst = (ns_s, ns_r) if i < 2 else (ew_s, ew_r)
                copies.append(
                    pltpu.make_async_remote_copy(
                        src_ref=src.at[i % 2],
                        dst_ref=dst.at[1 - i % 2],
                        send_sem=ss.at[i],
                        recv_sem=rs.at[i],
                        device_id=sides[i],
                        device_id_type=MESH,
                    )
                )
            return copies

        rims0 = rim_copies(ns0_send, ns0_recv, ew0_send, ew0_recv, rim0_ss, rim0_rs)
        for copy in rims0:
            copy.start()

        req_copies = []
        for q in others:
            copy = pltpu.make_async_remote_copy(
                src_ref=req_send.at[q // per_group],
                dst_ref=req_recv.at[q],
                send_sem=req_ss.at[q],
                recv_sem=req_rs.at[q],
                device_id=peer(q, 1),
                device_id_type=MESH,
            )
            copy.start()
            req_copies.append(copy)
        req_recv[0] = req_send[0]

        has_north = jnp.where(gx > 0, 1.0, 0.0)
        has_south = jnp.where(gx < n_gx - 1, 1.0, 0.0)
        has_west = jnp.where(gy > 0, 1.0, 0.0)
        has_east = jnp.where(gy < n_gy - 1, 1.0, 0.0)

        def column_rims(pad, index, source, lane_at):
            for side, has, at in ((0, has_west, 0), (1, has_east, col1)):
                value = source[side, :, lane_at : lane_at + 1] * has
                pad[(*index, slice(row0, row1), slice(at, at + LANES))] = jnp.broadcast_to(
                    value, (rows, LANES)
                )

        for copy in rims0:
            copy.wait_recv()
        kpad[first - 1 : first, col0:col1] = ns0_recv[0, 1:2] * has_north
        kpad[last + 1 : last + 2, col0:col1] = ns0_recv[1, 1:2] * has_south
        column_rims(kpad, (), ew0_recv, 1)
        tpad[top, first - 1 : first, col0:col1] = ns0_recv[0, 0:1] * has_north
        tpad[top, last + 1 : last + 2, col0:col1] = ns0_recv[1, 0:1] * has_south
        column_rims(tpad, (top,), ew0_recv, 0)

        def around(pad, index, r):
            a, b = row0 + r * TR, row0 + (r + 1) * TR
            return (
                pad[(*index, slice(a, b), slice(col0, col1))],
                pad[(*index, slice(a, b), slice(col0 + 1, col1 + 1))],
                pad[(*index, slice(a, b), slice(col0 - 1, col1 - 1))],
                pad[(*index, slice(a - 1, b - 1), slice(col0, col1))],
                pad[(*index, slice(a + 1, b + 1), slice(col0, col1))],
            )

        for r in range(strips):
            kc, ke, kw, kn, ks = around(kpad, (), r)
            strip = slice(r * TR, (r + 1) * TR)
            faces = [0.5 * RATE_PLANE * (kc + other) for other in (ke, kw, kn, ks)]
            for i in range(4):
                coef[i, strip] = faces[i]
            tc, te, tw, tn, ts = around(tpad, (top,), r)
            under = tpad[top - 1, row0 + r * TR : row0 + (r + 1) * TR, col0:col1]
            value = tc + RATE_VERTICAL * (under - tc)
            for face, other in zip(faces, (te, tw, tn, ts)):
                value = value + face * (other - tc)
            for u in range(tile_cols):
                tiles3[r * tile_cols + u] = value[:, u * TC : (u + 1) * TC]

        def partner_copy(src, dst, i):
            return pltpu.make_async_remote_copy(
                src_ref=src,
                dst_ref=dst,
                send_sem=x_ss.at[i],
                recv_sem=x_rs.at[i],
                device_id=partner,
                device_id_type=MESH,
            )

        for rr in range(TR):
            x_send[:, rr * TC : (rr + 1) * TC] = tiles3[:, rr, :]
        x_copy = partner_copy(x_send, x_recv, 0)
        x_copy.start()

        for copy in req_copies:
            copy.wait_recv()
        group_lane = iota((per_group, LANES), 1) // CAP
        group_row = iota((per_group, LANES), 0)
        tile_row = iota((tiles, LANES), 0).astype(F32)
        for f in range(2):
            picks = []
            for g in range(groups):
                block = req_recv[g * per_group : (g + 1) * per_group, f, :]
                line = jnp.sum(
                    jnp.where(group_lane == group_row, block, 0.0), axis=0, keepdims=True
                )
                picks.append(jnp.where(line - 1.0 == tile_row, 1.0, 0.0))
            pick = jnp.concatenate(picks, axis=1)
            onehot[:, f * half : (f + 1) * half] = pick
            turned = jnp.transpose(jnp.concatenate([pick, pick], axis=0)).astype(BF16)
            lhs1[f * half : (f + 1) * half, 0 : 2 * tiles] = turned
            lhs1[f * half : (f + 1) * half, 2 * tiles : 4 * tiles] = turned

        def block_copy(src, dst, ss, rs, sign, f, q):
            b = f * PLANE + q
            at = pl.ds(pl.multiple_of(b * CAP, CAP), CAP)
            return pltpu.make_async_remote_copy(
                src_ref=src.at[at],
                dst_ref=dst.at[at],
                send_sem=ss.at[b],
                recv_sem=rs.at[b],
                device_id=peer(q, sign),
                device_id_type=MESH,
            )

        def exchange(*args):
            starts, waits = [[], []], [[], []]
            for f in range(2):
                for one, two in order:
                    starts[f].append(block_copy(*args, f, one + core * (two - one)))
                for q in others:
                    waits[f].append(block_copy(*args, f, q))
            return starts, waits

        def pack_and_send(lhs, src, dst, copies, f):
            at = slice(f * half, (f + 1) * half)
            src[at] = jnp.dot(lhs[at], rhs[...], preferred_element_type=F32)
            for copy in copies[f]:
                copy.start()
            dst[f * half : f * half + CAP] = src[f * half : f * half + CAP]

        def fill_tiles(source):
            for i, part in enumerate(three_parts(source)):
                rhs[i * tiles : (i + 1) * tiles] = part
            rhs[3 * tiles : 4 * tiles] = jnp.zeros((tiles, cols), BF16)

        starts1, copies1 = exchange(send1, recv1, a1_ss, a1_rs, -1)
        fill_tiles(x_send[...])
        pack_and_send(lhs1, send1, recv1, starts1, 0)

        for load in loads[2:4]:
            load.wait()
        for side, row in ((0, first), (1, last)):
            ns_send[side, 0:top] = tpad[0:top, row, col0:col1]
            ns_send[side, layers : layers + top] = apad[0:top, row, col0:col1]
        for side, col in ((0, col0), (1, col1 - 1)):
            packed = jnp.zeros((rows, LANES), F32)
            for l in range(top):
                packed = jnp.where(rim_lane == l, tpad[l, row0:row1, col : col + 1], packed)
                packed = jnp.where(
                    rim_lane == layers + l, apad[l, row0:row1, col : col + 1], packed
                )
            ew_send[side] = packed
        rims = rim_copies(ns_send, ns_recv, ew_send, ew_recv, rim_ss, rim_rs)
        for copy in rims:
            copy.start()

        halves = jnp.concatenate(two_parts(wsel[...]), axis=0).astype(F32)
        turned = jnp.transpose(halves).astype(BF16)
        lhs2[:, 0 : 2 * tiles] = turned
        lhs2[:, 2 * tiles : 4 * tiles] = turned

        for copy in rims:
            copy.wait_recv()
        for l in range(top):
            column_rims(tpad, (l,), ew_recv, l)
            column_rims(apad, (l,), ew_recv, layers + l)
        tpad[0:top, first - 1, col0:col1] = ns_recv[0, 0:top] * has_north
        tpad[0:top, last + 1, col0:col1] = ns_recv[1, 0:top] * has_south
        apad[0:top, first - 1, col0:col1] = ns_recv[0, layers : layers + top] * has_north
        apad[0:top, last + 1, col0:col1] = ns_recv[1, layers : layers + top] * has_south

        def layer_step(l, r, total):
            strip = slice(r * TR, (r + 1) * TR)
            tc, *t_near = around(tpad, (l,), r)
            ac, *a_near = around(apad, (l,), r)
            flow = jnp.zeros_like(ac)
            for i in range(4):
                step = a_near[i] - ac
                flow = flow + coef[i, strip] * step
                total = total + (t_near[i] - tc) * step
            return ac + flow, ac, total

        def inner_layers(r):
            strip = slice(r * TR, (r + 1) * TR)
            inner = slice(row0 + r * TR, row0 + (r + 1) * TR)

            def body(l, total):
                value, ac, total = layer_step(l, r, total)
                above = apad[l + 1, inner, col0:col1]
                under = apad[jnp.maximum(l - 1, 0), inner, col0:col1]
                outv[l, strip] = value + RATE_VERTICAL * ((above - ac) + (under - ac))
                return total

            gacc[strip] = lax.fori_loop(0, top, body, jnp.zeros((TR, cols), F32))

        for r in range(strips // 2):
            inner_layers(r)

        x_copy.wait_recv()
        fill_tiles(x_recv[...])
        pack_and_send(lhs1, send1, recv1, starts1, 1)

        for r in range(strips // 2, strips):
            inner_layers(r)
        early = pltpu.make_async_copy(
            outv.at[0 : top - 1], adj_out.at[0 : top - 1], out_sem.at[0]
        )
        early.start()

        loads[4].wait()
        loads[5].wait()
        frame = as_column(frame_ref[...].astype(F32)).astype(jnp.int32)
        seen = jnp.zeros((tiles, cols), F32)
        for f in range(frames):
            seen = jnp.where(frame == f, obs_v[f], seen)
        misv[...] = -seen

        for f in range(2):
            for copy in copies1[f]:
                copy.wait_recv()
            at = slice(f * half, (f + 1) * half)
            wh, wl = two_parts(wsel[:, at])
            rh, rl = two_parts(recv1[at])
            misv[...] += jnp.dot(
                jnp.concatenate([wh, wl, wh], axis=1),
                jnp.concatenate([rh, rh, rl], axis=0),
                preferred_element_type=F32,
            )
        mis_copy = pltpu.make_async_copy(misv, misfit_out, out_sem.at[1])
        mis_copy.start()

        mh, ml = two_parts(misv[...])
        rhs[0:tiles] = mh
        rhs[tiles : 2 * tiles] = mh
        rhs[2 * tiles : 3 * tiles] = ml
        rhs[3 * tiles : 4 * tiles] = ml
        starts2, copies2 = exchange(send2, recv2, a2_ss, a2_rs, 1)
        for f in (1, 0):
            pack_and_send(lhs2, send2, recv2, starts2, f)

        def gathered(f):
            for copy in copies2[f]:
                copy.wait_recv()
            at = slice(f * half, (f + 1) * half)
            pick = onehot[:, at].astype(BF16)
            return jnp.dot(
                jnp.concatenate([pick, pick, pick], axis=1),
                jnp.concatenate(three_parts(recv2[at]), axis=0),
                preferred_element_type=F32,
            )

        xa_send[...] = gathered(1)
        xa_copy = partner_copy(xa_send, xa_recv, 1)
        xa_copy.start()
        added = gathered(0)
        xa_copy.wait_recv()
        added = added + xa_recv[...]
        for rr in range(TR):
            tiles3[:, rr, :] = added[:, rr * TC : (rr + 1) * TC]
        for r in range(strips):
            strip = slice(r * TR, (r + 1) * TR)
            inner = slice(row0 + r * TR, row0 + (r + 1) * TR)
            extra = jnp.concatenate(
                [tiles3[r * tile_cols + u] for u in range(tile_cols)], axis=1
            )
            apad[top, inner, col0:col1] += extra
            outv[top - 1, strip] += RATE_VERTICAL * extra

        for side, row in ((0, first), (1, last)):
            ns2_send[side] = apad[top, row : row + 1, col0:col1]
        for side, col in ((0, col0), (1, col1 - 1)):
            ew2_send[side] = jnp.broadcast_to(
                apad[top, row0:row1, col : col + 1], (rows, LANES)
            )
        rims2 = rim_copies(ns2_send, ns2_recv, ew2_send, ew2_recv, rim2_ss, rim2_rs)
        for copy in rims2:
            copy.start()
        late = pltpu.make_async_copy(
            outv.at[top - 1], adj_out.at[top - 1], out_sem.at[2]
        )
        late.start()
        for copy in rims2:
            copy.wait_recv()
        apad[top, first - 1 : first, col0:col1] = ns2_recv[0] * has_north
        apad[top, last + 1 : last + 2, col0:col1] = ns2_recv[1] * has_south
        apad[top, row0:row1, 0:col0] = ew2_recv[0] * has_west
        apad[top, row0:row1, col1 : col1 + LANES] = ew2_recv[1] * has_east

        for r in range(strips):
            strip = slice(r * TR, (r + 1) * TR)
            inner = slice(row0 + r * TR, row0 + (r + 1) * TR)
            value, ac, total = layer_step(top, r, gacc[strip])
            under = apad[top - 1, inner, col0:col1]
            outv[top, strip] = value + RATE_VERTICAL * (under - ac)
            gradv[strip] = gin[strip] - (0.5 * RATE_PLANE) * total

        last_copies = [
            pltpu.make_async_copy(outv.at[top], adj_out.at[top], out_sem.at[3]),
            pltpu.make_async_copy(gradv, grad_out, out_sem.at[4]),
        ]
        for copy in last_copies:
            copy.start()
        sent = rims0 + rims + rims2 + req_copies + [x_copy, xa_copy]
        for copy in sent + copies1[0] + copies1[1] + copies2[0] + copies2[1]:
            copy.wait_send()
        for copy in [early, mis_copy, late] + last_copies:
            copy.wait()

    dma = pltpu.SemaphoreType.DMA

    def vmem(*shape, dtype=F32):
        return pltpu.VMEM(shape, dtype)

    def pair(*shape):
        return [vmem(*shape), vmem(*shape)]

    tile = TR * TC
    scratch = [
        vmem(layers, rows + 2 * TR, cols + 2 * LANES),
        vmem(layers, rows + 2 * TR, cols + 2 * LANES),
        vmem(rows + 2 * TR, cols + 2 * LANES),
        vmem(rows, cols),
        vmem(frames, tiles, tile),
        vmem(4, rows, cols),
        vmem(rows, cols),
        vmem(layers, rows, cols),
        vmem(tiles, tile),
        vmem(rows, cols),
        *pair(2, 2, cols),
        *pair(2, rows, LANES),
        *pair(2, 2 * layers, cols),
        *pair(2, rows, LANES),
        *pair(2, 1, cols),
        *pair(2, rows, LANES),
        vmem(groups, 8, LANES),
        vmem(PLANE, 8, LANES),
        vmem(tiles, TR, TC),
        *pair(tiles, n_slots),
        vmem(n_slots, 4 * tiles, dtype=BF16),
        vmem(n_slots, 4 * tiles, dtype=BF16),
        vmem(4 * tiles, tile, dtype=BF16),
        *pair(tiles, tile),
        *pair(tiles, tile),
        *pair(n_slots, tile),
        *pair(n_slots, tile),
        dma((6,)),
        dma((5,)),
        *[dma((4,)) for _ in range(6)],
        dma((2,)), dma((2,)),
        dma((PLANE,)), dma((PLANE,)),
        *[dma((2 * PLANE,)) for _ in range(4)],
    ]
    in_hbm = pl.BlockSpec(memory_space=pltpu.HBM)
    anywhere = pl.BlockSpec(memory_space=pl.ANY)
    in_vmem = pl.BlockSpec(memory_space=pltpu.VMEM)
    return pl.pallas_call(
        kernel,
        out_shape=(
            jax.ShapeDtypeStruct((tiles, tile), F32),
            jax.ShapeDtypeStruct((layers, rows, cols), F32),
            jax.ShapeDtypeStruct((rows, cols), F32),
        ),
        in_specs=[in_hbm] * 5 + [in_vmem] * 3,
        out_specs=[anywhere] * 3,
        scratch_shapes=scratch,
        compiler_params=pltpu.CompilerParams(
            collective_id=0, has_side_effects=True, vmem_limit_bytes=48 * 1024 * 1024
        ),
    )


def solution(mesh):
    n_gx, n_gy = mesh.shape["gx"], mesh.shape["gy"]

    def local(temp, cond, adj, grad, obs, frame_index, source_map, source_weight):
        layers, rows, cols = temp.shape
        call = make_kernel(n_gx, n_gy, layers, rows, cols, obs.shape[0], source_map.shape[1])
        operands = (
            temp, cond, adj, grad, obs, frame_index[None, :], source_map.T, source_weight.T
        )
        return call(*(pltpu.with_memory_space_constraint(x, pltpu.HBM) for x in operands))

    placed = (
        P(None, "gx", "gy"),
        P("gx", "gy"),
        P(None, "gx", "gy"),
        P("gx", "gy"),
        P(None, ("gx", "gy"), None),
        P(("gx", "gy")),
        P(("gx", "gy"), None),
        P(("gx", "gy"), None),
    )
    return jax.shard_map(
        local,
        mesh=mesh,
        in_specs=placed,
        out_specs=(P(("gx", "gy"), None), P(None, "gx", "gy"), P("gx", "gy")),
        check_vma=False,
    )
```

```python
import jax
import jax.numpy as jnp
from jax import lax
from jax.experimental import pallas as pl
from jax.experimental.pallas import tpu as pltpu
from jax.sharding import PartitionSpec as P

TR = 8
TC = 128
CAP = 16
LANES = 128
RATE_PLANE = 0.2
RATE_VERTICAL = 0.08
MESH = pl.DeviceIdType.MESH
F32 = jnp.float32
BF16 = jnp.bfloat16


def iota(shape, dim):
    return lax.broadcasted_iota(jnp.int32, shape, dim)


def two_parts(x):
    hi = x.astype(BF16)
    lo = (x - hi.astype(F32)).astype(BF16)
    return hi, lo


def three_parts(x):
    hi = x.astype(BF16)
    rest = x - hi.astype(F32)
    mid = rest.astype(BF16)
    lo = (rest - mid.astype(F32)).astype(BF16)
    return hi, mid, lo


RING = 4
PLANE = RING * RING
FARTHEST_FIRST = (2, 1, 3)


def make_kernel(n_gx, n_gy, layers, rows, cols, frames, k_blocks):
    tiles = (rows // TR) * (cols // TC)
    half = PLANE * CAP
    n_slots = 2 * half
    row0, col0 = TR, LANES
    row1, col1 = row0 + rows, col0 + cols
    strips = rows // TR
    tile_cols = cols // TC
    top = layers - 1
    per_group = LANES // CAP
    groups = PLANE // per_group
    others = range(1, PLANE)
    wide = cols // 2

    def kernel(
        temp, cond, adj, grad, obs, frame_ref, map_ref, weight_ref,
        misfit_out, adj_out, grad_out,
        tpad, apad, kpad, gin, obs_v, coef, gacc, outv, gradv,
        ns0_send, ns0_recv, ew0_send, ew0_recv,
        ns_send, ns_recv, ew_send, ew_recv,
        ns2_send, ns2_recv, ew2_send, ew2_recv,
        req_send, req_recv, tiles3, onehot, lhs1, rhs, rhs2,
        wsend, wblk, wcat, lhs2,
        x_send, x_recv, xa_send, xa_recv,
        send1, recv1, part, part_recv, mis, mis_recv, send2, recv2,
        in_sem, out_sem,
        rim0_ss, rim0_rs, rim_ss, rim_rs, rim2_ss, rim2_rs, x_ss, x_rs,
        req_ss, req_rs, w_ss, w_rs, s1_ss, s1_rs, p_ss, p_rs, m_ss, m_rs, s2_ss, s2_rs,
    ):
        gx = lax.axis_index("gx")
        gy = lax.axis_index("gy")
        gx_y = lax.rem(gx, RING)
        gx_x = lax.rem(gx // RING, 2)
        gx_z = gx // (2 * RING)
        north, south = lax.rem(gx + n_gx - 1, n_gx), lax.rem(gx + 1, n_gx)
        west, east = lax.rem(gy + n_gy - 1, n_gy), lax.rem(gy + 1, n_gy)
        sides = ({"gx": north}, {"gx": south}, {"gy": west}, {"gy": east})
        partner = {"gx": gx + RING - 2 * RING * gx_x}

        def along(dz, dy):
            z = lax.rem(gx_z + dz % RING, RING)
            y = lax.rem(gx_y + dy % RING, RING)
            return {"gx": z * (2 * RING) + gx_x * RING + y}

        def slot_peer(h, d):
            return along(0, d) if h == 0 else along(d, 0)

        def dense_peer(h, d):
            return along(d, 0) if h == 0 else along(0, d)

        def send(src, dst, ss, rs, device):
            return pltpu.make_async_remote_copy(
                src_ref=src,
                dst_ref=dst,
                send_sem=ss,
                recv_sem=rs,
                device_id=device,
                device_id_type=MESH,
            )

        barrier = pltpu.get_barrier_semaphore()
        greeted = [along(b % RING, b // RING) for b in others] + [partner] + list(sides)
        for device in greeted:
            pl.semaphore_signal(barrier, inc=1, device_id=device, device_id_type=MESH)

        body_at = (slice(row0, row1), slice(col0, col1))
        loads = [
            pltpu.make_async_copy(
                temp.at[top - 1 : layers],
                tpad.at[(slice(top - 1, layers), *body_at)],
                in_sem.at[0],
            ),
            pltpu.make_async_copy(cond, kpad.at[body_at], in_sem.at[1]),
            pltpu.make_async_copy(
                temp.at[0 : top - 1], tpad.at[(slice(0, top - 1), *body_at)], in_sem.at[2]
            ),
            pltpu.make_async_copy(adj, apad.at[(slice(None), *body_at)], in_sem.at[3]),
            pltpu.make_async_copy(grad, gin, in_sem.at[4]),
            pltpu.make_async_copy(obs, obs_v, in_sem.at[5]),
        ]
        for load in loads:
            load.start()

        eye = iota((tiles, tiles), 0) == iota((tiles, tiles), 1)

        def as_column(line):
            spread = jnp.where(eye, jnp.broadcast_to(line, (tiles, tiles)), 0)
            return jnp.sum(spread, axis=1, keepdims=True)

        lane = iota((tiles, LANES), 1)
        lane_slot = iota((tiles, n_slots), 1)
        below = jnp.where(iota((tiles, tiles), 0) > iota((tiles, tiles), 1), 1.0, 0.0)
        base = jnp.zeros((1, LANES), F32)
        wanted = jnp.zeros((tiles, n_slots), F32)
        weights = [jnp.zeros((tiles, n_slots), F32) for _ in range(2)]
        for k in range(k_blocks):
            code = as_column(map_ref[k : k + 1, :].astype(F32)).astype(jnp.int32)
            weight = as_column(weight_ref[k : k + 1, :])
            plate = code >> ((tiles * n_gy).bit_length() - 1)
            far = ((plate ^ gx) >> 2) & 1
            dz = ((plate >> 3) - gx_z) & 3
            dy = (plate - gx) & 3
            block = far * PLANE + dy * RING + dz
            local = code & (tiles - 1)
            hit = jnp.where(block == lane, 1.0, 0.0)
            before = jnp.dot(below, hit, preferred_element_type=F32) + base
            base = base + jnp.sum(hit, axis=0, keepdims=True)
            rank = jnp.sum(hit * before, axis=1, keepdims=True).astype(jnp.int32)
            here = block * CAP + rank == lane_slot
            wanted = wanted + jnp.where(here, (local + 1).astype(F32), 0.0)
            for h, (dense, slot) in enumerate(((dz, dy), (dy, dz))):
                at = dense * LANES + far * (LANES // 2) + slot * CAP + rank
                weights[h] = weights[h] + jnp.where(at == lane_slot, weight, 0.0)
        for h in range(2):
            for d in range(RING):
                wsend[h, d] = weights[h][:, d * LANES : (d + 1) * LANES]
            wblk[h, 0] = weights[h][:, 0:LANES]
        asked = jnp.sum(wanted, axis=0, keepdims=True)
        for g in range(groups):
            for f in range(2):
                at = f * half + g * LANES
                req_send[g, f : f + 1] = asked[:, at : at + LANES]

        for load in loads[:2]:
            load.wait()
        first, last = row0, row1 - 1
        rim_lane = iota((rows, LANES), 1)
        for side, row in ((0, first), (1, last)):
            ns0_send[side, 0:1] = tpad[top, row : row + 1, col0:col1]
            ns0_send[side, 1:2] = kpad[row : row + 1, col0:col1]
        for side, col in ((0, col0), (1, col1 - 1)):
            ew0_send[side] = jnp.where(
                rim_lane == 0,
                tpad[top, row0:row1, col : col + 1],
                kpad[row0:row1, col : col + 1],
            )

        pl.semaphore_wait(barrier, len(greeted))

        def rim_copies(ns_s, ns_r, ew_s, ew_r, ss, rs):
            copies = []
            for i in range(4):
                src, dst = (ns_s, ns_r) if i < 2 else (ew_s, ew_r)
                copies.append(
                    pltpu.make_async_remote_copy(
                        src_ref=src.at[i % 2],
                        dst_ref=dst.at[1 - i % 2],
                        send_sem=ss.at[i],
                        recv_sem=rs.at[i],
                        device_id=sides[i],
                        device_id_type=MESH,
                    )
                )
            return copies

        rims0 = rim_copies(ns0_send, ns0_recv, ew0_send, ew0_recv, rim0_ss, rim0_rs)
        for copy in rims0:
            copy.start()

        req_copies = []
        for b in others:
            copy = send(
                req_send.at[b // per_group],
                req_recv.at[b],
                req_ss.at[b],
                req_rs.at[b],
                along(b % RING, b // RING),
            )
            copy.start()
            req_copies.append(copy)
        w_copies = []
        for h in range(2):
            for d in range(1, RING):
                i = h * RING + d
                copy = send(
                    wsend.at[h, d], wblk.at[h, d], w_ss.at[i], w_rs.at[i], dense_peer(h, d)
                )
                copy.start()
                w_copies.append(copy)
        req_recv[0] = req_send[0]

        has_north = jnp.where(gx > 0, 1.0, 0.0)
        has_south = jnp.where(gx < n_gx - 1, 1.0, 0.0)
        has_west = jnp.where(gy > 0, 1.0, 0.0)
        has_east = jnp.where(gy < n_gy - 1, 1.0, 0.0)

        def column_rims(pad, index, source, lane_at):
            for side, has, at in ((0, has_west, 0), (1, has_east, col1)):
                value = source[side, :, lane_at : lane_at + 1] * has
                pad[(*index, slice(row0, row1), slice(at, at + LANES))] = jnp.broadcast_to(
                    value, (rows, LANES)
                )

        for copy in rims0:
            copy.wait_recv()
        kpad[first - 1 : first, col0:col1] = ns0_recv[0, 1:2] * has_north
        kpad[last + 1 : last + 2, col0:col1] = ns0_recv[1, 1:2] * has_south
        column_rims(kpad, (), ew0_recv, 1)
        tpad[top, first - 1 : first, col0:col1] = ns0_recv[0, 0:1] * has_north
        tpad[top, last + 1 : last + 2, col0:col1] = ns0_recv[1, 0:1] * has_south
        column_rims(tpad, (top,), ew0_recv, 0)

        def around(pad, index, r):
            a, b = row0 + r * TR, row0 + (r + 1) * TR
            return (
                pad[(*index, slice(a, b), slice(col0, col1))],
                pad[(*index, slice(a, b), slice(col0 + 1, col1 + 1))],
                pad[(*index, slice(a, b), slice(col0 - 1, col1 - 1))],
                pad[(*index, slice(a - 1, b - 1), slice(col0, col1))],
                pad[(*index, slice(a + 1, b + 1), slice(col0, col1))],
            )

        for r in range(strips):
            kc, ke, kw, kn, ks = around(kpad, (), r)
            strip = slice(r * TR, (r + 1) * TR)
            faces = [0.5 * RATE_PLANE * (kc + other) for other in (ke, kw, kn, ks)]
            for i in range(4):
                coef[i, strip] = faces[i]
            tc, te, tw, tn, ts = around(tpad, (top,), r)
            under = tpad[top - 1, row0 + r * TR : row0 + (r + 1) * TR, col0:col1]
            value = tc + RATE_VERTICAL * (under - tc)
            for face, other in zip(faces, (te, tw, tn, ts)):
                value = value + face * (other - tc)
            for u in range(tile_cols):
                tiles3[r * tile_cols + u] = value[:, u * TC : (u + 1) * TC]

        for rr in range(TR):
            x_send[:, rr * TC : (rr + 1) * TC] = tiles3[:, rr, :]
        x_copy = send(x_send, x_recv, x_ss.at[0], x_rs.at[0], partner)
        x_copy.start()

        for copy in req_copies:
            copy.wait_recv()
        group_lane = iota((per_group, LANES), 1) // CAP
        group_row = iota((per_group, LANES), 0)
        tile_row = iota((tiles, LANES), 0).astype(F32)
        for f in range(2):
            picks = []
            for g in range(groups):
                block = req_recv[g * per_group : (g + 1) * per_group, f, :]
                line = jnp.sum(
                    jnp.where(group_lane == group_row, block, 0.0), axis=0, keepdims=True
                )
                picks.append(jnp.where(line - 1.0 == tile_row, 1.0, 0.0))
            pick = jnp.concatenate(picks, axis=1)
            onehot[:, f * half : (f + 1) * half] = pick
            turned = jnp.transpose(jnp.concatenate([pick, pick], axis=0)).astype(BF16)
            lhs1[f * half : (f + 1) * half, 0 : 2 * tiles] = turned
            lhs1[f * half : (f + 1) * half, 2 * tiles : 4 * tiles] = turned

        def plane_rows(ref, h, f, d):
            return ref.at[0, f, d] if h == 0 else ref.at[1, f, :, d]

        slots1 = {}
        for h in range(2):
            for f in range(2):
                for d in range(1, RING):
                    i = (h * 2 + f) * RING + d
                    slots1[h, f, d] = send(
                        plane_rows(send1, h, f, d),
                        recv1.at[h, :, f, d],
                        s1_ss.at[i],
                        s1_rs.at[i],
                        slot_peer(h, -d),
                    )

        def fill_tiles(source):
            for i, three in enumerate(three_parts(source)):
                rhs[i * tiles : (i + 1) * tiles] = three
            rhs[3 * tiles : 4 * tiles] = jnp.zeros((tiles, cols), BF16)

        def pack_tiles(f):
            for h in range(2):
                packed = jnp.dot(
                    lhs1[f * half : (f + 1) * half],
                    rhs[:, h * wide : (h + 1) * wide],
                    preferred_element_type=F32,
                )
                send1[h, f] = packed.reshape(RING, RING, CAP, wide)
                for d in FARTHEST_FIRST:
                    slots1[h, f, d].start()
            recv1[0, :, f, 0] = send1[0, f, 0]
            recv1[1, :, f, 0] = send1[1, f, :, 0]

        fill_tiles(x_send[...])
        pack_tiles(0)

        for load in loads[2:4]:
            load.wait()
        for side, row in ((0, first), (1, last)):
            ns_send[side, 0:top] = tpad[0:top, row, col0:col1]
            ns_send[side, layers : layers + top] = apad[0:top, row, col0:col1]
        for side, col in ((0, col0), (1, col1 - 1)):
            packed = jnp.zeros((rows, LANES), F32)
            for l in range(top):
                packed = jnp.where(rim_lane == l, tpad[l, row0:row1, col : col + 1], packed)
                packed = jnp.where(
                    rim_lane == layers + l, apad[l, row0:row1, col : col + 1], packed
                )
            ew_send[side] = packed
        rims = rim_copies(ns_send, ns_recv, ew_send, ew_recv, rim_ss, rim_rs)
        for copy in rims:
            copy.start()

        for copy in w_copies:
            copy.wait_recv()
        for h in range(2):
            for d in range(RING):
                wh, wl = two_parts(wblk[h, d])
                for f in range(2):
                    at = slice(f * (LANES // 2), (f + 1) * (LANES // 2))
                    wcat[h, d, f] = jnp.concatenate(
                        [wh[:, at], wl[:, at], wh[:, at], wl[:, at]], axis=1
                    )
                turned = jnp.transpose(jnp.concatenate([wh, wl], axis=0).astype(F32))
                lhs2[h, d, :, 0 : 2 * tiles] = turned.astype(BF16)
                lhs2[h, d, :, 2 * tiles : 4 * tiles] = turned.astype(BF16)

        for copy in rims:
            copy.wait_recv()
        for l in range(top):
            column_rims(tpad, (l,), ew_recv, l)
            column_rims(apad, (l,), ew_recv, layers + l)
        tpad[0:top, first - 1, col0:col1] = ns_recv[0, 0:top] * has_north
        tpad[0:top, last + 1, col0:col1] = ns_recv[1, 0:top] * has_south
        apad[0:top, first - 1, col0:col1] = ns_recv[0, layers : layers + top] * has_north
        apad[0:top, last + 1, col0:col1] = ns_recv[1, layers : layers + top] * has_south

        def layer_step(l, r, total):
            strip = slice(r * TR, (r + 1) * TR)
            tc, *t_near = around(tpad, (l,), r)
            ac, *a_near = around(apad, (l,), r)
            flow = jnp.zeros_like(ac)
            for i in range(4):
                step = a_near[i] - ac
                flow = flow + coef[i, strip] * step
                total = total + (t_near[i] - tc) * step
            return ac + flow, ac, total

        def inner_layers(r):
            strip = slice(r * TR, (r + 1) * TR)
            inner = slice(row0 + r * TR, row0 + (r + 1) * TR)

            def body(l, total):
                value, ac, total = layer_step(l, r, total)
                above = apad[l + 1, inner, col0:col1]
                under = apad[jnp.maximum(l - 1, 0), inner, col0:col1]
                outv[l, strip] = value + RATE_VERTICAL * ((above - ac) + (under - ac))
                return total

            gacc[strip] = lax.fori_loop(0, top, body, jnp.zeros((TR, cols), F32))

        for r in range(0, 2):
            inner_layers(r)

        x_copy.wait_recv()
        fill_tiles(x_recv[...])
        pack_tiles(1)

        for r in range(2, 4):
            inner_layers(r)

        loads[4].wait()
        loads[5].wait()
        frame = as_column(frame_ref[...].astype(F32)).astype(jnp.int32)
        for h in range(2):
            seen = jnp.zeros((tiles, wide), F32)
            for f in range(frames):
                seen = jnp.where(frame == f, obs_v[f, :, h * wide : (h + 1) * wide], seen)
            mis[h] = -seen

        def weigh(h, f, d):
            rh, rl = two_parts(recv1[h, d, f].reshape(RING * CAP, wide))
            return jnp.dot(
                wcat[h, d, f],
                jnp.concatenate([rh, rh, rl, rl], axis=0),
                preferred_element_type=F32,
            )

        parts = {}
        for h in range(2):
            for d in range(1, RING):
                i = h * RING + d
                parts[h, d] = send(
                    part.at[h, d], part_recv.at[h, d], p_ss.at[i], p_rs.at[i], dense_peer(h, -d)
                )
        for f in range(2):
            for h in range(2):
                for d in range(1, RING):
                    slots1[h, f, d].wait_recv()
                for d in FARTHEST_FIRST + (0,):
                    if f == 0:
                        part[h, d] = weigh(h, f, d)
                    else:
                        part[h, d] += weigh(h, f, d)
                        if d:
                            parts[h, d].start()

        for r in range(4, 6):
            inner_layers(r)

        spread = {}
        for h in range(2):
            for d in range(1, RING):
                i = h * RING + d
                spread[h, d] = send(
                    mis.at[h], mis_recv.at[h, d], m_ss.at[i], m_rs.at[i], dense_peer(h, d)
                )
        mis_copies = []
        for h in range(2):
            for d in range(1, RING):
                parts[h, d].wait_recv()
            mis[h] += (part[h, 0] + part_recv[h, 1]) + (part_recv[h, 2] + part_recv[h, 3])
            for d in FARTHEST_FIRST:
                spread[h, d].start()
            copy = pltpu.make_async_copy(
                mis.at[h], misfit_out.at[:, h * wide : (h + 1) * wide], out_sem.at[5 + h]
            )
            copy.start()
            mis_copies.append(copy)

        for r in range(6, 7):
            inner_layers(r)

        slots2 = {}
        for h in range(2):
            for f in range(2):
                for d in range(1, RING):
                    i = (h * 2 + f) * RING + d
                    slots2[h, f, d] = send(
                        send2.at[h, :, f, d],
                        plane_rows(recv2, h, f, d),
                        s2_ss.at[i],
                        s2_rs.at[i],
                        slot_peer(h, d),
                    )
        n_half = LANES // 2
        for f in (1, 0):
            for h in range(2):
                for d in range(RING):
                    if f == 1:
                        if d:
                            spread[h, d].wait_recv()
                        mh, ml = two_parts(mis_recv[h, d] if d else mis[h])
                        at = slice(h * wide, (h + 1) * wide)
                        for i, piece in enumerate((mh, mh, ml, ml)):
                            rhs2[d, i * tiles : (i + 1) * tiles, at] = piece
                    packed = jnp.dot(
                        lhs2[h, d, f * n_half : (f + 1) * n_half],
                        rhs2[d, :, h * wide : (h + 1) * wide],
                        preferred_element_type=F32,
                    )
                    send2[h, d, f] = packed.reshape(RING, CAP, wide)
                for d in FARTHEST_FIRST:
                    slots2[h, f, d].start()
            recv2[0, f, 0] = send2[0, :, f, 0]
            recv2[1, f, :, 0] = send2[1, :, f, 0]

        for r in range(7, strips):
            inner_layers(r)
        early = pltpu.make_async_copy(
            outv.at[0 : top - 1], adj_out.at[0 : top - 1], out_sem.at[0]
        )
        early.start()

        def gathered(h, f):
            for d in range(1, RING):
                slots2[h, f, d].wait_recv()
            pick = onehot[:, f * half : (f + 1) * half].astype(BF16)
            return jnp.dot(
                jnp.concatenate([pick, pick, pick], axis=1),
                jnp.concatenate(three_parts(recv2[h, f].reshape(half, wide)), axis=0),
                preferred_element_type=F32,
            )

        xa_copies = []
        for h in range(2):
            xa_send[h] = gathered(h, 1)
            copy = send(xa_send.at[h], xa_recv.at[h], x_ss.at[1 + h], x_rs.at[1 + h], partner)
            copy.start()
            xa_copies.append(copy)
        sums = [gathered(h, 0) for h in range(2)]
        for h in range(2):
            xa_copies[h].wait_recv()
        added = jnp.concatenate([sums[h] + xa_recv[h] for h in range(2)], axis=1)
        for rr in range(TR):
            tiles3[:, rr, :] = added[:, rr * TC : (rr + 1) * TC]
        for r in range(strips):
            strip = slice(r * TR, (r + 1) * TR)
            inner = slice(row0 + r * TR, row0 + (r + 1) * TR)
            extra = jnp.concatenate(
                [tiles3[r * tile_cols + u] for u in range(tile_cols)], axis=1
            )
            apad[top, inner, col0:col1] += extra
            outv[top - 1, strip] += RATE_VERTICAL * extra

        for side, row in ((0, first), (1, last)):
            ns2_send[side] = apad[top, row : row + 1, col0:col1]
        for side, col in ((0, col0), (1, col1 - 1)):
            ew2_send[side] = jnp.broadcast_to(
                apad[top, row0:row1, col : col + 1], (rows, LANES)
            )
        rims2 = rim_copies(ns2_send, ns2_recv, ew2_send, ew2_recv, rim2_ss, rim2_rs)
        for copy in rims2:
            copy.start()
        late = pltpu.make_async_copy(
            outv.at[top - 1], adj_out.at[top - 1], out_sem.at[2]
        )
        late.start()
        for copy in rims2:
            copy.wait_recv()
        apad[top, first - 1 : first, col0:col1] = ns2_recv[0] * has_north
        apad[top, last + 1 : last + 2, col0:col1] = ns2_recv[1] * has_south
        apad[top, row0:row1, 0:col0] = ew2_recv[0] * has_west
        apad[top, row0:row1, col1 : col1 + LANES] = ew2_recv[1] * has_east

        for r in range(strips):
            strip = slice(r * TR, (r + 1) * TR)
            inner = slice(row0 + r * TR, row0 + (r + 1) * TR)
            value, ac, total = layer_step(top, r, gacc[strip])
            under = apad[top - 1, inner, col0:col1]
            outv[top, strip] = value + RATE_VERTICAL * (under - ac)
            gradv[strip] = gin[strip] - (0.5 * RATE_PLANE) * total

        last_copies = [
            pltpu.make_async_copy(outv.at[top], adj_out.at[top], out_sem.at[3]),
            pltpu.make_async_copy(gradv, grad_out, out_sem.at[4]),
        ]
        for copy in last_copies:
            copy.start()
        sent = rims0 + rims + rims2 + req_copies + w_copies + [x_copy] + xa_copies
        for group in (slots1, parts, spread, slots2):
            sent.extend(group.values())
        for copy in sent:
            copy.wait_send()
        for copy in [early, late] + mis_copies + last_copies:
            copy.wait()

    dma = pltpu.SemaphoreType.DMA

    def vmem(*shape, dtype=F32):
        return pltpu.VMEM(shape, dtype)

    def pair(*shape):
        return [vmem(*shape), vmem(*shape)]

    tile = TR * TC
    scratch = [
        vmem(layers, rows + 2 * TR, cols + 2 * LANES),
        vmem(layers, rows + 2 * TR, cols + 2 * LANES),
        vmem(rows + 2 * TR, cols + 2 * LANES),
        vmem(rows, cols),
        vmem(frames, tiles, tile),
        vmem(4, rows, cols),
        vmem(rows, cols),
        vmem(layers, rows, cols),
        vmem(rows, cols),
        *pair(2, 2, cols),
        *pair(2, rows, LANES),
        *pair(2, 2 * layers, cols),
        *pair(2, rows, LANES),
        *pair(2, 1, cols),
        *pair(2, rows, LANES),
        vmem(groups, 8, LANES),
        vmem(PLANE, 8, LANES),
        vmem(tiles, TR, TC),
        vmem(tiles, n_slots),
        vmem(n_slots, 4 * tiles, dtype=BF16),
        vmem(4 * tiles, tile, dtype=BF16),
        vmem(RING, 4 * tiles, tile, dtype=BF16),
        *pair(2, RING, tiles, LANES),
        vmem(2, RING, 2, tiles, 4 * tiles, dtype=BF16),
        vmem(2, RING, LANES, 4 * tiles, dtype=BF16),
        *pair(tiles, tile),
        *pair(2, tiles, tile // 2),
        vmem(2, 2, RING, RING, CAP, tile // 2),
        vmem(2, RING, 2, RING, CAP, tile // 2),
        *pair(2, RING, tiles, tile // 2),
        vmem(2, tiles, tile // 2),
        vmem(2, RING, tiles, tile // 2),
        vmem(2, RING, 2, RING, CAP, tile // 2),
        vmem(2, 2, RING, RING, CAP, tile // 2),
        dma((6,)),
        dma((7,)),
        *[dma((4,)) for _ in range(6)],
        dma((3,)), dma((3,)),
        dma((PLANE,)), dma((PLANE,)),
        dma((2 * RING,)), dma((2 * RING,)),
        dma((4 * RING,)), dma((4 * RING,)),
        dma((2 * RING,)), dma((2 * RING,)),
        dma((2 * RING,)), dma((2 * RING,)),
        dma((4 * RING,)), dma((4 * RING,)),
    ]
    in_hbm = pl.BlockSpec(memory_space=pltpu.HBM)
    anywhere = pl.BlockSpec(memory_space=pl.ANY)
    in_vmem = pl.BlockSpec(memory_space=pltpu.VMEM)
    return pl.pallas_call(
        kernel,
        out_shape=(
            jax.ShapeDtypeStruct((tiles, tile), F32),
            jax.ShapeDtypeStruct((layers, rows, cols), F32),
            jax.ShapeDtypeStruct((rows, cols), F32),
        ),
        in_specs=[in_hbm] * 5 + [in_vmem] * 3,
        out_specs=[anywhere] * 3,
        scratch_shapes=scratch,
        compiler_params=pltpu.CompilerParams(
            collective_id=0, has_side_effects=True, vmem_limit_bytes=48 * 1024 * 1024
        ),
    )


def solution(mesh):
    n_gx, n_gy = mesh.shape["gx"], mesh.shape["gy"]

    def local(temp, cond, adj, grad, obs, frame_index, source_map, source_weight):
        layers, rows, cols = temp.shape
        call = make_kernel(n_gx, n_gy, layers, rows, cols, obs.shape[0], source_map.shape[1])
        operands = (
            temp, cond, adj, grad, obs, frame_index[None, :], source_map.T, source_weight.T
        )
        return call(*(pltpu.with_memory_space_constraint(x, pltpu.HBM) for x in operands))

    placed = (
        P(None, "gx", "gy"),
        P("gx", "gy"),
        P(None, "gx", "gy"),
        P("gx", "gy"),
        P(None, ("gx", "gy"), None),
        P(("gx", "gy")),
        P(("gx", "gy"), None),
        P(("gx", "gy"), None),
    )
    return jax.shard_map(
        local,
        mesh=mesh,
        in_specs=placed,
        out_specs=(P(("gx", "gy"), None), P(None, "gx", "gy"), P("gx", "gy")),
        check_vma=False,
    )
```

```python
import jax
import jax.numpy as jnp
from jax import lax
from jax.experimental import pallas as pl
from jax.experimental.pallas import tpu as pltpu
from jax.sharding import PartitionSpec as P

TR = 8
TC = 128
LANES = 128
RATE_PLANE = 0.2
RATE_VERTICAL = 0.08
MESH = pl.DeviceIdType.MESH
F32 = jnp.float32
BF16 = jnp.bfloat16


def iota(shape, dim):
    return lax.broadcasted_iota(jnp.int32, shape, dim)


def two_parts(x):
    hi = x.astype(BF16)
    lo = (x - hi.astype(F32)).astype(BF16)
    return hi, lo


RING = 4
FARTHEST_FIRST = (2, 1, 3)


def make_kernel(n_gx, n_gy, layers, rows, cols, frames, k_blocks):
    tiles = (rows // TR) * (cols // TC)
    row0, col0 = TR, LANES
    row1, col1 = row0 + rows, col0 + cols
    strips = rows // TR
    tile_cols = cols // TC
    top = layers - 1
    n_chunks = 4
    wide = cols // n_chunks
    ring = RING * tiles

    def kernel(
        temp, cond, adj, grad, obs, frame_ref, map_ref, weight_ref,
        misfit_out, adj_out, grad_out,
        tpad, apad, kpad, gin, obs_v, coef, gacc, outv, gradv,
        ns0_send, ns0_recv, ew0_send, ew0_recv,
        ns_send, ns_recv, ew_send, ew_recv,
        ns2_send, ns2_recv, ew2_send, ew2_recv,
        small, tiles3, wfull, lhs1, lhs2,
        gat, part, part_recv, mis, con, con_recv, xa_send, xa_recv,
        in_sem, out_sem,
        rim0_ss, rim0_rs, rim_ss, rim_rs, rim2_ss, rim2_rs, x_ss, x_rs,
        w_ss, w_rs, s1_ss, s1_rs, p_ss, p_rs, m_ss, m_rs, s2_ss, s2_rs,
    ):
        gx = lax.axis_index("gx")
        gy = lax.axis_index("gy")
        gx_y = lax.rem(gx, RING)
        gx_x = lax.rem(gx // RING, 2)
        gx_z = gx // (2 * RING)
        north, south = lax.rem(gx + n_gx - 1, n_gx), lax.rem(gx + 1, n_gx)
        west, east = lax.rem(gy + n_gy - 1, n_gy), lax.rem(gy + 1, n_gy)
        sides = ({"gx": north}, {"gx": south}, {"gy": west}, {"gy": east})
        partner = {"gx": gx + RING - 2 * RING * gx_x}

        def along(dz, dy):
            z = lax.rem(gx_z + dz % RING, RING)
            y = lax.rem(gx_y + dy % RING, RING)
            return {"gx": z * (2 * RING) + gx_x * RING + y}

        def plate_peer(c, d):
            return along(0, d) if c % 2 == 0 else along(d, 0)

        def camera_peer(c, d):
            return along(d, 0) if c % 2 == 0 else along(0, d)

        def send(src, dst, ss, rs, device):
            return pltpu.make_async_remote_copy(
                src_ref=src,
                dst_ref=dst,
                send_sem=ss,
                recv_sem=rs,
                device_id=device,
                device_id_type=MESH,
            )

        barrier = pltpu.get_barrier_semaphore()
        greeted = [along(d, 0) for d in range(1, RING)] + [along(0, d) for d in range(1, RING)]
        greeted += [partner] + list(sides)
        for device in greeted:
            pl.semaphore_signal(barrier, inc=1, device_id=device, device_id_type=MESH)

        body_at = (slice(row0, row1), slice(col0, col1))
        loads = [
            pltpu.make_async_copy(
                temp.at[top - 1 : layers],
                tpad.at[(slice(top - 1, layers), *body_at)],
                in_sem.at[0],
            ),
            pltpu.make_async_copy(cond, kpad.at[body_at], in_sem.at[1]),
            pltpu.make_async_copy(
                temp.at[0 : top - 1], tpad.at[(slice(0, top - 1), *body_at)], in_sem.at[2]
            ),
            pltpu.make_async_copy(adj, apad.at[(slice(None), *body_at)], in_sem.at[3]),
            pltpu.make_async_copy(grad, gin, in_sem.at[4]),
            pltpu.make_async_copy(obs, obs_v, in_sem.at[5]),
        ]
        for load in loads:
            load.start()

        for load in loads[:2]:
            load.wait()
        first, last = row0, row1 - 1
        rim_lane = iota((rows, LANES), 1)
        for side, row in ((0, first), (1, last)):
            ns0_send[side, 0:1] = tpad[top, row : row + 1, col0:col1]
            ns0_send[side, 1:2] = kpad[row : row + 1, col0:col1]
        for side, col in ((0, col0), (1, col1 - 1)):
            ew0_send[side] = jnp.where(
                rim_lane == 0,
                tpad[top, row0:row1, col : col + 1],
                kpad[row0:row1, col : col + 1],
            )

        small[0, 0:k_blocks, 0:tiles] = map_ref[...].astype(F32)
        small[0, k_blocks : 2 * k_blocks, 0:tiles] = weight_ref[...]
        small[2 * RING - 1, 0:1, 0:tiles] = frame_ref[...].astype(F32)

        pl.semaphore_wait(barrier, len(greeted))

        def rim_copies(ns_s, ns_r, ew_s, ew_r, ss, rs):
            copies = []
            for i in range(4):
                src, dst = (ns_s, ns_r) if i < 2 else (ew_s, ew_r)
                copies.append(
                    pltpu.make_async_remote_copy(
                        src_ref=src.at[i % 2],
                        dst_ref=dst.at[1 - i % 2],
                        send_sem=ss.at[i],
                        recv_sem=rs.at[i],
                        device_id=sides[i],
                        device_id_type=MESH,
                    )
                )
            return copies

        rims0 = rim_copies(ns0_send, ns0_recv, ew0_send, ew0_recv, rim0_ss, rim0_rs)
        for copy in rims0:
            copy.start()

        w_copies = []
        for h in range(2):
            for d in range(1, RING):
                i = h * (RING - 1) + d
                copy = send(
                    small.at[0], small.at[i], w_ss.at[i], w_rs.at[i], camera_peer(h, d)
                )
                copy.start()
                w_copies.append(copy)

        has_north = jnp.where(gx > 0, 1.0, 0.0)
        has_south = jnp.where(gx < n_gx - 1, 1.0, 0.0)
        has_west = jnp.where(gy > 0, 1.0, 0.0)
        has_east = jnp.where(gy < n_gy - 1, 1.0, 0.0)

        def column_rims(pad, index, source, lane_at):
            for side, has, at in ((0, has_west, 0), (1, has_east, col1)):
                value = source[side, :, lane_at : lane_at + 1] * has
                pad[(*index, slice(row0, row1), slice(at, at + LANES))] = jnp.broadcast_to(
                    value, (rows, LANES)
                )

        for copy in rims0:
            copy.wait_recv()
        kpad[first - 1 : first, col0:col1] = ns0_recv[0, 1:2] * has_north
        kpad[last + 1 : last + 2, col0:col1] = ns0_recv[1, 1:2] * has_south
        column_rims(kpad, (), ew0_recv, 1)
        tpad[top, first - 1 : first, col0:col1] = ns0_recv[0, 0:1] * has_north
        tpad[top, last + 1 : last + 2, col0:col1] = ns0_recv[1, 0:1] * has_south
        column_rims(tpad, (top,), ew0_recv, 0)

        def around(pad, index, r):
            a, b = row0 + r * TR, row0 + (r + 1) * TR
            return (
                pad[(*index, slice(a, b), slice(col0, col1))],
                pad[(*index, slice(a, b), slice(col0 + 1, col1 + 1))],
                pad[(*index, slice(a, b), slice(col0 - 1, col1 - 1))],
                pad[(*index, slice(a - 1, b - 1), slice(col0, col1))],
                pad[(*index, slice(a + 1, b + 1), slice(col0, col1))],
            )

        for r in range(strips):
            kc, ke, kw, kn, ks = around(kpad, (), r)
            strip = slice(r * TR, (r + 1) * TR)
            faces = [0.5 * RATE_PLANE * (kc + other) for other in (ke, kw, kn, ks)]
            for i in range(4):
                coef[i, strip] = faces[i]
            tc, te, tw, tn, ts = around(tpad, (top,), r)
            under = tpad[top - 1, row0 + r * TR : row0 + (r + 1) * TR, col0:col1]
            value = tc + RATE_VERTICAL * (under - tc)
            for face, other in zip(faces, (te, tw, tn, ts)):
                value = value + face * (other - tc)
            for u in range(tile_cols):
                tiles3[r * tile_cols + u] = value[:, u * TC : (u + 1) * TC]

        x_copies, slots1 = [], {}
        for c in range(n_chunks):
            for rr in range(wide // TC):
                gat[c, 0, 0, :, rr * TC : (rr + 1) * TC] = tiles3[:, c * (wide // TC) + rr, :]
            x_copies.append(
                send(gat.at[c, 0, 0], gat.at[c, 1, 0], x_ss.at[c], x_rs.at[c], partner)
            )
            for f in range(2):
                for d in range(1, RING):
                    i = (c * 2 + f) * RING + d
                    slots1[c, f, d] = send(
                        gat.at[c, f, 0], gat.at[c, f, d], s1_ss.at[i], s1_rs.at[i], plate_peer(c, -d)
                    )
            x_copies[c].start()
            for d in FARTHEST_FIRST:
                slots1[c, 0, d].start()

        def pass_far(c):
            x_copies[c].wait_recv()
            for d in FARTHEST_FIRST:
                slots1[c, 1, d].start()

        for load in loads[2:4]:
            load.wait()
        for side, row in ((0, first), (1, last)):
            ns_send[side, 0:top] = tpad[0:top, row, col0:col1]
            ns_send[side, layers : layers + top] = apad[0:top, row, col0:col1]
        for side, col in ((0, col0), (1, col1 - 1)):
            packed = jnp.zeros((rows, LANES), F32)
            for l in range(top):
                packed = jnp.where(rim_lane == l, tpad[l, row0:row1, col : col + 1], packed)
                packed = jnp.where(
                    rim_lane == layers + l, apad[l, row0:row1, col : col + 1], packed
                )
            ew_send[side] = packed
        rims = rim_copies(ns_send, ns_recv, ew_send, ew_recv, rim_ss, rim_rs)
        for copy in rims:
            copy.start()


        pass_far(0)
        for copy in w_copies:
            copy.wait_recv()
        turned = jnp.transpose(small[...].reshape(2 * RING * TR, LANES))[0:tiles]
        lane_tile = iota((tiles, 2 * ring), 1)

        def weigh_matrix(h):
            for d in range(RING):
                i = (h * (RING - 1) + d) * TR if d else 0
                code = turned[:, i : i + k_blocks].astype(jnp.int32)
                weight = turned[:, i + k_blocks : i + 2 * k_blocks]
                plate = code >> ((tiles * n_gy).bit_length() - 1)
                far = ((plate ^ gx) >> 2) & 1
                dz = ((plate >> 3) - gx_z) & 3
                dy = (plate - gx) & 3
                here, step = (dz, dy) if h == 0 else (dy, dz)
                at = jnp.where(here == 0, far * ring + step * tiles + (code & (tiles - 1)), -1)
                total = jnp.zeros((tiles, 2 * ring), F32)
                for k in range(k_blocks):
                    hit = at[:, k : k + 1] == lane_tile
                    total = total + jnp.where(hit, weight[:, k : k + 1], 0.0)
                wfull[h, d * tiles : (d + 1) * tiles] = total
                for i, piece in enumerate(two_parts(total)):
                    for f in range(2):
                        lhs1[h, f, i * ring + d * tiles : i * ring + (d + 1) * tiles] = piece[
                            :, f * ring : (f + 1) * ring
                        ]

        weigh_matrix(0)
        pass_far(1)
        weigh_matrix(1)
        pass_far(2)
        pass_far(3)

        def weigh(lhs, value):
            hi, lo = two_parts(value)
            both = jnp.dot(lhs[...], hi, preferred_element_type=F32)
            more = jnp.dot(lhs[0:ring], lo, preferred_element_type=F32)
            return both[0:ring] + (both[ring : 2 * ring] + more)

        for h in range(2):
            for i, piece in enumerate(two_parts(jnp.transpose(wfull[h]))):
                for f in range(2):
                    lhs2[h, f, i * ring : (i + 1) * ring] = piece[f * ring : (f + 1) * ring]

        edge = jnp.zeros((rows, LANES), F32)
        apad[top, row0:row1, 0:col0] = edge
        apad[top, row0:row1, col1 : col1 + LANES] = edge
        apad[top, first - 1 : first, col0:col1] = jnp.zeros((1, cols), F32)
        apad[top, last + 1 : last + 2, col0:col1] = jnp.zeros((1, cols), F32)

        for copy in rims:
            copy.wait_recv()
        for l in range(top):
            column_rims(tpad, (l,), ew_recv, l)
            column_rims(apad, (l,), ew_recv, layers + l)
        tpad[0:top, first - 1, col0:col1] = ns_recv[0, 0:top] * has_north
        tpad[0:top, last + 1, col0:col1] = ns_recv[1, 0:top] * has_south
        apad[0:top, first - 1, col0:col1] = ns_recv[0, layers : layers + top] * has_north
        apad[0:top, last + 1, col0:col1] = ns_recv[1, layers : layers + top] * has_south

        def layer_step(l, r, total):
            strip = slice(r * TR, (r + 1) * TR)
            tc, *t_near = around(tpad, (l,), r)
            ac, *a_near = around(apad, (l,), r)
            flow = jnp.zeros_like(ac)
            for i in range(4):
                step = a_near[i] - ac
                flow = flow + coef[i, strip] * step
                total = total + (t_near[i] - tc) * step
            return ac + flow, ac, total

        def inner_layers(r):
            strip = slice(r * TR, (r + 1) * TR)
            inner = slice(row0 + r * TR, row0 + (r + 1) * TR)

            def body(l, total):
                value, ac, total = layer_step(l, r, total)
                above = apad[l + 1, inner, col0:col1]
                under = apad[jnp.maximum(l - 1, 0), inner, col0:col1]
                outv[l, strip] = value + RATE_VERTICAL * ((above - ac) + (under - ac))
                return total

            gacc[strip] = lax.fori_loop(0, top, body, jnp.zeros((TR, cols), F32))

        for r in range(0, 2):
            inner_layers(r)

        loads[4].wait()
        loads[5].wait()
        i = (2 * RING - 1) * TR
        frame = turned[:, i : i + 1].astype(jnp.int32)

        def columns(c):
            return slice(c * wide, (c + 1) * wide)

        for c in range(n_chunks):
            seen = jnp.zeros((tiles, wide), F32)
            for f in range(frames):
                seen = jnp.where(frame == f, obs_v[f, :, columns(c)], seen)
            mis[c, 0] = -seen

        parts, spread = {}, {}
        for c in range(n_chunks):
            for d in range(1, RING):
                i = c * RING + d
                parts[c, d] = send(
                    part.at[c, d], part_recv.at[c, d], p_ss.at[i], p_rs.at[i], camera_peer(c, -d)
                )
                spread[c, d] = send(
                    mis.at[c, 0], mis.at[c, d], m_ss.at[i], m_rs.at[i], camera_peer(c, d)
                )
        for f in range(2):
            for c in range(n_chunks):
                for d in range(1, RING):
                    slots1[c, f, d].wait_recv()
                value = weigh(lhs1.at[c % 2, f], gat[c, f].reshape(ring, wide))
                value = value.reshape(RING, tiles, wide)
                if f == 0:
                    part[c] = value
                else:
                    part[c] += value
                    for d in FARTHEST_FIRST:
                        parts[c, d].start()

        inner_layers(2)

        mis_copies = []
        for c in range(n_chunks):
            for d in range(1, RING):
                parts[c, d].wait_recv()
            mis[c, 0] += (part[c, 0] + part_recv[c, 1]) + (part_recv[c, 2] + part_recv[c, 3])
            for d in FARTHEST_FIRST:
                spread[c, d].start()
            copy = pltpu.make_async_copy(
                mis.at[c, 0], misfit_out.at[:, columns(c)], out_sem.at[4 + c]
            )
            copy.start()
            mis_copies.append(copy)

        inner_layers(3)

        back = {}
        for f in (1, 0):
            for c in range(n_chunks):
                if f == 1:
                    for d in range(1, RING):
                        spread[c, d].wait_recv()
                value = weigh(lhs2.at[c % 2, f], mis[c].reshape(ring, wide))
                con[c, f] = value.reshape(RING, tiles, wide)
                for d in FARTHEST_FIRST:
                    i = (c * 2 + f) * RING + d
                    back[c, f, d] = send(
                        con.at[c, f, d], con_recv.at[c, f, d], s2_ss.at[i], s2_rs.at[i], plate_peer(c, d)
                    )
                    back[c, f, d].start()

        for r in range(4, strips):
            inner_layers(r)
        early = pltpu.make_async_copy(
            outv.at[0 : top - 1], adj_out.at[0 : top - 1], out_sem.at[0]
        )
        early.start()
        sent = rims0 + rims + w_copies + x_copies
        for group in (slots1, parts, spread):
            sent.extend(group.values())
        for copy in sent:
            copy.wait_send()

        def gathered(c, f):
            for d in range(1, RING):
                back[c, f, d].wait_recv()
            return (con[c, f, 0] + con_recv[c, f, 1]) + (con_recv[c, f, 2] + con_recv[c, f, 3])

        xa_copies = []
        for c in range(n_chunks):
            xa_send[c] = gathered(c, 1)
            i = n_chunks + c
            copy = send(xa_send.at[c], xa_recv.at[c], x_ss.at[i], x_rs.at[i], partner)
            copy.start()
            xa_copies.append(copy)
        for c in range(n_chunks):
            near = gathered(c, 0)
            xa_copies[c].wait_recv()
            added = near + xa_recv[c]
            for rr in range(wide // TC):
                tiles3[:, c * (wide // TC) + rr, :] = added[:, rr * TC : (rr + 1) * TC]
        for r in range(strips):
            strip = slice(r * TR, (r + 1) * TR)
            inner = slice(row0 + r * TR, row0 + (r + 1) * TR)
            extra = jnp.concatenate(
                [tiles3[r * tile_cols + u] for u in range(tile_cols)], axis=1
            )
            apad[top, inner, col0:col1] += extra
            outv[top - 1, strip] += RATE_VERTICAL * extra

        for side, row in ((0, first), (1, last)):
            ns2_send[side] = apad[top, row : row + 1, col0:col1]
        for side, col in ((0, col0), (1, col1 - 1)):
            ew2_send[side] = jnp.broadcast_to(
                apad[top, row0:row1, col : col + 1], (rows, LANES)
            )
        rims2 = rim_copies(ns2_send, ns2_recv, ew2_send, ew2_recv, rim2_ss, rim2_rs)
        for copy in rims2:
            copy.start()
        late = pltpu.make_async_copy(
            outv.at[top - 1], adj_out.at[top - 1], out_sem.at[2]
        )
        late.start()
        for r in range(strips):
            strip = slice(r * TR, (r + 1) * TR)
            inner = slice(row0 + r * TR, row0 + (r + 1) * TR)
            value, ac, total = layer_step(top, r, gacc[strip])
            under = apad[top - 1, inner, col0:col1]
            outv[top, strip] = value + RATE_VERTICAL * (under - ac)
            gradv[strip] = gin[strip] - (0.5 * RATE_PLANE) * total
        for copy in list(back.values()) + xa_copies:
            copy.wait_send()

        for copy in rims2:
            copy.wait_recv()
        for side, has, row, beyond in ((0, has_north, 0, first - 1), (1, has_south, rows - 1, last + 1)):
            at = slice(row, row + 1)
            rim = ns2_recv[side] * has
            slope = tpad[top, beyond : beyond + 1, col0:col1] - tpad[
                top, row0 + row : row0 + row + 1, col0:col1
            ]
            outv[top, at] += coef[2 + side, at] * rim
            gradv[at] -= (0.5 * RATE_PLANE) * slope * rim
        for side, has, face, at, beyond, edge_lane in (
            (0, has_west, 1, 0, 0, 0),
            (1, has_east, 0, cols - LANES, col1, LANES - 1),
        ):
            at = slice(at, at + LANES)
            rim = jnp.where(rim_lane == edge_lane, ew2_recv[side] * has, 0.0)
            slope = tpad[top, row0:row1, beyond : beyond + LANES] - tpad[
                top, row0:row1, col0 + at.start : col0 + at.stop
            ]
            outv[top, :, at] += coef[face, :, at] * rim
            gradv[:, at] -= (0.5 * RATE_PLANE) * slope * rim

        last_copies = [
            pltpu.make_async_copy(outv.at[top], adj_out.at[top], out_sem.at[3]),
            pltpu.make_async_copy(gradv, grad_out, out_sem.at[1]),
        ]
        for copy in last_copies:
            copy.start()
        for copy in rims2:
            copy.wait_send()
        for copy in [early, late] + mis_copies + last_copies:
            copy.wait()

    dma = pltpu.SemaphoreType.DMA

    def vmem(*shape, dtype=F32):
        return pltpu.VMEM(shape, dtype)

    def pair(*shape):
        return [vmem(*shape), vmem(*shape)]

    tile = TR * TC
    scratch = [
        vmem(layers, rows + 2 * TR, cols + 2 * LANES),
        vmem(layers, rows + 2 * TR, cols + 2 * LANES),
        vmem(rows + 2 * TR, cols + 2 * LANES),
        vmem(rows, cols),
        vmem(frames, tiles, tile),
        vmem(4, rows, cols),
        vmem(rows, cols),
        vmem(layers, rows, cols),
        vmem(rows, cols),
        *pair(2, 2, cols),
        *pair(2, rows, LANES),
        *pair(2, 2 * layers, cols),
        *pair(2, rows, LANES),
        *pair(2, 1, cols),
        *pair(2, rows, LANES),
        vmem(2 * RING, TR, LANES),
        vmem(tiles, TR, TC),
        vmem(2, ring, 2 * ring),
        vmem(2, 2, 2 * ring, ring, dtype=BF16),
        vmem(2, 2, 2 * ring, ring, dtype=BF16),
        vmem(n_chunks, 2, RING, tiles, wide),
        *pair(n_chunks, RING, tiles, wide),
        vmem(n_chunks, RING, tiles, wide),
        *pair(n_chunks, 2, RING, tiles, wide),
        *pair(n_chunks, tiles, wide),
        dma((6,)),
        dma((4 + n_chunks,)),
        *[dma((4,)) for _ in range(6)],
        dma((2 * n_chunks,)), dma((2 * n_chunks,)),
        dma((2 * RING,)), dma((2 * RING,)),
        dma((2 * n_chunks * RING,)), dma((2 * n_chunks * RING,)),
        dma((n_chunks * RING,)), dma((n_chunks * RING,)),
        dma((n_chunks * RING,)), dma((n_chunks * RING,)),
        dma((2 * n_chunks * RING,)), dma((2 * n_chunks * RING,)),
    ]
    in_hbm = pl.BlockSpec(memory_space=pltpu.HBM)
    anywhere = pl.BlockSpec(memory_space=pl.ANY)
    in_vmem = pl.BlockSpec(memory_space=pltpu.VMEM)
    return pl.pallas_call(
        kernel,
        out_shape=(
            jax.ShapeDtypeStruct((tiles, tile), F32),
            jax.ShapeDtypeStruct((layers, rows, cols), F32),
            jax.ShapeDtypeStruct((rows, cols), F32),
        ),
        in_specs=[in_hbm] * 5 + [in_vmem] * 3,
        out_specs=[anywhere] * 3,
        scratch_shapes=scratch,
        compiler_params=pltpu.CompilerParams(
            collective_id=0, has_side_effects=True, vmem_limit_bytes=48 * 1024 * 1024
        ),
    )


def solution(mesh):
    n_gx, n_gy = mesh.shape["gx"], mesh.shape["gy"]

    def local(temp, cond, adj, grad, obs, frame_index, source_map, source_weight):
        layers, rows, cols = temp.shape
        call = make_kernel(n_gx, n_gy, layers, rows, cols, obs.shape[0], source_map.shape[1])
        operands = (
            temp, cond, adj, grad, obs, frame_index[None, :], source_map.T, source_weight.T
        )
        return call(*(pltpu.with_memory_space_constraint(x, pltpu.HBM) for x in operands))

    placed = (
        P(None, "gx", "gy"),
        P("gx", "gy"),
        P(None, "gx", "gy"),
        P("gx", "gy"),
        P(None, ("gx", "gy"), None),
        P(("gx", "gy")),
        P(("gx", "gy"), None),
        P(("gx", "gy"), None),
    )
    return jax.shard_map(
        local,
        mesh=mesh,
        in_specs=placed,
        out_specs=(P(("gx", "gy"), None), P(None, "gx", "gy"), P("gx", "gy")),
        check_vma=False,
    )
```

```python
import jax
import jax.numpy as jnp
from jax import lax
from jax.experimental import pallas as pl
from jax.experimental.pallas import tpu as pltpu
from jax.sharding import PartitionSpec as P

TR = 8
TC = 128
CAP = 16
LANES = 128
RATE_PLANE = 0.2
RATE_VERTICAL = 0.08
MESH = pl.DeviceIdType.MESH
F32 = jnp.float32
BF16 = jnp.bfloat16


def iota(shape, dim):
    return lax.broadcasted_iota(jnp.int32, shape, dim)


def two_parts(x):
    hi = x.astype(BF16)
    lo = (x - hi.astype(F32)).astype(BF16)
    return hi, lo


RING = 4
PLANE = RING * RING
FARTHEST_FIRST = (2, 1, 3)


def make_kernel(n_gx, n_gy, layers, rows, cols, frames, k_blocks):
    tiles = (rows // TR) * (cols // TC)
    half = PLANE * CAP
    n_slots = 2 * half
    row0, col0 = TR, LANES
    row1, col1 = row0 + rows, col0 + cols
    strips = rows // TR
    tile_cols = cols // TC
    top = layers - 1
    per_group = LANES // CAP
    groups = PLANE // per_group
    others = range(1, PLANE)
    n_chunks = 4
    wide = cols // n_chunks

    def kernel(
        temp, cond, adj, grad, obs, frame_in, map_in, weight_in,
        misfit_out, outv, gradv,
        tpad, apad, kpad, gin, obs_v, coef, gacc, map_v, weight_v, frame_v,
        ns0_send, ns0_recv, ew0_send, ew0_recv,
        ns_send, ns_recv, ew_send, ew_recv,
        ns2_send, ns2_recv, ew2_send, ew2_recv,
        small, req_send, req_recv, tiles3, onehot, lhs1, rhs,
        wsend, wblk, wcat, lhs2,
        x_send, x_recv, xa_send, xa_recv,
        send1, recv1, part, part_recv, mis, mis_recv, send2, recv2,
        in_sem,
        rim0_ss, rim0_rs, rim_ss, rim_rs, rim2_ss, rim2_rs, x_ss, x_rs,
        req_ss, req_rs, w_ss, w_rs, s1_ss, s1_rs, p_ss, p_rs, m_ss, m_rs, s2_ss, s2_rs,
    ):
        gx = lax.axis_index("gx")
        gy = lax.axis_index("gy")
        gx_y = lax.rem(gx, RING)
        gx_x = lax.rem(gx // RING, 2)
        gx_z = gx // (2 * RING)
        north, south = lax.rem(gx + n_gx - 1, n_gx), lax.rem(gx + 1, n_gx)
        west, east = lax.rem(gy + n_gy - 1, n_gy), lax.rem(gy + 1, n_gy)
        sides = ({"gx": north}, {"gx": south}, {"gy": west}, {"gy": east})
        partner = {"gx": gx + RING - 2 * RING * gx_x}

        def along(dz, dy):
            z = lax.rem(gx_z + dz % RING, RING)
            y = lax.rem(gx_y + dy % RING, RING)
            return {"gx": z * (2 * RING) + gx_x * RING + y}

        def slot_peer(h, d):
            return along(0, d) if h == 0 else along(d, 0)

        def dense_peer(h, d):
            return along(d, 0) if h == 0 else along(0, d)

        def send(src, dst, ss, rs, device):
            return pltpu.make_async_remote_copy(
                src_ref=src,
                dst_ref=dst,
                send_sem=ss,
                recv_sem=rs,
                device_id=device,
                device_id_type=MESH,
            )

        body_at = (slice(row0, row1), slice(col0, col1))
        loads = [
            pltpu.make_async_copy(
                temp.at[top - 1 : layers],
                tpad.at[(slice(top - 1, layers), *body_at)],
                in_sem.at[0],
            ),
            pltpu.make_async_copy(cond, kpad.at[body_at], in_sem.at[1]),
            pltpu.make_async_copy(
                temp.at[0 : top - 1], tpad.at[(slice(0, top - 1), *body_at)], in_sem.at[2]
            ),
            pltpu.make_async_copy(adj, apad.at[(slice(None), *body_at)], in_sem.at[3]),
            pltpu.make_async_copy(grad, gin, in_sem.at[4]),
            pltpu.make_async_copy(obs, obs_v, in_sem.at[5]),
            pltpu.make_async_copy(map_in, map_v, in_sem.at[6]),
            pltpu.make_async_copy(weight_in, weight_v, in_sem.at[7]),
            pltpu.make_async_copy(frame_in, frame_v, in_sem.at[8]),
        ]
        for load in loads[:2]:
            load.start()

        barrier = pltpu.get_barrier_semaphore()
        greeted = [along(b % RING, b // RING) for b in others] + [partner] + list(sides)
        for device in greeted:
            pl.semaphore_signal(barrier, inc=1, device_id=device, device_id_type=MESH)

        for load in loads[6:] + loads[2:6]:
            load.start()

        for load in loads[:2]:
            load.wait()
        first, last = row0, row1 - 1
        rim_lane = iota((rows, LANES), 1)
        for side, row in ((0, first), (1, last)):
            ns0_send[side, 0:1] = tpad[top, row : row + 1, col0:col1]
            ns0_send[side, 1:2] = kpad[row : row + 1, col0:col1]
        for side, col in ((0, col0), (1, col1 - 1)):
            ew0_send[side] = jnp.where(
                rim_lane == 0,
                tpad[top, row0:row1, col : col + 1],
                kpad[row0:row1, col : col + 1],
            )

        pl.semaphore_wait(barrier, len(greeted))

        def rim_copies(ns_s, ns_r, ew_s, ew_r, ss, rs):
            copies = []
            for i in range(4):
                src, dst = (ns_s, ns_r) if i < 2 else (ew_s, ew_r)
                copies.append(
                    pltpu.make_async_remote_copy(
                        src_ref=src.at[i % 2],
                        dst_ref=dst.at[1 - i % 2],
                        send_sem=ss.at[i],
                        recv_sem=rs.at[i],
                        device_id=sides[i],
                        device_id_type=MESH,
                    )
                )
            return copies

        rims0 = rim_copies(ns0_send, ns0_recv, ew0_send, ew0_recv, rim0_ss, rim0_rs)
        for copy in rims0:
            copy.start()

        for load in loads[6:]:
            load.wait()
        small[0:k_blocks, 0:tiles] = map_v[...].astype(F32)
        small[k_blocks : 2 * k_blocks, 0:tiles] = weight_v[...]
        small[2 * k_blocks : 2 * k_blocks + 1, 0:tiles] = frame_v[...].astype(F32)
        columns_of = jnp.transpose(small[...])[0:tiles]
        weight = columns_of[:, k_blocks : 2 * k_blocks]
        code = columns_of[:, 0:k_blocks].astype(jnp.int32)
        plate = code >> ((tiles * n_gy).bit_length() - 1)
        far = ((plate ^ gx) >> 2) & 1
        dz = ((plate >> 3) - gx_z) & 3
        dy = (plate - gx) & 3
        block = far * PLANE + dy * RING + dz
        wish = ((code & (tiles - 1)) + 1).astype(F32)
        lane = iota((tiles, LANES), 1)
        lane_slot = iota((tiles, n_slots), 1)
        below = jnp.where(iota((tiles, tiles), 0) > iota((tiles, tiles), 1), 1.0, 0.0)
        hits = [jnp.where(block[:, k : k + 1] == lane, 1.0, 0.0) for k in range(k_blocks)]
        before = jnp.dot(below, jnp.concatenate(hits, axis=1), preferred_element_type=F32)
        base = jnp.zeros((1, LANES), F32)
        wanted = jnp.zeros((tiles, n_slots), F32)
        weights = [jnp.zeros((tiles, n_slots), F32) for _ in range(2)]
        for k in range(k_blocks):
            earlier = before[:, k * LANES : (k + 1) * LANES] + base
            base = base + jnp.sum(hits[k], axis=0, keepdims=True)
            rank = jnp.sum(hits[k] * earlier, axis=1, keepdims=True).astype(jnp.int32)
            col = slice(k, k + 1)
            here = block[:, col] * CAP + rank == lane_slot
            wanted = wanted + jnp.where(here, wish[:, col], 0.0)
            for h, (dense, slot) in enumerate(((dz, dy), (dy, dz))):
                at = (dense * LANES + far * (LANES // 2) + slot * CAP)[:, col] + rank
                weights[h] = weights[h] + jnp.where(at == lane_slot, weight[:, col], 0.0)
        for h in range(2):
            for d in range(RING):
                wsend[h, d] = weights[h][:, d * LANES : (d + 1) * LANES]
            wblk[h, 0] = weights[h][:, 0:LANES]
        asked = jnp.sum(wanted, axis=0, keepdims=True)
        for g in range(groups):
            for f in range(2):
                at = f * half + g * LANES
                req_send[g, f : f + 1] = asked[:, at : at + LANES]

        req_copies = []
        for b in others:
            copy = send(
                req_send.at[b // per_group],
                req_recv.at[b],
                req_ss.at[b],
                req_rs.at[b],
                along(b % RING, b // RING),
            )
            copy.start()
            req_copies.append(copy)
        w_copies = []
        for h in range(2):
            for d in range(1, RING):
                i = h * RING + d
                copy = send(
                    wsend.at[h, d], wblk.at[h, d], w_ss.at[i], w_rs.at[i], dense_peer(h, d)
                )
                copy.start()
                w_copies.append(copy)
        req_recv[0] = req_send[0]

        has_north = jnp.where(gx > 0, 1.0, 0.0)
        has_south = jnp.where(gx < n_gx - 1, 1.0, 0.0)
        has_west = jnp.where(gy > 0, 1.0, 0.0)
        has_east = jnp.where(gy < n_gy - 1, 1.0, 0.0)

        def column_rims(pad, index, source, lane_at):
            for side, has, at in ((0, has_west, 0), (1, has_east, col1)):
                value = source[side, :, lane_at : lane_at + 1] * has
                pad[(*index, slice(row0, row1), slice(at, at + LANES))] = jnp.broadcast_to(
                    value, (rows, LANES)
                )

        for copy in rims0:
            copy.wait_recv()
        kpad[first - 1 : first, col0:col1] = ns0_recv[0, 1:2] * has_north
        kpad[last + 1 : last + 2, col0:col1] = ns0_recv[1, 1:2] * has_south
        column_rims(kpad, (), ew0_recv, 1)
        tpad[top, first - 1 : first, col0:col1] = ns0_recv[0, 0:1] * has_north
        tpad[top, last + 1 : last + 2, col0:col1] = ns0_recv[1, 0:1] * has_south
        column_rims(tpad, (top,), ew0_recv, 0)

        def around(pad, index, r):
            a, b = row0 + r * TR, row0 + (r + 1) * TR
            return (
                pad[(*index, slice(a, b), slice(col0, col1))],
                pad[(*index, slice(a, b), slice(col0 + 1, col1 + 1))],
                pad[(*index, slice(a, b), slice(col0 - 1, col1 - 1))],
                pad[(*index, slice(a - 1, b - 1), slice(col0, col1))],
                pad[(*index, slice(a + 1, b + 1), slice(col0, col1))],
            )

        for r in range(strips):
            kc, ke, kw, kn, ks = around(kpad, (), r)
            strip = slice(r * TR, (r + 1) * TR)
            faces = [0.5 * RATE_PLANE * (kc + other) for other in (ke, kw, kn, ks)]
            for i in range(4):
                coef[i, strip] = faces[i]
            tc, te, tw, tn, ts = around(tpad, (top,), r)
            under = tpad[top - 1, row0 + r * TR : row0 + (r + 1) * TR, col0:col1]
            value = tc + RATE_VERTICAL * (under - tc)
            for face, other in zip(faces, (te, tw, tn, ts)):
                value = value + face * (other - tc)
            for u in range(tile_cols):
                tiles3[r * tile_cols + u] = value[:, u * TC : (u + 1) * TC]

        x_copies = []
        for i in range(2):
            for rr in range(TR // 2):
                x_send[i, :, rr * TC : (rr + 1) * TC] = tiles3[:, i * (TR // 2) + rr, :]
            copy = send(x_send.at[i], x_recv.at[i], x_ss.at[i], x_rs.at[i], partner)
            copy.start()
            x_copies.append(copy)

        for copy in req_copies:
            copy.wait_recv()
        group_lane = iota((per_group, LANES), 1) // CAP
        group_row = iota((per_group, LANES), 0)
        tile_row = iota((tiles, LANES), 0).astype(F32)
        for f in range(2):
            picks = []
            for g in range(groups):
                block = req_recv[g * per_group : (g + 1) * per_group, f, :]
                line = jnp.sum(
                    jnp.where(group_lane == group_row, block, 0.0), axis=0, keepdims=True
                )
                picks.append(jnp.where(line - 1.0 == tile_row, 1.0, 0.0))
            pick = jnp.concatenate(picks, axis=1)
            onehot[:, f * half : (f + 1) * half] = pick
            turned = jnp.transpose(jnp.concatenate([pick, pick], axis=0)).astype(BF16)
            lhs1[f * half : (f + 1) * half] = turned

        def plane_rows(ref, c, f, d):
            return ref.at[c, f, d] if c % 2 == 0 else ref.at[c, f, :, d]

        slots1 = {}
        for c in range(n_chunks):
            for f in range(2):
                for d in range(1, RING):
                    i = (c * 2 + f) * RING + d
                    slots1[c, f, d] = send(
                        plane_rows(send1, c, f, d),
                        recv1.at[c, :, f, d],
                        s1_ss.at[i],
                        s1_rs.at[i],
                        slot_peer(c % 2, -d),
                    )

        def columns(c, count=1):
            return slice(c * wide, (c + count) * wide)

        def pack_tiles(f, pair, source):
            for i, piece in enumerate(two_parts(source)):
                rhs[i * tiles : (i + 1) * tiles, columns(pair, 2)] = piece
            for c in (pair, pair + 1):
                packed = jnp.dot(
                    lhs1[f * half : (f + 1) * half],
                    rhs[:, columns(c)],
                    preferred_element_type=F32,
                )
                send1[c, f] = packed.reshape(RING, RING, CAP, wide)
                for d in FARTHEST_FIRST:
                    slots1[c, f, d].start()
                recv1[c, :, f, 0] = send1[c, f, 0] if c % 2 == 0 else send1[c, f, :, 0]

        for pair in (0, 2):
            pack_tiles(0, pair, x_send[pair // 2])

        for load in loads[2:4]:
            load.wait()
        for side, row in ((0, first), (1, last)):
            ns_send[side, 0:top] = tpad[0:top, row, col0:col1]
            ns_send[side, layers : layers + top] = apad[0:top, row, col0:col1]
        for side, col in ((0, col0), (1, col1 - 1)):
            packed = jnp.zeros((rows, LANES), F32)
            for l in range(top):
                packed = jnp.where(rim_lane == l, tpad[l, row0:row1, col : col + 1], packed)
                packed = jnp.where(
                    rim_lane == layers + l, apad[l, row0:row1, col : col + 1], packed
                )
            ew_send[side] = packed
        rims = rim_copies(ns_send, ns_recv, ew_send, ew_recv, rim_ss, rim_rs)
        for copy in rims:
            copy.start()

        for copy in w_copies:
            copy.wait_recv()
        for h in range(2):
            for d in range(RING):
                for i, piece in enumerate(two_parts(wblk[h, d])):
                    wcat[h, d, i * tiles : (i + 1) * tiles] = jnp.concatenate(
                        [piece, piece], axis=1
                    )

        for pair in (0, 2):
            x_copies[pair // 2].wait_recv()
            pack_tiles(1, pair, x_recv[pair // 2])

        for h in range(2):
            for d in range(RING):
                parts_of = jnp.concatenate(two_parts(wblk[h, d]), axis=0).astype(F32)
                turned = jnp.transpose(parts_of).astype(BF16)
                lhs2[h, d, :, 0 : 2 * tiles] = turned
                lhs2[h, d, :, 2 * tiles : 4 * tiles] = turned

        edge = jnp.zeros((rows, LANES), F32)
        apad[top, row0:row1, 0:col0] = edge
        apad[top, row0:row1, col1 : col1 + LANES] = edge
        apad[top, first - 1 : first, col0:col1] = jnp.zeros((1, cols), F32)
        apad[top, last + 1 : last + 2, col0:col1] = jnp.zeros((1, cols), F32)

        for copy in rims:
            copy.wait_recv()
        for l in range(top):
            column_rims(tpad, (l,), ew_recv, l)
            column_rims(apad, (l,), ew_recv, layers + l)
        tpad[0:top, first - 1, col0:col1] = ns_recv[0, 0:top] * has_north
        tpad[0:top, last + 1, col0:col1] = ns_recv[1, 0:top] * has_south
        apad[0:top, first - 1, col0:col1] = ns_recv[0, layers : layers + top] * has_north
        apad[0:top, last + 1, col0:col1] = ns_recv[1, layers : layers + top] * has_south

        def layer_step(l, r, total):
            strip = slice(r * TR, (r + 1) * TR)
            tc, *t_near = around(tpad, (l,), r)
            ac, *a_near = around(apad, (l,), r)
            flow = jnp.zeros_like(ac)
            for i in range(4):
                step = a_near[i] - ac
                flow = flow + coef[i, strip] * step
                total = total + (t_near[i] - tc) * step
            return ac + flow, ac, total

        def inner_layers(r):
            strip = slice(r * TR, (r + 1) * TR)
            inner = slice(row0 + r * TR, row0 + (r + 1) * TR)

            def body(l, total):
                value, ac, total = layer_step(l, r, total)
                above = apad[l + 1, inner, col0:col1]
                under = apad[jnp.maximum(l - 1, 0), inner, col0:col1]
                outv[l, strip] = value + RATE_VERTICAL * ((above - ac) + (under - ac))
                return total

            gacc[strip] = lax.fori_loop(0, top, body, jnp.zeros((TR, cols), F32))

        for r in range(0, 2):
            inner_layers(r)

        loads[4].wait()
        loads[5].wait()
        frame = columns_of[:, 2 * k_blocks : 2 * k_blocks + 1].astype(jnp.int32)
        for c in range(n_chunks):
            seen = jnp.zeros((tiles, wide), F32)
            for f in range(frames):
                seen = jnp.where(frame == f, obs_v[f, :, columns(c)], seen)
            mis[c] = -seen

        def weigh(c, d):
            both = jnp.dot(
                wcat[c % 2, d],
                jnp.concatenate(two_parts(recv1[c, d].reshape(LANES, wide)), axis=0),
                preferred_element_type=F32,
            )
            return both[0:tiles] + both[tiles : 2 * tiles]

        parts, spread = {}, {}
        for c in range(n_chunks):
            for d in range(1, RING):
                i = c * RING + d
                parts[c, d] = send(
                    part.at[c, d],
                    part_recv.at[c, d],
                    p_ss.at[i],
                    p_rs.at[i],
                    dense_peer(c % 2, -d),
                )
                spread[c, d] = send(
                    mis.at[c], mis_recv.at[c, d], m_ss.at[i], m_rs.at[i], dense_peer(c % 2, d)
                )
        for c in range(n_chunks):
            for f in range(2):
                for d in range(1, RING):
                    slots1[c, f, d].wait_recv()
            for d in FARTHEST_FIRST:
                part[c, d] = weigh(c, d)
                parts[c, d].start()
            mis[c] += weigh(c, 0)

        inner_layers(2)

        for c in range(n_chunks):
            for d in range(1, RING):
                parts[c, d].wait_recv()
            mis[c] += part_recv[c, 1] + (part_recv[c, 2] + part_recv[c, 3])
            for d in FARTHEST_FIRST:
                spread[c, d].start()
            misfit_out[:, columns(c)] = mis[c]

        inner_layers(3)

        slots2 = {}
        for c in range(n_chunks):
            for f in range(2):
                for d in range(1, RING):
                    i = (c * 2 + f) * RING + d
                    slots2[c, f, d] = send(
                        send2.at[c, :, f, d],
                        plane_rows(recv2, c, f, d),
                        s2_ss.at[i],
                        s2_rs.at[i],
                        slot_peer(c % 2, d),
                    )
        for c in range(n_chunks):
            for d in range(RING):
                if d:
                    spread[c, d].wait_recv()
                mh, ml = two_parts(mis_recv[c, d] if d else mis[c])
                packed = jnp.dot(
                    lhs2[c % 2, d],
                    jnp.concatenate([mh, mh, ml, ml], axis=0),
                    preferred_element_type=F32,
                )
                send2[c, d] = packed.reshape(2, RING, CAP, wide)
            for d in FARTHEST_FIRST:
                slots2[c, 1, d].start()
        for c in range(n_chunks):
            for d in FARTHEST_FIRST:
                slots2[c, 0, d].start()
        for c in range(n_chunks):
            for f in range(2):
                if c % 2 == 0:
                    recv2[c, f, 0] = send2[c, :, f, 0]
                else:
                    recv2[c, f, :, 0] = send2[c, :, f, 0]

        for r in range(4, strips):
            inner_layers(r)
        sent = rims0 + rims + req_copies + w_copies + x_copies
        for group in (slots1, parts, spread):
            sent.extend(group.values())
        for copy in sent:
            copy.wait_send()

        def gathered(c, f):
            for d in range(1, RING):
                slots2[c, f, d].wait_recv()
            pick = onehot[:, f * half : (f + 1) * half].astype(BF16)
            return jnp.dot(
                jnp.concatenate([pick, pick], axis=1),
                jnp.concatenate(two_parts(recv2[c, f].reshape(half, wide)), axis=0),
                preferred_element_type=F32,
            )

        xa_copies = []
        for c in range(n_chunks):
            xa_send[c] = gathered(c, 1)
            copy = send(xa_send.at[c], xa_recv.at[c], x_ss.at[2 + c], x_rs.at[2 + c], partner)
            copy.start()
            xa_copies.append(copy)
        sums = [gathered(c, 0) for c in range(n_chunks)]
        for copy in xa_copies:
            copy.wait_recv()
        added = jnp.concatenate([sums[c] + xa_recv[c] for c in range(n_chunks)], axis=1)
        for rr in range(TR):
            tiles3[:, rr, :] = added[:, rr * TC : (rr + 1) * TC]
        for r in range(strips):
            strip = slice(r * TR, (r + 1) * TR)
            inner = slice(row0 + r * TR, row0 + (r + 1) * TR)
            extra = jnp.concatenate(
                [tiles3[r * tile_cols + u] for u in range(tile_cols)], axis=1
            )
            apad[top, inner, col0:col1] += extra
            outv[top - 1, strip] += RATE_VERTICAL * extra

        for side, row in ((0, first), (1, last)):
            ns2_send[side] = apad[top, row : row + 1, col0:col1]
        for side, col in ((0, col0), (1, col1 - 1)):
            ew2_send[side] = jnp.broadcast_to(
                apad[top, row0:row1, col : col + 1], (rows, LANES)
            )
        rims2 = rim_copies(ns2_send, ns2_recv, ew2_send, ew2_recv, rim2_ss, rim2_rs)
        for copy in rims2:
            copy.start()
        for r in range(strips):
            strip = slice(r * TR, (r + 1) * TR)
            inner = slice(row0 + r * TR, row0 + (r + 1) * TR)
            value, ac, total = layer_step(top, r, gacc[strip])
            under = apad[top - 1, inner, col0:col1]
            outv[top, strip] = value + RATE_VERTICAL * (under - ac)
            gradv[strip] = gin[strip] - (0.5 * RATE_PLANE) * total
        for copy in list(slots2.values()) + xa_copies:
            copy.wait_send()

        for copy in rims2:
            copy.wait_recv()
        for side, has, row, beyond in ((0, has_north, 0, first - 1), (1, has_south, rows - 1, last + 1)):
            at = slice(row, row + 1)
            rim = ns2_recv[side] * has
            slope = tpad[top, beyond : beyond + 1, col0:col1] - tpad[
                top, row0 + row : row0 + row + 1, col0:col1
            ]
            outv[top, at] += coef[2 + side, at] * rim
            gradv[at] -= (0.5 * RATE_PLANE) * slope * rim
        for side, has, face, at, beyond, edge_lane in (
            (0, has_west, 1, 0, 0, 0),
            (1, has_east, 0, cols - LANES, col1, LANES - 1),
        ):
            at = slice(at, at + LANES)
            rim = jnp.where(rim_lane == edge_lane, ew2_recv[side] * has, 0.0)
            slope = tpad[top, row0:row1, beyond : beyond + LANES] - tpad[
                top, row0:row1, col0 + at.start : col0 + at.stop
            ]
            outv[top, :, at] += coef[face, :, at] * rim
            gradv[:, at] -= (0.5 * RATE_PLANE) * slope * rim

        for copy in rims2:
            copy.wait_send()

    dma = pltpu.SemaphoreType.DMA

    def vmem(*shape, dtype=F32):
        return pltpu.VMEM(shape, dtype)

    def pair(*shape):
        return [vmem(*shape), vmem(*shape)]

    tile = TR * TC
    scratch = [
        vmem(layers, rows + 2 * TR, cols + 2 * LANES),
        vmem(layers, rows + 2 * TR, cols + 2 * LANES),
        vmem(rows + 2 * TR, cols + 2 * LANES),
        vmem(rows, cols),
        vmem(frames, tiles, tile),
        vmem(4, rows, cols),
        vmem(rows, cols),
        vmem(k_blocks, tiles, dtype=jnp.int32),
        vmem(k_blocks, tiles),
        vmem(1, tiles, dtype=jnp.int32),
        *pair(2, 2, cols),
        *pair(2, rows, LANES),
        *pair(2, 2 * layers, cols),
        *pair(2, rows, LANES),
        *pair(2, 1, cols),
        *pair(2, rows, LANES),
        vmem(2 * TR, LANES),
        vmem(groups, 8, LANES),
        vmem(PLANE, 8, LANES),
        vmem(tiles, TR, TC),
        vmem(tiles, n_slots),
        vmem(n_slots, 2 * tiles, dtype=BF16),
        vmem(2 * tiles, tile, dtype=BF16),
        *pair(2, RING, tiles, LANES),
        vmem(2, RING, 2 * tiles, 4 * tiles, dtype=BF16),
        vmem(2, RING, LANES, 4 * tiles, dtype=BF16),
        *pair(2, tiles, tile // 2),
        *pair(n_chunks, tiles, wide),
        vmem(n_chunks, 2, RING, RING, CAP, wide),
        vmem(n_chunks, RING, 2, RING, CAP, wide),
        *pair(n_chunks, RING, tiles, wide),
        vmem(n_chunks, tiles, wide),
        vmem(n_chunks, RING, tiles, wide),
        vmem(n_chunks, RING, 2, RING, CAP, wide),
        vmem(n_chunks, 2, RING, RING, CAP, wide),
        dma((9,)),
        *[dma((4,)) for _ in range(6)],
        dma((2 + n_chunks,)), dma((2 + n_chunks,)),
        dma((PLANE,)), dma((PLANE,)),
        dma((2 * RING,)), dma((2 * RING,)),
        dma((2 * n_chunks * RING,)), dma((2 * n_chunks * RING,)),
        dma((n_chunks * RING,)), dma((n_chunks * RING,)),
        dma((n_chunks * RING,)), dma((n_chunks * RING,)),
        dma((2 * n_chunks * RING,)), dma((2 * n_chunks * RING,)),
    ]
    in_hbm = pl.BlockSpec(memory_space=pltpu.HBM)
    in_vmem = pl.BlockSpec(memory_space=pltpu.VMEM)
    return pl.pallas_call(
        kernel,
        out_shape=(
            jax.ShapeDtypeStruct((tiles, tile), F32),
            jax.ShapeDtypeStruct((layers, rows, cols), F32),
            jax.ShapeDtypeStruct((rows, cols), F32),
        ),
        in_specs=[in_hbm] * 8,
        out_specs=[in_vmem] * 3,
        scratch_shapes=scratch,
        compiler_params=pltpu.CompilerParams(
            collective_id=0, has_side_effects=True, vmem_limit_bytes=48 * 1024 * 1024
        ),
    )


def write_out(results):
    count = len(results)

    def kernel(*refs):
        copies = [
            pltpu.make_async_copy(refs[i], refs[count + i], refs[-1].at[i]) for i in range(count)
        ]
        for copy in copies:
            copy.start()
        for copy in copies:
            copy.wait()

    return pl.pallas_call(
        kernel,
        out_shape=tuple(jax.ShapeDtypeStruct(x.shape, x.dtype) for x in results),
        in_specs=[pl.BlockSpec(memory_space=pltpu.VMEM)] * count,
        out_specs=[pl.BlockSpec(memory_space=pl.ANY)] * count,
        scratch_shapes=[pltpu.SemaphoreType.DMA((count,))],
        compiler_params=pltpu.CompilerParams(vmem_limit_bytes=8 * 1024 * 1024),
    )(*results)


def solution(mesh):
    n_gx, n_gy = mesh.shape["gx"], mesh.shape["gy"]

    def local(temp, cond, adj, grad, obs, frame_index, source_map, source_weight):
        layers, rows, cols = temp.shape
        call = make_kernel(n_gx, n_gy, layers, rows, cols, obs.shape[0], source_map.shape[1])
        operands = (
            temp, cond, adj, grad, obs, frame_index[None, :], source_map.T, source_weight.T
        )
        results = call(*(pltpu.with_memory_space_constraint(x, pltpu.HBM) for x in operands))
        return write_out(results)

    placed = (
        P(None, "gx", "gy"),
        P("gx", "gy"),
        P(None, "gx", "gy"),
        P("gx", "gy"),
        P(None, ("gx", "gy"), None),
        P(("gx", "gy")),
        P(("gx", "gy"), None),
        P(("gx", "gy"), None),
    )
    return jax.shard_map(
        local,
        mesh=mesh,
        in_specs=placed,
        out_specs=(P(("gx", "gy"), None), P(None, "gx", "gy"), P("gx", "gy")),
        check_vma=False,
    )
```

```python
import jax
import jax.numpy as jnp
from jax import lax
from jax.experimental import pallas as pl
from jax.experimental.pallas import tpu as pltpu
from jax.sharding import PartitionSpec as P

TR = 8
TC = 128
LANES = 128
RATE_PLANE = 0.2
RATE_VERTICAL = 0.08
MESH = pl.DeviceIdType.MESH
F32 = jnp.float32
BF16 = jnp.bfloat16


def iota(shape, dim):
    return lax.broadcasted_iota(jnp.int32, shape, dim)


def two_parts(x):
    hi = x.astype(BF16)
    lo = (x - hi.astype(F32)).astype(BF16)
    return hi, lo


RING = 4
FARTHEST_FIRST = (2, 1, 3)


def make_kernel(n_gx, n_gy, layers, rows, cols, frames, k_blocks):
    tiles = (rows // TR) * (cols // TC)
    row0, col0 = TR, LANES
    row1, col1 = row0 + rows, col0 + cols
    strips = rows // TR
    tile_cols = cols // TC
    top = layers - 1
    n_chunks = 4
    wide = cols // n_chunks
    ring = RING * tiles

    def kernel(
        temp, cond, adj, grad, obs, frame_in, map_in, weight_in,
        misfit_out, outv, gradv,
        tpad, apad, kpad, gin, obs_v, coef, gacc, map_v, weight_v, frame_v,
        ns0_send, ns0_recv, ew0_send, ew0_recv,
        ns_send, ns_recv, ew_send, ew_recv,
        ns2_send, ns2_recv, ew2_send, ew2_recv,
        small, tiles3, wfull, lhs1, lhs2,
        gat, part, part_recv, mis, con, con_recv, over_recv, xa_send, xa_recv,
        in_sem,
        rim0_ss, rim0_rs, rim_ss, rim_rs, rim2_ss, rim2_rs, x_ss, x_rs,
        w_ss, w_rs, s1_ss, s1_rs, p_ss, p_rs, m_ss, m_rs, s2_ss, s2_rs, o_ss, o_rs,
    ):
        gx = lax.axis_index("gx")
        gy = lax.axis_index("gy")
        gx_y = lax.rem(gx, RING)
        gx_x = lax.rem(gx // RING, 2)
        gx_z = gx // (2 * RING)
        north, south = lax.rem(gx + n_gx - 1, n_gx), lax.rem(gx + 1, n_gx)
        west, east = lax.rem(gy + n_gy - 1, n_gy), lax.rem(gy + 1, n_gy)
        sides = ({"gx": north}, {"gx": south}, {"gy": west}, {"gy": east})
        partner = {"gx": gx + RING - 2 * RING * gx_x}

        def along(dz, dy):
            z = lax.rem(gx_z + dz % RING, RING)
            y = lax.rem(gx_y + dy % RING, RING)
            return {"gx": z * (2 * RING) + gx_x * RING + y}

        def plate_peer(c, d):
            return along(0, d) if c % 2 == 0 else along(d, 0)

        def camera_peer(c, d):
            return along(d, 0) if c % 2 == 0 else along(0, d)

        def send(src, dst, ss, rs, device):
            return pltpu.make_async_remote_copy(
                src_ref=src,
                dst_ref=dst,
                send_sem=ss,
                recv_sem=rs,
                device_id=device,
                device_id_type=MESH,
            )

        body_at = (slice(row0, row1), slice(col0, col1))
        loads = [
            pltpu.make_async_copy(
                temp.at[top - 1 : layers],
                tpad.at[(slice(top - 1, layers), *body_at)],
                in_sem.at[0],
            ),
            pltpu.make_async_copy(cond, kpad.at[body_at], in_sem.at[1]),
            pltpu.make_async_copy(
                temp.at[0 : top - 1], tpad.at[(slice(0, top - 1), *body_at)], in_sem.at[2]
            ),
            pltpu.make_async_copy(adj, apad.at[(slice(None), *body_at)], in_sem.at[3]),
            pltpu.make_async_copy(grad, gin, in_sem.at[4]),
            pltpu.make_async_copy(obs, obs_v, in_sem.at[5]),
            pltpu.make_async_copy(map_in, map_v, in_sem.at[6]),
            pltpu.make_async_copy(weight_in, weight_v, in_sem.at[7]),
            pltpu.make_async_copy(frame_in, frame_v, in_sem.at[8]),
        ]
        for load in loads[:2]:
            load.start()

        barrier = pltpu.get_barrier_semaphore()
        greeted = [along(d, 0) for d in range(1, RING)] + [along(0, d) for d in range(1, RING)]
        greeted += [partner] + list(sides)
        for device in greeted:
            pl.semaphore_signal(barrier, inc=1, device_id=device, device_id_type=MESH)

        for load in loads[6:] + loads[2:6]:
            load.start()

        for load in loads[:2]:
            load.wait()
        first, last = row0, row1 - 1
        rim_lane = iota((rows, LANES), 1)
        for side, row in ((0, first), (1, last)):
            ns0_send[side, 0:1] = tpad[top, row : row + 1, col0:col1]
            ns0_send[side, 1:2] = kpad[row : row + 1, col0:col1]
        for side, col in ((0, col0), (1, col1 - 1)):
            ew0_send[side] = jnp.where(
                rim_lane == 0,
                tpad[top, row0:row1, col : col + 1],
                kpad[row0:row1, col : col + 1],
            )

        for load in loads[6:]:
            load.wait()
        small[0, 0:k_blocks, 0:tiles] = map_v[...].astype(F32)
        small[0, k_blocks : 2 * k_blocks, 0:tiles] = weight_v[...]
        small[2 * RING - 1, 0:1, 0:tiles] = frame_v[...].astype(F32)

        pl.semaphore_wait(barrier, len(greeted))

        def rim_copies(ns_s, ns_r, ew_s, ew_r, ss, rs):
            copies = []
            for i in range(4):
                src, dst = (ns_s, ns_r) if i < 2 else (ew_s, ew_r)
                copies.append(
                    pltpu.make_async_remote_copy(
                        src_ref=src.at[i % 2],
                        dst_ref=dst.at[1 - i % 2],
                        send_sem=ss.at[i],
                        recv_sem=rs.at[i],
                        device_id=sides[i],
                        device_id_type=MESH,
                    )
                )
            return copies

        rims0 = rim_copies(ns0_send, ns0_recv, ew0_send, ew0_recv, rim0_ss, rim0_rs)
        for copy in rims0:
            copy.start()

        w_copies = []
        for h in range(2):
            for d in range(1, RING):
                i = h * (RING - 1) + d
                copy = send(
                    small.at[0], small.at[i], w_ss.at[i], w_rs.at[i], camera_peer(h, d)
                )
                copy.start()
                w_copies.append(copy)

        has_north = jnp.where(gx > 0, 1.0, 0.0)
        has_south = jnp.where(gx < n_gx - 1, 1.0, 0.0)
        has_west = jnp.where(gy > 0, 1.0, 0.0)
        has_east = jnp.where(gy < n_gy - 1, 1.0, 0.0)

        def column_rims(pad, index, source, lane_at):
            for side, has, at in ((0, has_west, 0), (1, has_east, col1)):
                value = source[side, :, lane_at : lane_at + 1] * has
                pad[(*index, slice(row0, row1), slice(at, at + LANES))] = jnp.broadcast_to(
                    value, (rows, LANES)
                )

        for copy in rims0:
            copy.wait_recv()
        kpad[first - 1 : first, col0:col1] = ns0_recv[0, 1:2] * has_north
        kpad[last + 1 : last + 2, col0:col1] = ns0_recv[1, 1:2] * has_south
        column_rims(kpad, (), ew0_recv, 1)
        tpad[top, first - 1 : first, col0:col1] = ns0_recv[0, 0:1] * has_north
        tpad[top, last + 1 : last + 2, col0:col1] = ns0_recv[1, 0:1] * has_south
        column_rims(tpad, (top,), ew0_recv, 0)

        def around(pad, index, r):
            a, b = row0 + r * TR, row0 + (r + 1) * TR
            return (
                pad[(*index, slice(a, b), slice(col0, col1))],
                pad[(*index, slice(a, b), slice(col0 + 1, col1 + 1))],
                pad[(*index, slice(a, b), slice(col0 - 1, col1 - 1))],
                pad[(*index, slice(a - 1, b - 1), slice(col0, col1))],
                pad[(*index, slice(a + 1, b + 1), slice(col0, col1))],
            )

        for r in range(strips):
            kc, ke, kw, kn, ks = around(kpad, (), r)
            strip = slice(r * TR, (r + 1) * TR)
            faces = [0.5 * RATE_PLANE * (kc + other) for other in (ke, kw, kn, ks)]
            for i in range(4):
                coef[i, strip] = faces[i]
            tc, te, tw, tn, ts = around(tpad, (top,), r)
            under = tpad[top - 1, row0 + r * TR : row0 + (r + 1) * TR, col0:col1]
            value = tc + RATE_VERTICAL * (under - tc)
            for face, other in zip(faces, (te, tw, tn, ts)):
                value = value + face * (other - tc)
            for u in range(tile_cols):
                tiles3[r * tile_cols + u] = value[:, u * TC : (u + 1) * TC]

        x_copies, slots1 = [], {}
        for c in range(n_chunks):
            for rr in range(wide // TC):
                gat[c, 0, 0, :, rr * TC : (rr + 1) * TC] = tiles3[:, c * (wide // TC) + rr, :]
            x_copies.append(
                send(gat.at[c, 0, 0], gat.at[c, 1, 0], x_ss.at[c], x_rs.at[c], partner)
            )
            for f, d in ((0, 2), (0, 1), (0, 3), (1, 1), (1, 3)):
                i = (c * 2 + f) * RING + d
                slots1[c, f, d] = send(
                    gat.at[c, f, 0], gat.at[c, f, d], s1_ss.at[i], s1_rs.at[i], plate_peer(c, -d)
                )
            x_copies[c].start()
            for d in FARTHEST_FIRST:
                slots1[c, 0, d].start()

        over1 = [
            send(gat.at[c, 0, 2], gat.at[c, 1, 2], o_ss.at[c], o_rs.at[c], partner)
            for c in range(n_chunks)
        ]

        def pass_far(c):
            x_copies[c].wait_recv()
            for d in (1, 3):
                slots1[c, 1, d].start()
            slots1[c, 0, 2].wait_recv()
            over1[c].start()

        for load in loads[2:4]:
            load.wait()
        for side, row in ((0, first), (1, last)):
            ns_send[side, 0:top] = tpad[0:top, row, col0:col1]
            ns_send[side, layers : layers + top] = apad[0:top, row, col0:col1]
        for side, col in ((0, col0), (1, col1 - 1)):
            packed = jnp.zeros((rows, LANES), F32)
            for l in range(top):
                packed = jnp.where(rim_lane == l, tpad[l, row0:row1, col : col + 1], packed)
                packed = jnp.where(
                    rim_lane == layers + l, apad[l, row0:row1, col : col + 1], packed
                )
            ew_send[side] = packed
        rims = rim_copies(ns_send, ns_recv, ew_send, ew_recv, rim_ss, rim_rs)
        for copy in rims:
            copy.start()


        pass_far(0)
        for copy in w_copies:
            copy.wait_recv()
        turned = jnp.transpose(small[...].reshape(2 * RING * TR, LANES))[0:tiles]
        lane_tile = iota((tiles, 2 * ring), 1)

        def weigh_matrix(h):
            for d in range(RING):
                i = (h * (RING - 1) + d) * TR if d else 0
                code = turned[:, i : i + k_blocks].astype(jnp.int32)
                weight = turned[:, i + k_blocks : i + 2 * k_blocks]
                plate = code >> ((tiles * n_gy).bit_length() - 1)
                far = ((plate ^ gx) >> 2) & 1
                dz = ((plate >> 3) - gx_z) & 3
                dy = (plate - gx) & 3
                here, step = (dz, dy) if h == 0 else (dy, dz)
                at = jnp.where(here == 0, far * ring + step * tiles + (code & (tiles - 1)), -1)
                total = jnp.zeros((tiles, 2 * ring), F32)
                for k in range(k_blocks):
                    hit = at[:, k : k + 1] == lane_tile
                    total = total + jnp.where(hit, weight[:, k : k + 1], 0.0)
                wfull[h, d * tiles : (d + 1) * tiles] = total
                for i, piece in enumerate(two_parts(total)):
                    for f in range(2):
                        lhs1[h, f, i * ring + d * tiles : i * ring + (d + 1) * tiles] = piece[
                            :, f * ring : (f + 1) * ring
                        ]

        weigh_matrix(0)
        pass_far(1)
        weigh_matrix(1)
        pass_far(2)
        pass_far(3)

        def weigh(lhs, value):
            hi, lo = two_parts(value)
            both = jnp.dot(lhs[...], hi, preferred_element_type=F32)
            more = jnp.dot(lhs[0:ring], lo, preferred_element_type=F32)
            return both[0:ring] + (both[ring : 2 * ring] + more)

        for h in range(2):
            for i, piece in enumerate(two_parts(jnp.transpose(wfull[h]))):
                for f in range(2):
                    lhs2[h, f, i * ring : (i + 1) * ring] = piece[f * ring : (f + 1) * ring]

        edge = jnp.zeros((rows, LANES), F32)
        apad[top, row0:row1, 0:col0] = edge
        apad[top, row0:row1, col1 : col1 + LANES] = edge
        apad[top, first - 1 : first, col0:col1] = jnp.zeros((1, cols), F32)
        apad[top, last + 1 : last + 2, col0:col1] = jnp.zeros((1, cols), F32)

        for copy in rims:
            copy.wait_recv()
        for l in range(top):
            column_rims(tpad, (l,), ew_recv, l)
            column_rims(apad, (l,), ew_recv, layers + l)
        tpad[0:top, first - 1, col0:col1] = ns_recv[0, 0:top] * has_north
        tpad[0:top, last + 1, col0:col1] = ns_recv[1, 0:top] * has_south
        apad[0:top, first - 1, col0:col1] = ns_recv[0, layers : layers + top] * has_north
        apad[0:top, last + 1, col0:col1] = ns_recv[1, layers : layers + top] * has_south

        def layer_step(l, r, total):
            strip = slice(r * TR, (r + 1) * TR)
            tc, *t_near = around(tpad, (l,), r)
            ac, *a_near = around(apad, (l,), r)
            flow = jnp.zeros_like(ac)
            for i in range(4):
                step = a_near[i] - ac
                flow = flow + coef[i, strip] * step
                total = total + (t_near[i] - tc) * step
            return ac + flow, ac, total

        def inner_layers(r):
            strip = slice(r * TR, (r + 1) * TR)
            inner = slice(row0 + r * TR, row0 + (r + 1) * TR)

            def body(l, total):
                value, ac, total = layer_step(l, r, total)
                above = apad[l + 1, inner, col0:col1]
                under = apad[jnp.maximum(l - 1, 0), inner, col0:col1]
                outv[l, strip] = value + RATE_VERTICAL * ((above - ac) + (under - ac))
                return total

            gacc[strip] = lax.fori_loop(0, top, body, jnp.zeros((TR, cols), F32))

        for r in range(0, 2):
            inner_layers(r)

        loads[4].wait()
        loads[5].wait()
        i = (2 * RING - 1) * TR
        frame = turned[:, i : i + 1].astype(jnp.int32)

        def columns(c):
            return slice(c * wide, (c + 1) * wide)

        for c in range(n_chunks):
            seen = jnp.zeros((tiles, wide), F32)
            for f in range(frames):
                seen = jnp.where(frame == f, obs_v[f, :, columns(c)], seen)
            mis[c, 0] = -seen

        parts, spread = {}, {}
        for c in range(n_chunks):
            for d in range(1, RING):
                i = c * RING + d
                parts[c, d] = send(
                    part.at[c, d], part_recv.at[c, d], p_ss.at[i], p_rs.at[i], camera_peer(c, -d)
                )
                spread[c, d] = send(
                    mis.at[c, 0], mis.at[c, d], m_ss.at[i], m_rs.at[i], camera_peer(c, d)
                )
        for f in range(2):
            for c in range(n_chunks):
                for d in (1, 3):
                    slots1[c, f, d].wait_recv()
                if f == 1:
                    over1[c].wait_recv()
                value = weigh(lhs1.at[c % 2, f], gat[c, f].reshape(ring, wide))
                value = value.reshape(RING, tiles, wide)
                if f == 0:
                    part[c] = value
                else:
                    part[c] += value
                    for d in FARTHEST_FIRST:
                        parts[c, d].start()

        inner_layers(2)

        for c in range(n_chunks):
            for d in range(1, RING):
                parts[c, d].wait_recv()
            mis[c, 0] += (part[c, 0] + part_recv[c, 1]) + (part_recv[c, 2] + part_recv[c, 3])
            for d in FARTHEST_FIRST:
                spread[c, d].start()
            misfit_out[:, columns(c)] = mis[c, 0]

        inner_layers(3)

        back = {}
        over2 = [
            send(
                con.at[c, 1, 2],
                over_recv.at[c],
                o_ss.at[n_chunks + c],
                o_rs.at[n_chunks + c],
                partner,
            )
            for c in range(n_chunks)
        ]
        for f in (1, 0):
            for c in range(n_chunks):
                if f == 1:
                    for d in range(1, RING):
                        spread[c, d].wait_recv()
                value = weigh(lhs2.at[c % 2, f], mis[c].reshape(ring, wide))
                con[c, f] = value.reshape(RING, tiles, wide)
                for d in (1, 3, 2):
                    i = (c * 2 + f) * RING + d
                    if f == 1 and d == 2:
                        over2[c].start()
                        continue
                    if d == 2:
                        over2[c].wait_recv()
                        con[c, 0, 2] += over_recv[c]
                    back[c, f, d] = send(
                        con.at[c, f, d], con_recv.at[c, f, d], s2_ss.at[i], s2_rs.at[i], plate_peer(c, d)
                    )
                    back[c, f, d].start()

        for r in range(4, strips):
            inner_layers(r)
        sent = rims0 + rims + w_copies + x_copies + over1
        for group in (slots1, parts, spread):
            sent.extend(group.values())
        for copy in sent:
            copy.wait_send()

        def gathered(c, f):
            for d in (1, 3):
                back[c, f, d].wait_recv()
            total = con[c, f, 0] + (con_recv[c, f, 1] + con_recv[c, f, 3])
            if f == 0:
                back[c, f, 2].wait_recv()
                total = total + con_recv[c, f, 2]
            return total

        xa_copies = []
        for c in range(n_chunks):
            xa_send[c] = gathered(c, 1)
            i = n_chunks + c
            copy = send(xa_send.at[c], xa_recv.at[c], x_ss.at[i], x_rs.at[i], partner)
            copy.start()
            xa_copies.append(copy)
        for c in range(n_chunks):
            near = gathered(c, 0)
            xa_copies[c].wait_recv()
            added = near + xa_recv[c]
            for rr in range(wide // TC):
                tiles3[:, c * (wide // TC) + rr, :] = added[:, rr * TC : (rr + 1) * TC]
        for r in range(strips):
            strip = slice(r * TR, (r + 1) * TR)
            inner = slice(row0 + r * TR, row0 + (r + 1) * TR)
            extra = jnp.concatenate(
                [tiles3[r * tile_cols + u] for u in range(tile_cols)], axis=1
            )
            apad[top, inner, col0:col1] += extra
            outv[top - 1, strip] += RATE_VERTICAL * extra

        for side, row in ((0, first), (1, last)):
            ns2_send[side] = apad[top, row : row + 1, col0:col1]
        for side, col in ((0, col0), (1, col1 - 1)):
            ew2_send[side] = jnp.broadcast_to(
                apad[top, row0:row1, col : col + 1], (rows, LANES)
            )
        rims2 = rim_copies(ns2_send, ns2_recv, ew2_send, ew2_recv, rim2_ss, rim2_rs)
        for copy in rims2:
            copy.start()
        for r in range(strips):
            strip = slice(r * TR, (r + 1) * TR)
            inner = slice(row0 + r * TR, row0 + (r + 1) * TR)
            value, ac, total = layer_step(top, r, gacc[strip])
            under = apad[top - 1, inner, col0:col1]
            outv[top, strip] = value + RATE_VERTICAL * (under - ac)
            gradv[strip] = gin[strip] - (0.5 * RATE_PLANE) * total
        for copy in list(back.values()) + over2 + xa_copies:
            copy.wait_send()

        for copy in rims2:
            copy.wait_recv()
        for side, has, row, beyond in ((0, has_north, 0, first - 1), (1, has_south, rows - 1, last + 1)):
            at = slice(row, row + 1)
            rim = ns2_recv[side] * has
            slope = tpad[top, beyond : beyond + 1, col0:col1] - tpad[
                top, row0 + row : row0 + row + 1, col0:col1
            ]
            outv[top, at] += coef[2 + side, at] * rim
            gradv[at] -= (0.5 * RATE_PLANE) * slope * rim
        for side, has, face, at, beyond, edge_lane in (
            (0, has_west, 1, 0, 0, 0),
            (1, has_east, 0, cols - LANES, col1, LANES - 1),
        ):
            at = slice(at, at + LANES)
            rim = jnp.where(rim_lane == edge_lane, ew2_recv[side] * has, 0.0)
            slope = tpad[top, row0:row1, beyond : beyond + LANES] - tpad[
                top, row0:row1, col0 + at.start : col0 + at.stop
            ]
            outv[top, :, at] += coef[face, :, at] * rim
            gradv[:, at] -= (0.5 * RATE_PLANE) * slope * rim

        for copy in rims2:
            copy.wait_send()

    dma = pltpu.SemaphoreType.DMA

    def vmem(*shape, dtype=F32):
        return pltpu.VMEM(shape, dtype)

    def pair(*shape):
        return [vmem(*shape), vmem(*shape)]

    tile = TR * TC
    scratch = [
        vmem(layers, rows + 2 * TR, cols + 2 * LANES),
        vmem(layers, rows + 2 * TR, cols + 2 * LANES),
        vmem(rows + 2 * TR, cols + 2 * LANES),
        vmem(rows, cols),
        vmem(frames, tiles, tile),
        vmem(4, rows, cols),
        vmem(rows, cols),
        vmem(k_blocks, tiles, dtype=jnp.int32),
        vmem(k_blocks, tiles),
        vmem(1, tiles, dtype=jnp.int32),
        *pair(2, 2, cols),
        *pair(2, rows, LANES),
        *pair(2, 2 * layers, cols),
        *pair(2, rows, LANES),
        *pair(2, 1, cols),
        *pair(2, rows, LANES),
        vmem(2 * RING, TR, LANES),
        vmem(tiles, TR, TC),
        vmem(2, ring, 2 * ring),
        vmem(2, 2, 2 * ring, ring, dtype=BF16),
        vmem(2, 2, 2 * ring, ring, dtype=BF16),
        vmem(n_chunks, 2, RING, tiles, wide),
        *pair(n_chunks, RING, tiles, wide),
        vmem(n_chunks, RING, tiles, wide),
        *pair(n_chunks, 2, RING, tiles, wide),
        vmem(n_chunks, tiles, wide),
        *pair(n_chunks, tiles, wide),
        dma((9,)),
        *[dma((4,)) for _ in range(6)],
        dma((2 * n_chunks,)), dma((2 * n_chunks,)),
        dma((2 * RING,)), dma((2 * RING,)),
        dma((2 * n_chunks * RING,)), dma((2 * n_chunks * RING,)),
        dma((n_chunks * RING,)), dma((n_chunks * RING,)),
        dma((n_chunks * RING,)), dma((n_chunks * RING,)),
        dma((2 * n_chunks * RING,)), dma((2 * n_chunks * RING,)),
        dma((2 * n_chunks,)), dma((2 * n_chunks,)),
    ]
    in_hbm = pl.BlockSpec(memory_space=pltpu.HBM)
    in_vmem = pl.BlockSpec(memory_space=pltpu.VMEM)
    return pl.pallas_call(
        kernel,
        out_shape=(
            jax.ShapeDtypeStruct((tiles, tile), F32),
            jax.ShapeDtypeStruct((layers, rows, cols), F32),
            jax.ShapeDtypeStruct((rows, cols), F32),
        ),
        in_specs=[in_hbm] * 8,
        out_specs=[in_vmem] * 3,
        scratch_shapes=scratch,
        compiler_params=pltpu.CompilerParams(
            collective_id=0, has_side_effects=True, vmem_limit_bytes=48 * 1024 * 1024
        ),
    )


def write_out(results):
    count = len(results)

    def kernel(*refs):
        copies = [
            pltpu.make_async_copy(refs[i], refs[count + i], refs[-1].at[i]) for i in range(count)
        ]
        for copy in copies:
            copy.start()
        for copy in copies:
            copy.wait()

    return pl.pallas_call(
        kernel,
        out_shape=tuple(jax.ShapeDtypeStruct(x.shape, x.dtype) for x in results),
        in_specs=[pl.BlockSpec(memory_space=pltpu.VMEM)] * count,
        out_specs=[pl.BlockSpec(memory_space=pl.ANY)] * count,
        scratch_shapes=[pltpu.SemaphoreType.DMA((count,))],
        compiler_params=pltpu.CompilerParams(vmem_limit_bytes=8 * 1024 * 1024),
    )(*results)


def solution(mesh):
    n_gx, n_gy = mesh.shape["gx"], mesh.shape["gy"]

    def local(temp, cond, adj, grad, obs, frame_index, source_map, source_weight):
        layers, rows, cols = temp.shape
        call = make_kernel(n_gx, n_gy, layers, rows, cols, obs.shape[0], source_map.shape[1])
        operands = (
            temp, cond, adj, grad, obs, frame_index[None, :], source_map.T, source_weight.T
        )
        results = call(*(pltpu.with_memory_space_constraint(x, pltpu.HBM) for x in operands))
        return write_out(results)

    placed = (
        P(None, "gx", "gy"),
        P("gx", "gy"),
        P(None, "gx", "gy"),
        P("gx", "gy"),
        P(None, ("gx", "gy"), None),
        P(("gx", "gy")),
        P(("gx", "gy"), None),
        P(("gx", "gy"), None),
    )
    return jax.shard_map(
        local,
        mesh=mesh,
        in_specs=placed,
        out_specs=(P(("gx", "gy"), None), P(None, "gx", "gy"), P("gx", "gy")),
        check_vma=False,
    )
```

```python
import jax
import jax.numpy as jnp
from jax import lax
from jax.experimental import pallas as pl
from jax.experimental.pallas import tpu as pltpu
from jax.sharding import PartitionSpec as P

TR = 8
TC = 128
CAP = 16
LANES = 128
RATE_PLANE = 0.2
RATE_VERTICAL = 0.08
MESH = pl.DeviceIdType.MESH
F32 = jnp.float32
BF16 = jnp.bfloat16


def iota(shape, dim):
    return lax.broadcasted_iota(jnp.int32, shape, dim)


def two_parts(x):
    hi = x.astype(BF16)
    lo = (x - hi.astype(F32)).astype(BF16)
    return hi, lo


RING = 4
PLANE = RING * RING
FARTHEST_FIRST = (2, 1, 3)


def make_kernel(n_gx, n_gy, layers, rows, cols, frames, k_blocks):
    tiles = (rows // TR) * (cols // TC)
    half = PLANE * CAP
    n_slots = 2 * half
    row0, row1 = TR, TR + rows
    strips = rows // TR
    tile_cols = cols // TC
    top = layers - 1
    per_group = LANES // CAP
    groups = PLANE // per_group
    others = range(1, PLANE)
    n_chunks = 4
    wide = cols // n_chunks

    def kernel(
        temp, cond, adj, grad, obs, frame_in, map_in, weight_in,
        misfit_out, outv, gradv,
        tpad, apad, kpad, gin, obs_v, coef, gacc, map_v, weight_v, frame_v,
        ns0_send, ns0_recv, ew0_send, ew0_recv,
        ns_send, ns_recv, ew_send, ew_recv,
        ns2_send, ns2_recv, ew2_send, ew2_recv,
        small, req_send, req_recv, tiles3, onehot, lhs1, rhs,
        wsend, wblk, wcat, lhs2,
        x_send, x_recv, xa_send, xa_recv,
        send1, recv1, part, part_recv, mis, mis_recv, send2, recv2,
        in_sem,
        rim0_ss, rim0_rs, rim_ss, rim_rs, rim2_ss, rim2_rs, x_ss, x_rs,
        req_ss, req_rs, w_ss, w_rs, s1_ss, s1_rs, p_ss, p_rs, m_ss, m_rs, s2_ss, s2_rs,
    ):
        gx = lax.axis_index("gx")
        gy = lax.axis_index("gy")
        gx_y = lax.rem(gx, RING)
        gx_x = lax.rem(gx // RING, 2)
        gx_z = gx // (2 * RING)
        north, south = lax.rem(gx + n_gx - 1, n_gx), lax.rem(gx + 1, n_gx)
        west, east = lax.rem(gy + n_gy - 1, n_gy), lax.rem(gy + 1, n_gy)
        sides = ({"gx": north}, {"gx": south}, {"gy": west}, {"gy": east})
        partner = {"gx": gx + RING - 2 * RING * gx_x}

        def along(dz, dy):
            z = lax.rem(gx_z + dz % RING, RING)
            y = lax.rem(gx_y + dy % RING, RING)
            return {"gx": z * (2 * RING) + gx_x * RING + y}

        def slot_peer(h, d):
            return along(0, d) if h == 0 else along(d, 0)

        def dense_peer(h, d):
            return along(d, 0) if h == 0 else along(0, d)

        def send(src, dst, ss, rs, device):
            return pltpu.make_async_remote_copy(
                src_ref=src,
                dst_ref=dst,
                send_sem=ss,
                recv_sem=rs,
                device_id=device,
                device_id_type=MESH,
            )

        def block_loads(src, src_layers, pad, pad_layers, sem):
            return [
                pltpu.make_async_copy(
                    src.at[(*src_layers, slice(None), slice(u * TC, (u + 1) * TC))],
                    pad.at[(*pad_layers, u + 1, slice(row0, row1))],
                    in_sem.at[sem + u],
                )
                for u in range(tile_cols)
            ]

        both = (slice(top - 1, layers),)
        rest = (slice(0, top - 1),)
        all_layers = (slice(0, layers),)
        first_loads = block_loads(temp, both, tpad, both, 9) + block_loads(
            cond, (), kpad, (), 9 + tile_cols
        )
        rim_loads = block_loads(temp, rest, tpad, rest, 9 + 2 * tile_cols) + block_loads(
            adj, all_layers, apad, all_layers, 9 + 3 * tile_cols
        )
        loads = [None] * 4 + [
            pltpu.make_async_copy(grad, gin, in_sem.at[4]),
            pltpu.make_async_copy(obs, obs_v, in_sem.at[5]),
            pltpu.make_async_copy(map_in, map_v, in_sem.at[6]),
            pltpu.make_async_copy(weight_in, weight_v, in_sem.at[7]),
            pltpu.make_async_copy(frame_in, frame_v, in_sem.at[8]),
        ]
        for load in first_loads:
            load.start()

        barrier = pltpu.get_barrier_semaphore()
        greeted = [along(b % RING, b // RING) for b in others] + [partner] + list(sides)
        for device in greeted:
            pl.semaphore_signal(barrier, inc=1, device_id=device, device_id_type=MESH)

        for load in loads[6:] + rim_loads + loads[4:6]:
            load.start()

        for load in first_loads:
            load.wait()
        first, last = row0, row1 - 1

        def across(pad, index, at):
            return jnp.concatenate(
                [pad[(*index, u, at, slice(None))] for u in range(1, tile_cols + 1)], axis=-1
            )

        def put_line(pad, index, at, value):
            for u in range(tile_cols):
                pad[(*index, u + 1, at, slice(None))] = value[..., u * TC : (u + 1) * TC]

        def edge_column(pad, index, side):
            u, at = ((1, 0), (tile_cols, TC - 1))[side]
            return pad[(*index, u, slice(row0, row1), slice(at, at + 1))]

        rim_lane = iota((rows, LANES), 1)
        for side, row in ((0, first), (1, last)):
            ns0_send[side, 0:1] = across(tpad, (top,), slice(row, row + 1))
            ns0_send[side, 1:2] = across(kpad, (), slice(row, row + 1))
        for side in range(2):
            ew0_send[side] = jnp.where(
                rim_lane == 0, edge_column(tpad, (top,), side), edge_column(kpad, (), side)
            )

        pl.semaphore_wait(barrier, len(greeted))

        def rim_copies(ns_s, ns_r, ew_s, ew_r, ss, rs):
            copies = []
            for i in range(4):
                src, dst = (ns_s, ns_r) if i < 2 else (ew_s, ew_r)
                copies.append(
                    pltpu.make_async_remote_copy(
                        src_ref=src.at[i % 2],
                        dst_ref=dst.at[1 - i % 2],
                        send_sem=ss.at[i],
                        recv_sem=rs.at[i],
                        device_id=sides[i],
                        device_id_type=MESH,
                    )
                )
            return copies

        rims0 = rim_copies(ns0_send, ns0_recv, ew0_send, ew0_recv, rim0_ss, rim0_rs)
        for copy in rims0:
            copy.start()

        for load in loads[6:]:
            load.wait()
        small[0:k_blocks, 0:tiles] = map_v[...].astype(F32)
        small[k_blocks : 2 * k_blocks, 0:tiles] = weight_v[...]
        small[2 * k_blocks : 2 * k_blocks + 1, 0:tiles] = frame_v[...].astype(F32)
        columns_of = jnp.transpose(small[...])[0:tiles]
        weight = columns_of[:, k_blocks : 2 * k_blocks]
        code = columns_of[:, 0:k_blocks].astype(jnp.int32)
        plate = code >> ((tiles * n_gy).bit_length() - 1)
        far = ((plate ^ gx) >> 2) & 1
        dz = ((plate >> 3) - gx_z) & 3
        dy = (plate - gx) & 3
        block = far * PLANE + dy * RING + dz
        wish = ((code & (tiles - 1)) + 1).astype(F32)
        lane = iota((tiles, LANES), 1)
        lane_slot = iota((tiles, n_slots), 1)
        lower = jnp.where(iota((tiles, tiles), 0) > iota((tiles, tiles), 1), 1.0, 0.0)
        hits = [jnp.where(block[:, k : k + 1] == lane, 1.0, 0.0) for k in range(k_blocks)]
        before = jnp.dot(lower, jnp.concatenate(hits, axis=1), preferred_element_type=F32)
        base = jnp.zeros((1, LANES), F32)
        wanted = jnp.zeros((tiles, n_slots), F32)
        weights = [jnp.zeros((tiles, n_slots), F32) for _ in range(2)]
        for k in range(k_blocks):
            earlier = before[:, k * LANES : (k + 1) * LANES] + base
            base = base + jnp.sum(hits[k], axis=0, keepdims=True)
            rank = jnp.sum(hits[k] * earlier, axis=1, keepdims=True).astype(jnp.int32)
            col = slice(k, k + 1)
            here = block[:, col] * CAP + rank == lane_slot
            wanted = wanted + jnp.where(here, wish[:, col], 0.0)
            for h, (dense, slot) in enumerate(((dz, dy), (dy, dz))):
                at = (dense * LANES + far * (LANES // 2) + slot * CAP)[:, col] + rank
                weights[h] = weights[h] + jnp.where(at == lane_slot, weight[:, col], 0.0)
        for h in range(2):
            for d in range(RING):
                wsend[h, d] = weights[h][:, d * LANES : (d + 1) * LANES]
            wblk[h, 0] = weights[h][:, 0:LANES]
        asked = jnp.sum(wanted, axis=0, keepdims=True)
        for g in range(groups):
            for f in range(2):
                at = f * half + g * LANES
                req_send[g, f : f + 1] = asked[:, at : at + LANES]

        req_copies = []
        for b in others:
            copy = send(
                req_send.at[b // per_group],
                req_recv.at[b],
                req_ss.at[b],
                req_rs.at[b],
                along(b % RING, b // RING),
            )
            copy.start()
            req_copies.append(copy)
        w_copies = []
        for h in range(2):
            for d in range(1, RING):
                i = h * RING + d
                copy = send(
                    wsend.at[h, d], wblk.at[h, d], w_ss.at[i], w_rs.at[i], dense_peer(h, d)
                )
                copy.start()
                w_copies.append(copy)
        req_recv[0] = req_send[0]

        has_north = jnp.where(gx > 0, 1.0, 0.0)
        has_south = jnp.where(gx < n_gx - 1, 1.0, 0.0)
        has_west = jnp.where(gy > 0, 1.0, 0.0)
        has_east = jnp.where(gy < n_gy - 1, 1.0, 0.0)

        def column_rims(pad, index, source, lane_at):
            for side, has, at in ((0, has_west, 0), (1, has_east, tile_cols + 1)):
                value = source[side, :, lane_at : lane_at + 1] * has
                pad[(*index, at, slice(row0, row1))] = jnp.broadcast_to(value, (rows, LANES))

        for copy in rims0:
            copy.wait_recv()
        above, below = slice(first - 1, first), slice(last + 1, last + 2)
        put_line(kpad, (), above, ns0_recv[0, 1:2] * has_north)
        put_line(kpad, (), below, ns0_recv[1, 1:2] * has_south)
        column_rims(kpad, (), ew0_recv, 1)
        put_line(tpad, (top,), above, ns0_recv[0, 0:1] * has_north)
        put_line(tpad, (top,), below, ns0_recv[1, 0:1] * has_south)
        column_rims(tpad, (top,), ew0_recv, 0)

        strip_lane = iota((TR, TC), 1)

        def around(pad, index, r):
            a, b = row0 + r * TR, row0 + (r + 1) * TR
            blocks = [pad[(*index, u, slice(a, b), slice(None))] for u in range(tile_cols + 2)]
            inside = blocks[1:-1]
            eastward = [pltpu.roll(x, TC - 1, 1) for x in inside] + blocks[-1:]
            westward = blocks[:1] + [pltpu.roll(x, 1, 1) for x in inside]
            e = [
                jnp.where(strip_lane == TC - 1, eastward[u + 1], eastward[u])
                for u in range(tile_cols)
            ]
            w = [
                jnp.where(strip_lane == 0, westward[u], westward[u + 1]) for u in range(tile_cols)
            ]
            return (
                jnp.concatenate(inside, axis=1),
                jnp.concatenate(e, axis=1),
                jnp.concatenate(w, axis=1),
                across(pad, index, slice(a - 1, b - 1)),
                across(pad, index, slice(a + 1, b + 1)),
            )

        for r in range(strips):
            kc, ke, kw, kn, ks = around(kpad, (), r)
            strip = slice(r * TR, (r + 1) * TR)
            faces = [0.5 * RATE_PLANE * (kc + other) for other in (ke, kw, kn, ks)]
            for i in range(4):
                coef[i, strip] = faces[i]
            tc, te, tw, tn, ts = around(tpad, (top,), r)
            under = across(tpad, (top - 1,), slice(row0 + r * TR, row0 + (r + 1) * TR))
            value = tc + RATE_VERTICAL * (under - tc)
            for face, other in zip(faces, (te, tw, tn, ts)):
                value = value + face * (other - tc)
            for u in range(tile_cols):
                tiles3[r * tile_cols + u] = value[:, u * TC : (u + 1) * TC]

        x_copies = []
        for i in range(2):
            for rr in range(TR // 2):
                x_send[i, :, rr * TC : (rr + 1) * TC] = tiles3[:, i * (TR // 2) + rr, :]
            copy = send(x_send.at[i], x_recv.at[i], x_ss.at[i], x_rs.at[i], partner)
            copy.start()
            x_copies.append(copy)

        for copy in req_copies:
            copy.wait_recv()
        group_lane = iota((per_group, LANES), 1) // CAP
        group_row = iota((per_group, LANES), 0)
        tile_row = iota((tiles, LANES), 0).astype(F32)
        for f in range(2):
            picks = []
            for g in range(groups):
                block = req_recv[g * per_group : (g + 1) * per_group, f, :]
                line = jnp.sum(
                    jnp.where(group_lane == group_row, block, 0.0), axis=0, keepdims=True
                )
                picks.append(jnp.where(line - 1.0 == tile_row, 1.0, 0.0))
            pick = jnp.concatenate(picks, axis=1)
            onehot[:, f * half : (f + 1) * half] = pick
            turned = jnp.transpose(jnp.concatenate([pick, pick], axis=0)).astype(BF16)
            lhs1[f * half : (f + 1) * half] = turned

        def plane_rows(ref, c, f, d):
            return ref.at[c, f, d] if c % 2 == 0 else ref.at[c, f, :, d]

        slots1 = {}
        for c in range(n_chunks):
            for f in range(2):
                for d in range(1, RING):
                    i = (c * 2 + f) * RING + d
                    slots1[c, f, d] = send(
                        plane_rows(send1, c, f, d),
                        recv1.at[c, :, f, d],
                        s1_ss.at[i],
                        s1_rs.at[i],
                        slot_peer(c % 2, -d),
                    )

        def columns(c, count=1):
            return slice(c * wide, (c + count) * wide)

        def pack_tiles(f, pair, source):
            for i, piece in enumerate(two_parts(source)):
                rhs[i * tiles : (i + 1) * tiles, columns(pair, 2)] = piece
            for c in (pair, pair + 1):
                packed = jnp.dot(
                    lhs1[f * half : (f + 1) * half],
                    rhs[:, columns(c)],
                    preferred_element_type=F32,
                )
                send1[c, f] = packed.reshape(RING, RING, CAP, wide)
                for d in FARTHEST_FIRST:
                    slots1[c, f, d].start()
                recv1[c, :, f, 0] = send1[c, f, 0] if c % 2 == 0 else send1[c, f, :, 0]

        for pair in (0, 2):
            pack_tiles(0, pair, x_send[pair // 2])

        for load in rim_loads:
            load.wait()
        for side, row in ((0, first), (1, last)):
            for u in range(tile_cols):
                at = slice(u * TC, (u + 1) * TC)
                ns_send[side, 0:top, at] = tpad[0:top, u + 1, row, :]
                ns_send[side, layers : layers + top, at] = apad[0:top, u + 1, row, :]
        for side in range(2):
            packed = jnp.zeros((rows, LANES), F32)
            for l in range(top):
                packed = jnp.where(rim_lane == l, edge_column(tpad, (l,), side), packed)
                packed = jnp.where(
                    rim_lane == layers + l, edge_column(apad, (l,), side), packed
                )
            ew_send[side] = packed
        rims = rim_copies(ns_send, ns_recv, ew_send, ew_recv, rim_ss, rim_rs)
        for copy in rims:
            copy.start()

        for copy in w_copies:
            copy.wait_recv()
        for h in range(2):
            for d in range(RING):
                for i, piece in enumerate(two_parts(wblk[h, d])):
                    wcat[h, d, i * tiles : (i + 1) * tiles] = jnp.concatenate(
                        [piece, piece], axis=1
                    )

        for pair in (0, 2):
            x_copies[pair // 2].wait_recv()
            pack_tiles(1, pair, x_recv[pair // 2])

        for h in range(2):
            for d in range(RING):
                parts_of = jnp.concatenate(two_parts(wblk[h, d]), axis=0).astype(F32)
                turned = jnp.transpose(parts_of).astype(BF16)
                lhs2[h, d, :, 0 : 2 * tiles] = turned
                lhs2[h, d, :, 2 * tiles : 4 * tiles] = turned

        edge = jnp.zeros((rows, LANES), F32)
        apad[top, 0, row0:row1] = edge
        apad[top, tile_cols + 1, row0:row1] = edge
        put_line(apad, (top,), above, jnp.zeros((1, cols), F32))
        put_line(apad, (top,), below, jnp.zeros((1, cols), F32))

        for copy in rims:
            copy.wait_recv()
        for l in range(top):
            column_rims(tpad, (l,), ew_recv, l)
            column_rims(apad, (l,), ew_recv, layers + l)
        for side, has, at in ((0, has_north, first - 1), (1, has_south, last + 1)):
            for u in range(tile_cols):
                cut = slice(u * TC, (u + 1) * TC)
                tpad[0:top, u + 1, at, :] = ns_recv[side, 0:top, cut] * has
                apad[0:top, u + 1, at, :] = ns_recv[side, layers : layers + top, cut] * has

        def layer_step(l, r, total):
            strip = slice(r * TR, (r + 1) * TR)
            tc, *t_near = around(tpad, (l,), r)
            ac, *a_near = around(apad, (l,), r)
            flow = jnp.zeros_like(ac)
            for i in range(4):
                step = a_near[i] - ac
                flow = flow + coef[i, strip] * step
                total = total + (t_near[i] - tc) * step
            return ac + flow, ac, total

        def inner_layers(r):
            strip = slice(r * TR, (r + 1) * TR)
            inner = slice(row0 + r * TR, row0 + (r + 1) * TR)

            def body(l, total):
                value, ac, total = layer_step(l, r, total)
                over = across(apad, (l + 1,), inner)
                under = across(apad, (jnp.maximum(l - 1, 0),), inner)
                outv[l, strip] = value + RATE_VERTICAL * ((over - ac) + (under - ac))
                return total

            gacc[strip] = lax.fori_loop(0, top, body, jnp.zeros((TR, cols), F32))

        for r in range(0, 2):
            inner_layers(r)

        loads[4].wait()
        loads[5].wait()
        frame = columns_of[:, 2 * k_blocks : 2 * k_blocks + 1].astype(jnp.int32)
        for c in range(n_chunks):
            seen = jnp.zeros((tiles, wide), F32)
            for f in range(frames):
                seen = jnp.where(frame == f, obs_v[f, :, columns(c)], seen)
            mis[c] = -seen

        def weigh(c, d):
            both = jnp.dot(
                wcat[c % 2, d],
                jnp.concatenate(two_parts(recv1[c, d].reshape(LANES, wide)), axis=0),
                preferred_element_type=F32,
            )
            return both[0:tiles] + both[tiles : 2 * tiles]

        parts, spread = {}, {}
        for c in range(n_chunks):
            for d in range(1, RING):
                i = c * RING + d
                parts[c, d] = send(
                    part.at[c, d],
                    part_recv.at[c, d],
                    p_ss.at[i],
                    p_rs.at[i],
                    dense_peer(c % 2, -d),
                )
                spread[c, d] = send(
                    mis.at[c], mis_recv.at[c, d], m_ss.at[i], m_rs.at[i], dense_peer(c % 2, d)
                )
        for c in range(n_chunks):
            for f in range(2):
                for d in range(1, RING):
                    slots1[c, f, d].wait_recv()
            for d in FARTHEST_FIRST:
                part[c, d] = weigh(c, d)
                parts[c, d].start()
            mis[c] += weigh(c, 0)

        inner_layers(2)

        for c in range(n_chunks):
            for d in range(1, RING):
                parts[c, d].wait_recv()
            mis[c] += part_recv[c, 1] + (part_recv[c, 2] + part_recv[c, 3])
            for d in FARTHEST_FIRST:
                spread[c, d].start()
            misfit_out[:, columns(c)] = mis[c]

        inner_layers(3)

        slots2 = {}
        for c in range(n_chunks):
            for f in range(2):
                for d in range(1, RING):
                    i = (c * 2 + f) * RING + d
                    slots2[c, f, d] = send(
                        send2.at[c, :, f, d],
                        plane_rows(recv2, c, f, d),
                        s2_ss.at[i],
                        s2_rs.at[i],
                        slot_peer(c % 2, d),
                    )
        for c in range(n_chunks):
            for d in range(RING):
                if d:
                    spread[c, d].wait_recv()
                mh, ml = two_parts(mis_recv[c, d] if d else mis[c])
                packed = jnp.dot(
                    lhs2[c % 2, d],
                    jnp.concatenate([mh, mh, ml, ml], axis=0),
                    preferred_element_type=F32,
                )
                send2[c, d] = packed.reshape(2, RING, CAP, wide)
            for d in FARTHEST_FIRST:
                slots2[c, 1, d].start()
        for c in range(n_chunks):
            for d in FARTHEST_FIRST:
                slots2[c, 0, d].start()
        for c in range(n_chunks):
            for f in range(2):
                if c % 2 == 0:
                    recv2[c, f, 0] = send2[c, :, f, 0]
                else:
                    recv2[c, f, :, 0] = send2[c, :, f, 0]

        for r in range(4, strips):
            inner_layers(r)
        sent = rims0 + rims + req_copies + w_copies + x_copies
        for group in (slots1, parts, spread):
            sent.extend(group.values())
        for copy in sent:
            copy.wait_send()

        def gathered(c, f):
            for d in range(1, RING):
                slots2[c, f, d].wait_recv()
            pick = onehot[:, f * half : (f + 1) * half].astype(BF16)
            return jnp.dot(
                jnp.concatenate([pick, pick], axis=1),
                jnp.concatenate(two_parts(recv2[c, f].reshape(half, wide)), axis=0),
                preferred_element_type=F32,
            )

        xa_copies = []
        for c in range(n_chunks):
            xa_send[c] = gathered(c, 1)
            copy = send(xa_send.at[c], xa_recv.at[c], x_ss.at[2 + c], x_rs.at[2 + c], partner)
            copy.start()
            xa_copies.append(copy)
        sums = [gathered(c, 0) for c in range(n_chunks)]
        for copy in xa_copies:
            copy.wait_recv()
        added = jnp.concatenate([sums[c] + xa_recv[c] for c in range(n_chunks)], axis=1)
        for rr in range(TR):
            tiles3[:, rr, :] = added[:, rr * TC : (rr + 1) * TC]
        for r in range(strips):
            strip = slice(r * TR, (r + 1) * TR)
            inner = slice(row0 + r * TR, row0 + (r + 1) * TR)
            extra = jnp.concatenate(
                [tiles3[r * tile_cols + u] for u in range(tile_cols)], axis=1
            )
            put_line(apad, (top,), inner, across(apad, (top,), inner) + extra)
            outv[top - 1, strip] += RATE_VERTICAL * extra

        for side, row in ((0, first), (1, last)):
            ns2_send[side] = across(apad, (top,), slice(row, row + 1))
        for side in range(2):
            ew2_send[side] = jnp.broadcast_to(edge_column(apad, (top,), side), (rows, LANES))
        rims2 = rim_copies(ns2_send, ns2_recv, ew2_send, ew2_recv, rim2_ss, rim2_rs)
        for copy in rims2:
            copy.start()
        for r in range(strips):
            strip = slice(r * TR, (r + 1) * TR)
            inner = slice(row0 + r * TR, row0 + (r + 1) * TR)
            value, ac, total = layer_step(top, r, gacc[strip])
            under = across(apad, (top - 1,), inner)
            outv[top, strip] = value + RATE_VERTICAL * (under - ac)
            gradv[strip] = gin[strip] - (0.5 * RATE_PLANE) * total
        for copy in list(slots2.values()) + xa_copies:
            copy.wait_send()

        for copy in rims2:
            copy.wait_recv()
        for side, has, row, beyond in ((0, has_north, 0, first - 1), (1, has_south, rows - 1, last + 1)):
            at = slice(row, row + 1)
            rim = ns2_recv[side] * has
            slope = across(tpad, (top,), slice(beyond, beyond + 1)) - across(
                tpad, (top,), slice(row0 + row, row0 + row + 1)
            )
            outv[top, at] += coef[2 + side, at] * rim
            gradv[at] -= (0.5 * RATE_PLANE) * slope * rim
        for side, has, face, inside, beyond, edge_lane in (
            (0, has_west, 1, 1, 0, 0),
            (1, has_east, 0, tile_cols, tile_cols + 1, TC - 1),
        ):
            at = slice((inside - 1) * TC, inside * TC)
            rim = jnp.where(rim_lane == edge_lane, ew2_recv[side] * has, 0.0)
            slope = tpad[top, beyond, row0:row1] - tpad[top, inside, row0:row1]
            outv[top, :, at] += coef[face, :, at] * rim
            gradv[:, at] -= (0.5 * RATE_PLANE) * slope * rim

        for copy in rims2:
            copy.wait_send()

    dma = pltpu.SemaphoreType.DMA

    def vmem(*shape, dtype=F32):
        return pltpu.VMEM(shape, dtype)

    def pair(*shape):
        return [vmem(*shape), vmem(*shape)]

    tile = TR * TC
    scratch = [
        vmem(layers, tile_cols + 2, rows + 2 * TR, TC),
        vmem(layers, tile_cols + 2, rows + 2 * TR, TC),
        vmem(tile_cols + 2, rows + 2 * TR, TC),
        vmem(rows, cols),
        vmem(frames, tiles, tile),
        vmem(4, rows, cols),
        vmem(rows, cols),
        vmem(k_blocks, tiles, dtype=jnp.int32),
        vmem(k_blocks, tiles),
        vmem(1, tiles, dtype=jnp.int32),
        *pair(2, 2, cols),
        *pair(2, rows, LANES),
        *pair(2, 2 * layers, cols),
        *pair(2, rows, LANES),
        *pair(2, 1, cols),
        *pair(2, rows, LANES),
        vmem(2 * TR, LANES),
        vmem(groups, 8, LANES),
        vmem(PLANE, 8, LANES),
        vmem(tiles, TR, TC),
        vmem(tiles, n_slots),
        vmem(n_slots, 2 * tiles, dtype=BF16),
        vmem(2 * tiles, tile, dtype=BF16),
        *pair(2, RING, tiles, LANES),
        vmem(2, RING, 2 * tiles, 4 * tiles, dtype=BF16),
        vmem(2, RING, LANES, 4 * tiles, dtype=BF16),
        *pair(2, tiles, tile // 2),
        *pair(n_chunks, tiles, wide),
        vmem(n_chunks, 2, RING, RING, CAP, wide),
        vmem(n_chunks, RING, 2, RING, CAP, wide),
        *pair(n_chunks, RING, tiles, wide),
        vmem(n_chunks, tiles, wide),
        vmem(n_chunks, RING, tiles, wide),
        vmem(n_chunks, RING, 2, RING, CAP, wide),
        vmem(n_chunks, 2, RING, RING, CAP, wide),
        dma((9 + 4 * tile_cols,)),
        *[dma((4,)) for _ in range(6)],
        dma((2 + n_chunks,)), dma((2 + n_chunks,)),
        dma((PLANE,)), dma((PLANE,)),
        dma((2 * RING,)), dma((2 * RING,)),
        dma((2 * n_chunks * RING,)), dma((2 * n_chunks * RING,)),
        dma((n_chunks * RING,)), dma((n_chunks * RING,)),
        dma((n_chunks * RING,)), dma((n_chunks * RING,)),
        dma((2 * n_chunks * RING,)), dma((2 * n_chunks * RING,)),
    ]
    in_hbm = pl.BlockSpec(memory_space=pltpu.HBM)
    in_vmem = pl.BlockSpec(memory_space=pltpu.VMEM)
    return pl.pallas_call(
        kernel,
        out_shape=(
            jax.ShapeDtypeStruct((tiles, tile), F32),
            jax.ShapeDtypeStruct((layers, rows, cols), F32),
            jax.ShapeDtypeStruct((rows, cols), F32),
        ),
        in_specs=[in_hbm] * 8,
        out_specs=[in_vmem] * 3,
        scratch_shapes=scratch,
        compiler_params=pltpu.CompilerParams(
            collective_id=0, has_side_effects=True, vmem_limit_bytes=48 * 1024 * 1024
        ),
    )


def write_out(results):
    count = len(results)

    def kernel(*refs):
        copies = [
            pltpu.make_async_copy(refs[i], refs[count + i], refs[-1].at[i]) for i in range(count)
        ]
        for copy in copies:
            copy.start()
        for copy in copies:
            copy.wait()

    return pl.pallas_call(
        kernel,
        out_shape=tuple(jax.ShapeDtypeStruct(x.shape, x.dtype) for x in results),
        in_specs=[pl.BlockSpec(memory_space=pltpu.VMEM)] * count,
        out_specs=[pl.BlockSpec(memory_space=pl.ANY)] * count,
        scratch_shapes=[pltpu.SemaphoreType.DMA((count,))],
        compiler_params=pltpu.CompilerParams(vmem_limit_bytes=8 * 1024 * 1024),
    )(*results)


def solution(mesh):
    n_gx, n_gy = mesh.shape["gx"], mesh.shape["gy"]

    def local(temp, cond, adj, grad, obs, frame_index, source_map, source_weight):
        layers, rows, cols = temp.shape
        call = make_kernel(n_gx, n_gy, layers, rows, cols, obs.shape[0], source_map.shape[1])
        operands = (
            temp, cond, adj, grad, obs, frame_index[None, :], source_map.T, source_weight.T
        )
        results = call(*(pltpu.with_memory_space_constraint(x, pltpu.HBM) for x in operands))
        return write_out(results)

    placed = (
        P(None, "gx", "gy"),
        P("gx", "gy"),
        P(None, "gx", "gy"),
        P("gx", "gy"),
        P(None, ("gx", "gy"), None),
        P(("gx", "gy")),
        P(("gx", "gy"), None),
        P(("gx", "gy"), None),
    )
    return jax.shard_map(
        local,
        mesh=mesh,
        in_specs=placed,
        out_specs=(P(("gx", "gy"), None), P(None, "gx", "gy"), P("gx", "gy")),
        check_vma=False,
    )
```

```python
import jax
import jax.numpy as jnp
from jax import lax
from jax.experimental import pallas as pl
from jax.experimental.pallas import tpu as pltpu
from jax.sharding import PartitionSpec as P

TR = 8
TC = 128
CAP = 16
LANES = 128
RATE_PLANE = 0.2
RATE_VERTICAL = 0.08
MESH = pl.DeviceIdType.MESH
F32 = jnp.float32
BF16 = jnp.bfloat16


def iota(shape, dim):
    return lax.broadcasted_iota(jnp.int32, shape, dim)


def two_parts(x):
    hi = x.astype(BF16)
    lo = (x - hi.astype(F32)).astype(BF16)
    return hi, lo


RING = 4
PLANE = RING * RING
FARTHEST_FIRST = (2, 1, 3)


def make_kernel(n_gx, n_gy, layers, rows, cols, frames, k_blocks):
    tiles = (rows // TR) * (cols // TC)
    half = PLANE * CAP
    n_slots = 2 * half
    row0, row1 = TR, TR + rows
    strips = rows // TR
    tile_cols = cols // TC
    top = layers - 1
    per_group = LANES // CAP
    groups = PLANE // per_group
    others = range(1, PLANE)
    n_chunks = 4
    wide = cols // n_chunks

    def kernel(
        temp, cond, adj, grad, obs, frame_in, map_in, weight_in,
        misfit_out, outv, gradv,
        tpad, apad, kpad, gin, obs_v, coef, gacc, map_v, weight_v, frame_v,
        ns0_send, ns0_recv, ew0_send, ew0_recv,
        ns_send, ns_recv, ew_send, ew_recv,
        ns2_send, ns2_recv, ew2_send, ew2_recv,
        small, req_send, req_recv, tiles3, onehot, lhs1, rhs,
        wsend, wblk, wcat, lhs2,
        x_send, x_recv, xa_send, xa_recv,
        send1, recv1, part, part_recv, mis, mis_recv, send2, recv2,
        in_sem,
        rim0_ss, rim0_rs, rim_ss, rim_rs, rim2_ss, rim2_rs, x_ss, x_rs,
        req_ss, req_rs, w_ss, w_rs, s1_ss, s1_rs, p_ss, p_rs, m_ss, m_rs, s2_ss, s2_rs,
    ):
        gx = lax.axis_index("gx")
        gy = lax.axis_index("gy")
        gx_y = lax.rem(gx, RING)
        gx_x = lax.rem(gx // RING, 2)
        gx_z = gx // (2 * RING)
        north, south = lax.rem(gx + n_gx - 1, n_gx), lax.rem(gx + 1, n_gx)
        west, east = lax.rem(gy + n_gy - 1, n_gy), lax.rem(gy + 1, n_gy)
        sides = ({"gx": north}, {"gx": south}, {"gy": west}, {"gy": east})
        partner = {"gx": gx + RING - 2 * RING * gx_x}

        def along(dz, dy):
            z = lax.rem(gx_z + dz % RING, RING)
            y = lax.rem(gx_y + dy % RING, RING)
            return {"gx": z * (2 * RING) + gx_x * RING + y}

        def slot_peer(h, d):
            return along(0, d) if h == 0 else along(d, 0)

        def dense_peer(h, d):
            return along(d, 0) if h == 0 else along(0, d)

        def wait_bytes(like, sem):
            pltpu.make_async_copy(like, like, sem).wait()

        def send(src, dst, ss, rs, device):
            return pltpu.make_async_remote_copy(
                src_ref=src,
                dst_ref=dst,
                send_sem=ss,
                recv_sem=rs,
                device_id=device,
                device_id_type=MESH,
            )

        def block_loads(src, src_layers, pad, pad_layers, sem):
            return [
                pltpu.make_async_copy(
                    src.at[(*src_layers, slice(None), slice(u * TC, (u + 1) * TC))],
                    pad.at[(*pad_layers, u + 1, slice(row0, row1))],
                    in_sem.at[sem + u],
                )
                for u in range(tile_cols)
            ]

        both = (slice(top - 1, layers),)
        rest = (slice(0, top - 1),)
        all_layers = (slice(0, layers),)
        first_loads = block_loads(temp, both, tpad, both, 9) + block_loads(
            cond, (), kpad, (), 9 + tile_cols
        )
        rim_loads = block_loads(temp, rest, tpad, rest, 9 + 2 * tile_cols) + block_loads(
            adj, all_layers, apad, all_layers, 9 + 3 * tile_cols
        )
        loads = [None] * 4 + [
            pltpu.make_async_copy(grad, gin, in_sem.at[4]),
            pltpu.make_async_copy(obs, obs_v, in_sem.at[5]),
            pltpu.make_async_copy(map_in, map_v, in_sem.at[6]),
            pltpu.make_async_copy(weight_in, weight_v, in_sem.at[7]),
            pltpu.make_async_copy(frame_in, frame_v, in_sem.at[8]),
        ]
        for load in first_loads:
            load.start()

        barrier = pltpu.get_barrier_semaphore()
        greeted = [along(b % RING, b // RING) for b in others] + [partner] + list(sides)
        for device in greeted:
            pl.semaphore_signal(barrier, inc=1, device_id=device, device_id_type=MESH)

        for load in loads[6:] + rim_loads + loads[4:6]:
            load.start()

        for load in first_loads:
            load.wait()
        first, last = row0, row1 - 1

        def across(pad, index, at):
            return jnp.concatenate(
                [pad[(*index, u, at, slice(None))] for u in range(1, tile_cols + 1)], axis=-1
            )

        def put_line(pad, index, at, value):
            for u in range(tile_cols):
                pad[(*index, u + 1, at, slice(None))] = value[..., u * TC : (u + 1) * TC]

        def edge_column(pad, index, side):
            u, at = ((1, 0), (tile_cols, TC - 1))[side]
            return pad[(*index, u, slice(row0, row1), slice(at, at + 1))]

        rim_lane = iota((rows, LANES), 1)
        for side, row in ((0, first), (1, last)):
            ns0_send[side, 0:1] = across(tpad, (top,), slice(row, row + 1))
            ns0_send[side, 1:2] = across(kpad, (), slice(row, row + 1))
        for side in range(2):
            ew0_send[side] = jnp.where(
                rim_lane == 0, edge_column(tpad, (top,), side), edge_column(kpad, (), side)
            )

        pl.semaphore_wait(barrier, len(greeted))

        def rim_copies(ns_s, ns_r, ew_s, ew_r, ss, rs):
            copies = []
            for i in range(4):
                src, dst = (ns_s, ns_r) if i < 2 else (ew_s, ew_r)
                copies.append(
                    pltpu.make_async_remote_copy(
                        src_ref=src.at[i % 2],
                        dst_ref=dst.at[1 - i % 2],
                        send_sem=ss.at[i // 2],
                        recv_sem=rs.at[i // 2],
                        device_id=sides[i],
                        device_id_type=MESH,
                    )
                )
            return copies

        rims0 = rim_copies(ns0_send, ns0_recv, ew0_send, ew0_recv, rim0_ss, rim0_rs)
        for copy in rims0:
            copy.start()

        for load in loads[6:]:
            load.wait()
        small[0:k_blocks, 0:tiles] = map_v[...].astype(F32)
        small[k_blocks : 2 * k_blocks, 0:tiles] = weight_v[...]
        small[2 * k_blocks : 2 * k_blocks + 1, 0:tiles] = frame_v[...].astype(F32)
        columns_of = jnp.transpose(small[...])[0:tiles]
        weight = columns_of[:, k_blocks : 2 * k_blocks]
        code = columns_of[:, 0:k_blocks].astype(jnp.int32)
        plate = code >> ((tiles * n_gy).bit_length() - 1)
        far = ((plate ^ gx) >> 2) & 1
        dz = ((plate >> 3) - gx_z) & 3
        dy = (plate - gx) & 3
        block = far * PLANE + dy * RING + dz
        wish = ((code & (tiles - 1)) + 1).astype(F32)
        lane = iota((tiles, LANES), 1)
        lane_slot = iota((tiles, n_slots), 1)
        lower = jnp.where(iota((tiles, tiles), 0) > iota((tiles, tiles), 1), 1.0, 0.0)
        hits = [jnp.where(block[:, k : k + 1] == lane, 1.0, 0.0) for k in range(k_blocks)]
        before = jnp.dot(lower, jnp.concatenate(hits, axis=1), preferred_element_type=F32)
        base = jnp.zeros((1, LANES), F32)
        wanted = jnp.zeros((tiles, n_slots), F32)
        weights = [jnp.zeros((tiles, n_slots), F32) for _ in range(2)]
        ranks = []
        for k in range(k_blocks):
            earlier = before[:, k * LANES : (k + 1) * LANES] + base
            base = base + jnp.sum(hits[k], axis=0, keepdims=True)
            ranks.append(jnp.sum(hits[k] * earlier, axis=1, keepdims=True).astype(jnp.int32))
            here = block[:, k : k + 1] * CAP + ranks[k] == lane_slot
            wanted = wanted + jnp.where(here, wish[:, k : k + 1], 0.0)
        asked = jnp.sum(wanted, axis=0, keepdims=True)
        for g in range(groups):
            for f in range(2):
                at = f * half + g * LANES
                req_send[g, f : f + 1] = asked[:, at : at + LANES]

        for b in others:
            send(
                req_send.at[b // per_group],
                req_recv.at[b],
                req_ss.at[0],
                req_rs.at[0],
                along(b % RING, b // RING),
            ).start()
        for k in range(k_blocks):
            col = slice(k, k + 1)
            for h, (dense, slot) in enumerate(((dz, dy), (dy, dz))):
                at = (dense * LANES + far * (LANES // 2) + slot * CAP)[:, col] + ranks[k]
                weights[h] = weights[h] + jnp.where(at == lane_slot, weight[:, col], 0.0)
        for h in range(2):
            for d in range(RING):
                wsend[h, d] = weights[h][:, d * LANES : (d + 1) * LANES]
            wblk[h, 0] = weights[h][:, 0:LANES]
            for d in range(1, RING):
                send(
                    wsend.at[h, d], wblk.at[h, d], w_ss.at[0], w_rs.at[0], dense_peer(h, d)
                ).start()
        req_recv[0] = req_send[0]

        has_north = jnp.where(gx > 0, 1.0, 0.0)
        has_south = jnp.where(gx < n_gx - 1, 1.0, 0.0)
        has_west = jnp.where(gy > 0, 1.0, 0.0)
        has_east = jnp.where(gy < n_gy - 1, 1.0, 0.0)

        def column_rims(pad, index, source, lane_at):
            for side, has, at in ((0, has_west, 0), (1, has_east, tile_cols + 1)):
                value = source[side, :, lane_at : lane_at + 1] * has
                pad[(*index, at, slice(row0, row1))] = jnp.broadcast_to(value, (rows, LANES))

        wait_bytes(ns0_recv, rim0_rs.at[0])
        wait_bytes(ew0_recv, rim0_rs.at[1])
        above, below = slice(first - 1, first), slice(last + 1, last + 2)
        put_line(kpad, (), above, ns0_recv[0, 1:2] * has_north)
        put_line(kpad, (), below, ns0_recv[1, 1:2] * has_south)
        column_rims(kpad, (), ew0_recv, 1)
        put_line(tpad, (top,), above, ns0_recv[0, 0:1] * has_north)
        put_line(tpad, (top,), below, ns0_recv[1, 0:1] * has_south)
        column_rims(tpad, (top,), ew0_recv, 0)

        strip_lane = iota((TR, TC), 1)

        def around(pad, index, r):
            a, b = row0 + r * TR, row0 + (r + 1) * TR
            blocks = [pad[(*index, u, slice(a, b), slice(None))] for u in range(tile_cols + 2)]
            inside = blocks[1:-1]
            eastward = [pltpu.roll(x, TC - 1, 1) for x in inside] + blocks[-1:]
            westward = blocks[:1] + [pltpu.roll(x, 1, 1) for x in inside]
            e = [
                jnp.where(strip_lane == TC - 1, eastward[u + 1], eastward[u])
                for u in range(tile_cols)
            ]
            w = [
                jnp.where(strip_lane == 0, westward[u], westward[u + 1]) for u in range(tile_cols)
            ]
            return (
                jnp.concatenate(inside, axis=1),
                jnp.concatenate(e, axis=1),
                jnp.concatenate(w, axis=1),
                across(pad, index, slice(a - 1, b - 1)),
                across(pad, index, slice(a + 1, b + 1)),
            )

        for r in range(strips):
            kc, ke, kw, kn, ks = around(kpad, (), r)
            strip = slice(r * TR, (r + 1) * TR)
            faces = [0.5 * RATE_PLANE * (kc + other) for other in (ke, kw, kn, ks)]
            for i in range(4):
                coef[i, strip] = faces[i]
            tc, te, tw, tn, ts = around(tpad, (top,), r)
            under = across(tpad, (top - 1,), slice(row0 + r * TR, row0 + (r + 1) * TR))
            value = tc + RATE_VERTICAL * (under - tc)
            for face, other in zip(faces, (te, tw, tn, ts)):
                value = value + face * (other - tc)
            for u in range(tile_cols):
                tiles3[r * tile_cols + u] = value[:, u * TC : (u + 1) * TC]

        x_copies = []
        for i in range(2):
            for rr in range(TR // 2):
                x_send[i, :, rr * TC : (rr + 1) * TC] = tiles3[:, i * (TR // 2) + rr, :]
            copy = send(x_send.at[i], x_recv.at[i], x_ss.at[i], x_rs.at[i], partner)
            copy.start()
            x_copies.append(copy)

        wait_bytes(req_recv.at[1:PLANE], req_rs.at[0])
        group_lane = iota((per_group, LANES), 1) // CAP
        group_row = iota((per_group, LANES), 0)
        tile_row = iota((tiles, LANES), 0).astype(F32)
        def make_picks(f):
            picks = []
            for g in range(groups):
                block = req_recv[g * per_group : (g + 1) * per_group, f, :]
                line = jnp.sum(
                    jnp.where(group_lane == group_row, block, 0.0), axis=0, keepdims=True
                )
                picks.append(jnp.where(line - 1.0 == tile_row, 1.0, 0.0))
            pick = jnp.concatenate(picks, axis=1)
            onehot[:, f * half : (f + 1) * half] = pick
            turned = jnp.transpose(jnp.concatenate([pick, pick], axis=0)).astype(BF16)
            lhs1[f * half : (f + 1) * half] = turned

        make_picks(0)

        def plane_rows(ref, c, f, d):
            return ref.at[c, f, d] if c % 2 == 0 else ref.at[c, f, :, d]

        slots1 = {}
        for c in range(n_chunks):
            for f in range(2):
                for d in range(1, RING):
                    slots1[c, f, d] = send(
                        plane_rows(send1, c, f, d),
                        recv1.at[c, :, f, d],
                        s1_ss.at[0],
                        s1_rs.at[c],
                        slot_peer(c % 2, -d),
                    )

        def columns(c, count=1):
            return slice(c * wide, (c + count) * wide)

        def pack_tiles(f, pair, source):
            for i, piece in enumerate(two_parts(source)):
                rhs[i * tiles : (i + 1) * tiles, columns(pair, 2)] = piece
            for c in (pair, pair + 1):
                packed = jnp.dot(
                    lhs1[f * half : (f + 1) * half],
                    rhs[:, columns(c)],
                    preferred_element_type=F32,
                )
                send1[c, f] = packed.reshape(RING, RING, CAP, wide)
                for d in FARTHEST_FIRST:
                    slots1[c, f, d].start()
                recv1[c, :, f, 0] = send1[c, f, 0] if c % 2 == 0 else send1[c, f, :, 0]

        for pair in (0, 2):
            pack_tiles(0, pair, x_send[pair // 2])
        make_picks(1)

        for load in rim_loads:
            load.wait()
        for side, row in ((0, first), (1, last)):
            for u in range(tile_cols):
                at = slice(u * TC, (u + 1) * TC)
                ns_send[side, 0:top, at] = tpad[0:top, u + 1, row, :]
                ns_send[side, layers : layers + top, at] = apad[0:top, u + 1, row, :]
        for side in range(2):
            packed = jnp.zeros((rows, LANES), F32)
            for l in range(top):
                packed = jnp.where(rim_lane == l, edge_column(tpad, (l,), side), packed)
                packed = jnp.where(
                    rim_lane == layers + l, edge_column(apad, (l,), side), packed
                )
            ew_send[side] = packed
        rims = rim_copies(ns_send, ns_recv, ew_send, ew_recv, rim_ss, rim_rs)
        for copy in rims:
            copy.start()

        wait_bytes(wblk.at[:, 1:RING], w_rs.at[0])
        for h in range(2):
            for d in range(RING):
                for i, piece in enumerate(two_parts(wblk[h, d])):
                    wcat[h, d, i * tiles : (i + 1) * tiles] = jnp.concatenate(
                        [piece, piece], axis=1
                    )

        for pair in (0, 2):
            x_copies[pair // 2].wait_recv()
            pack_tiles(1, pair, x_recv[pair // 2])

        for h in range(2):
            for d in range(RING):
                parts_of = jnp.concatenate(two_parts(wblk[h, d]), axis=0).astype(F32)
                turned = jnp.transpose(parts_of).astype(BF16)
                lhs2[h, d, :, 0 : 2 * tiles] = turned
                lhs2[h, d, :, 2 * tiles : 4 * tiles] = turned

        edge = jnp.zeros((rows, LANES), F32)
        apad[top, 0, row0:row1] = edge
        apad[top, tile_cols + 1, row0:row1] = edge
        put_line(apad, (top,), above, jnp.zeros((1, cols), F32))
        put_line(apad, (top,), below, jnp.zeros((1, cols), F32))

        wait_bytes(ns_recv, rim_rs.at[0])
        wait_bytes(ew_recv, rim_rs.at[1])
        for l in range(top):
            column_rims(tpad, (l,), ew_recv, l)
            column_rims(apad, (l,), ew_recv, layers + l)
        for side, has, at in ((0, has_north, first - 1), (1, has_south, last + 1)):
            for u in range(tile_cols):
                cut = slice(u * TC, (u + 1) * TC)
                tpad[0:top, u + 1, at, :] = ns_recv[side, 0:top, cut] * has
                apad[0:top, u + 1, at, :] = ns_recv[side, layers : layers + top, cut] * has

        def layer_step(l, r, total):
            strip = slice(r * TR, (r + 1) * TR)
            tc, *t_near = around(tpad, (l,), r)
            ac, *a_near = around(apad, (l,), r)
            flow = jnp.zeros_like(ac)
            for i in range(4):
                step = a_near[i] - ac
                flow = flow + coef[i, strip] * step
                total = total + (t_near[i] - tc) * step
            return ac + flow, ac, total

        def inner_layers(r):
            strip = slice(r * TR, (r + 1) * TR)
            inner = slice(row0 + r * TR, row0 + (r + 1) * TR)

            def body(l, total):
                value, ac, total = layer_step(l, r, total)
                over = across(apad, (l + 1,), inner)
                under = across(apad, (jnp.maximum(l - 1, 0),), inner)
                outv[l, strip] = value + RATE_VERTICAL * ((over - ac) + (under - ac))
                return total

            gacc[strip] = lax.fori_loop(0, top, body, jnp.zeros((TR, cols), F32))

        for r in range(0, 2):
            inner_layers(r)

        loads[4].wait()
        loads[5].wait()
        frame = columns_of[:, 2 * k_blocks : 2 * k_blocks + 1].astype(jnp.int32)
        for c in range(n_chunks):
            seen = jnp.zeros((tiles, wide), F32)
            for f in range(frames):
                seen = jnp.where(frame == f, obs_v[f, :, columns(c)], seen)
            mis[c] = -seen

        def weigh(c, d):
            both = jnp.dot(
                wcat[c % 2, d],
                jnp.concatenate(two_parts(recv1[c, d].reshape(LANES, wide)), axis=0),
                preferred_element_type=F32,
            )
            return both[0:tiles] + both[tiles : 2 * tiles]

        parts, spread = {}, {}
        for c in range(n_chunks):
            for d in range(1, RING):
                parts[c, d] = send(
                    part.at[c, d],
                    part_recv.at[c, d],
                    p_ss.at[0],
                    p_rs.at[c],
                    dense_peer(c % 2, -d),
                )
                spread[c, d] = send(
                    mis.at[c], mis_recv.at[c, d], m_ss.at[0], m_rs.at[c], dense_peer(c % 2, d)
                )
        for c in range(n_chunks):
            wait_bytes(recv1.at[c, 0 : RING - 1], s1_rs.at[c])
            for d in FARTHEST_FIRST:
                part[c, d] = weigh(c, d)
                parts[c, d].start()
            mis[c] += weigh(c, 0)

        inner_layers(2)

        for c in range(n_chunks):
            wait_bytes(part_recv.at[c, 1:RING], p_rs.at[c])
            mis[c] += part_recv[c, 1] + (part_recv[c, 2] + part_recv[c, 3])
            for d in FARTHEST_FIRST:
                spread[c, d].start()
            misfit_out[:, columns(c)] = mis[c]

        inner_layers(3)

        slots2 = {}
        for c in range(n_chunks):
            for f in range(2):
                for d in range(1, RING):
                    slots2[c, f, d] = send(
                        send2.at[c, :, f, d],
                        plane_rows(recv2, c, f, d),
                        s2_ss.at[0],
                        s2_rs.at[2 * c + f],
                        slot_peer(c % 2, d),
                    )
        for c in range(n_chunks):
            wait_bytes(mis_recv.at[c, 1:RING], m_rs.at[c])
            for d in range(RING):
                mh, ml = two_parts(mis_recv[c, d] if d else mis[c])
                packed = jnp.dot(
                    lhs2[c % 2, d],
                    jnp.concatenate([mh, mh, ml, ml], axis=0),
                    preferred_element_type=F32,
                )
                send2[c, d] = packed.reshape(2, RING, CAP, wide)
            for d in FARTHEST_FIRST:
                slots2[c, 1, d].start()
        for c in range(n_chunks):
            for d in FARTHEST_FIRST:
                slots2[c, 0, d].start()
        for c in range(n_chunks):
            for f in range(2):
                if c % 2 == 0:
                    recv2[c, f, 0] = send2[c, :, f, 0]
                else:
                    recv2[c, f, :, 0] = send2[c, :, f, 0]

        for r in range(4, strips):
            inner_layers(r)
        for like, sem in (
            (ns0_recv, rim0_ss.at[0]),
            (ew0_recv, rim0_ss.at[1]),
            (ns_recv, rim_ss.at[0]),
            (ew_recv, rim_ss.at[1]),
            (req_recv.at[1:PLANE], req_ss.at[0]),
            (wblk.at[:, 1:RING], w_ss.at[0]),
            (recv1.at[:, 0 : RING - 1], s1_ss.at[0]),
            (part.at[:, 1:RING], p_ss.at[0]),
            (part.at[:, 1:RING], m_ss.at[0]),
        ):
            wait_bytes(like, sem)
        for copy in x_copies:
            copy.wait_send()

        def gathered(c, f):
            wait_bytes(recv2.at[c, f, 0 : RING - 1], s2_rs.at[2 * c + f])
            pick = onehot[:, f * half : (f + 1) * half].astype(BF16)
            return jnp.dot(
                jnp.concatenate([pick, pick], axis=1),
                jnp.concatenate(two_parts(recv2[c, f].reshape(half, wide)), axis=0),
                preferred_element_type=F32,
            )

        xa_copies = []
        for c in range(n_chunks):
            xa_send[c] = gathered(c, 1)
            copy = send(xa_send.at[c], xa_recv.at[c], x_ss.at[2 + c], x_rs.at[2 + c], partner)
            copy.start()
            xa_copies.append(copy)
        sums = [gathered(c, 0) for c in range(n_chunks)]
        for copy in xa_copies:
            copy.wait_recv()
        added = jnp.concatenate([sums[c] + xa_recv[c] for c in range(n_chunks)], axis=1)
        for rr in range(TR):
            tiles3[:, rr, :] = added[:, rr * TC : (rr + 1) * TC]
        for r in range(strips):
            strip = slice(r * TR, (r + 1) * TR)
            inner = slice(row0 + r * TR, row0 + (r + 1) * TR)
            extra = jnp.concatenate(
                [tiles3[r * tile_cols + u] for u in range(tile_cols)], axis=1
            )
            put_line(apad, (top,), inner, across(apad, (top,), inner) + extra)
            outv[top - 1, strip] += RATE_VERTICAL * extra

        for side, row in ((0, first), (1, last)):
            ns2_send[side] = across(apad, (top,), slice(row, row + 1))
        for side in range(2):
            ew2_send[side] = jnp.broadcast_to(edge_column(apad, (top,), side), (rows, LANES))
        rims2 = rim_copies(ns2_send, ns2_recv, ew2_send, ew2_recv, rim2_ss, rim2_rs)
        for copy in rims2:
            copy.start()
        for r in range(strips):
            strip = slice(r * TR, (r + 1) * TR)
            inner = slice(row0 + r * TR, row0 + (r + 1) * TR)
            value, ac, total = layer_step(top, r, gacc[strip])
            under = across(apad, (top - 1,), inner)
            outv[top, strip] = value + RATE_VERTICAL * (under - ac)
            gradv[strip] = gin[strip] - (0.5 * RATE_PLANE) * total
        wait_bytes(recv2.at[:, :, 0 : RING - 1], s2_ss.at[0])
        for copy in xa_copies:
            copy.wait_send()

        wait_bytes(ns2_recv, rim2_rs.at[0])
        wait_bytes(ew2_recv, rim2_rs.at[1])
        for side, has, row, beyond in ((0, has_north, 0, first - 1), (1, has_south, rows - 1, last + 1)):
            at = slice(row, row + 1)
            rim = ns2_recv[side] * has
            slope = across(tpad, (top,), slice(beyond, beyond + 1)) - across(
                tpad, (top,), slice(row0 + row, row0 + row + 1)
            )
            outv[top, at] += coef[2 + side, at] * rim
            gradv[at] -= (0.5 * RATE_PLANE) * slope * rim
        for side, has, face, inside, beyond, edge_lane in (
            (0, has_west, 1, 1, 0, 0),
            (1, has_east, 0, tile_cols, tile_cols + 1, TC - 1),
        ):
            at = slice((inside - 1) * TC, inside * TC)
            rim = jnp.where(rim_lane == edge_lane, ew2_recv[side] * has, 0.0)
            slope = tpad[top, beyond, row0:row1] - tpad[top, inside, row0:row1]
            outv[top, :, at] += coef[face, :, at] * rim
            gradv[:, at] -= (0.5 * RATE_PLANE) * slope * rim

        wait_bytes(ns2_recv, rim2_ss.at[0])
        wait_bytes(ew2_recv, rim2_ss.at[1])

    dma = pltpu.SemaphoreType.DMA

    def vmem(*shape, dtype=F32):
        return pltpu.VMEM(shape, dtype)

    def pair(*shape):
        return [vmem(*shape), vmem(*shape)]

    tile = TR * TC
    scratch = [
        vmem(layers, tile_cols + 2, rows + 2 * TR, TC),
        vmem(layers, tile_cols + 2, rows + 2 * TR, TC),
        vmem(tile_cols + 2, rows + 2 * TR, TC),
        vmem(rows, cols),
        vmem(frames, tiles, tile),
        vmem(4, rows, cols),
        vmem(rows, cols),
        vmem(k_blocks, tiles, dtype=jnp.int32),
        vmem(k_blocks, tiles),
        vmem(1, tiles, dtype=jnp.int32),
        *pair(2, 2, cols),
        *pair(2, rows, LANES),
        *pair(2, 2 * layers, cols),
        *pair(2, rows, LANES),
        *pair(2, 1, cols),
        *pair(2, rows, LANES),
        vmem(2 * TR, LANES),
        vmem(groups, 8, LANES),
        vmem(PLANE, 8, LANES),
        vmem(tiles, TR, TC),
        vmem(tiles, n_slots),
        vmem(n_slots, 2 * tiles, dtype=BF16),
        vmem(2 * tiles, tile, dtype=BF16),
        *pair(2, RING, tiles, LANES),
        vmem(2, RING, 2 * tiles, 4 * tiles, dtype=BF16),
        vmem(2, RING, LANES, 4 * tiles, dtype=BF16),
        *pair(2, tiles, tile // 2),
        *pair(n_chunks, tiles, wide),
        vmem(n_chunks, 2, RING, RING, CAP, wide),
        vmem(n_chunks, RING, 2, RING, CAP, wide),
        *pair(n_chunks, RING, tiles, wide),
        vmem(n_chunks, tiles, wide),
        vmem(n_chunks, RING, tiles, wide),
        vmem(n_chunks, RING, 2, RING, CAP, wide),
        vmem(n_chunks, 2, RING, RING, CAP, wide),
        dma((9 + 4 * tile_cols,)),
        *[dma((2,)) for _ in range(6)],
        dma((2 + n_chunks,)), dma((2 + n_chunks,)),
        dma((1,)), dma((1,)),
        dma((1,)), dma((1,)),
        dma((1,)), dma((n_chunks,)),
        dma((1,)), dma((n_chunks,)),
        dma((1,)), dma((n_chunks,)),
        dma((1,)), dma((2 * n_chunks,)),
    ]
    in_hbm = pl.BlockSpec(memory_space=pltpu.HBM)
    in_vmem = pl.BlockSpec(memory_space=pltpu.VMEM)
    return pl.pallas_call(
        kernel,
        out_shape=(
            jax.ShapeDtypeStruct((tiles, tile), F32),
            jax.ShapeDtypeStruct((layers, rows, cols), F32),
            jax.ShapeDtypeStruct((rows, cols), F32),
        ),
        in_specs=[in_hbm] * 8,
        out_specs=[in_vmem] * 3,
        scratch_shapes=scratch,
        compiler_params=pltpu.CompilerParams(
            collective_id=0, has_side_effects=True, vmem_limit_bytes=48 * 1024 * 1024
        ),
    )


def write_out(results):
    count = len(results)

    def kernel(*refs):
        copies = [
            pltpu.make_async_copy(refs[i], refs[count + i], refs[-1].at[i]) for i in range(count)
        ]
        for copy in copies:
            copy.start()
        for copy in copies:
            copy.wait()

    return pl.pallas_call(
        kernel,
        out_shape=tuple(jax.ShapeDtypeStruct(x.shape, x.dtype) for x in results),
        in_specs=[pl.BlockSpec(memory_space=pltpu.VMEM)] * count,
        out_specs=[pl.BlockSpec(memory_space=pl.ANY)] * count,
        scratch_shapes=[pltpu.SemaphoreType.DMA((count,))],
        compiler_params=pltpu.CompilerParams(vmem_limit_bytes=8 * 1024 * 1024),
    )(*results)


def solution(mesh):
    n_gx, n_gy = mesh.shape["gx"], mesh.shape["gy"]

    def local(temp, cond, adj, grad, obs, frame_index, source_map, source_weight):
        layers, rows, cols = temp.shape
        call = make_kernel(n_gx, n_gy, layers, rows, cols, obs.shape[0], source_map.shape[1])
        operands = (
            temp, cond, adj, grad, obs, frame_index[None, :], source_map.T, source_weight.T
        )
        results = call(*(pltpu.with_memory_space_constraint(x, pltpu.HBM) for x in operands))
        return write_out(results)

    placed = (
        P(None, "gx", "gy"),
        P("gx", "gy"),
        P(None, "gx", "gy"),
        P("gx", "gy"),
        P(None, ("gx", "gy"), None),
        P(("gx", "gy")),
        P(("gx", "gy"), None),
        P(("gx", "gy"), None),
    )
    return jax.shard_map(
        local,
        mesh=mesh,
        in_specs=placed,
        out_specs=(P(("gx", "gy"), None), P(None, "gx", "gy"), P("gx", "gy")),
        check_vma=False,
    )
```

```python
import jax
import jax.numpy as jnp
from jax import lax
from jax.experimental import pallas as pl
from jax.experimental.pallas import tpu as pltpu
from jax.sharding import PartitionSpec as P

TR = 8
TC = 128
CAP = 16
LANES = 128
RATE_PLANE = 0.2
RATE_VERTICAL = 0.08
MESH = pl.DeviceIdType.MESH
F32 = jnp.float32
BF16 = jnp.bfloat16


def iota(shape, dim):
    return lax.broadcasted_iota(jnp.int32, shape, dim)


def two_parts(x):
    hi = x.astype(BF16)
    lo = (x - hi.astype(F32)).astype(BF16)
    return hi, lo


RING = 4
PLANE = RING * RING
FARTHEST_FIRST = (2, 1, 3)


def make_kernel(n_gx, n_gy, layers, rows, cols, frames, k_blocks):
    tiles = (rows // TR) * (cols // TC)
    half = PLANE * CAP
    n_slots = 2 * half
    row0, row1 = TR, TR + rows
    strips = rows // TR
    tile_cols = cols // TC
    top = layers - 1
    per_group = LANES // CAP
    groups = PLANE // per_group
    others = range(1, PLANE)
    n_chunks = 4
    wide = cols // n_chunks

    def kernel(
        temp, cond, adj, grad, obs, frame_in, map_in, weight_in,
        misfit_out, outv, gradv,
        tpad, apad, kpad, gin, obs_v, coef, gacc, map_v, weight_v, frame_v,
        ns0_send, ns0_recv, ew0_send, ew0_recv,
        ns_send, ns_recv, ew_send, ew_recv,
        ns2_send, ns2_recv, ew2_send, ew2_recv,
        small, req_send, req_recv, tiles3, onehot, lhs1, rhs,
        wsend, wblk, wcat, lhs2,
        x_send, x_recv, xa_send, xa_recv,
        send1, recv1, part, part_recv, mis, mis_recv, send2, recv2,
        in_sem,
        rim0_ss, rim0_rs, rim_ss, rim_rs, rim2_ss, rim2_rs, x_ss, x_rs,
        req_ss, req_rs, w_ss, w_rs, s1_ss, s1_rs, p_ss, p_rs, m_ss, m_rs, s2_ss, s2_rs,
    ):
        gx = lax.axis_index("gx")
        gy = lax.axis_index("gy")
        gx_y = lax.rem(gx, RING)
        gx_x = lax.rem(gx // RING, 2)
        gx_z = gx // (2 * RING)
        north, south = lax.rem(gx + n_gx - 1, n_gx), lax.rem(gx + 1, n_gx)
        west, east = lax.rem(gy + n_gy - 1, n_gy), lax.rem(gy + 1, n_gy)
        sides = ({"gx": north}, {"gx": south}, {"gy": west}, {"gy": east})
        partner = {"gx": gx + RING - 2 * RING * gx_x}

        def along(dz, dy):
            z = lax.rem(gx_z + dz % RING, RING)
            y = lax.rem(gx_y + dy % RING, RING)
            return {"gx": z * (2 * RING) + gx_x * RING + y}

        def slot_peer(h, d):
            return along(0, d) if h == 0 else along(d, 0)

        def dense_peer(h, d):
            return along(d, 0) if h == 0 else along(0, d)

        def wait_bytes(like, sem):
            pltpu.make_async_copy(like, like, sem).wait()

        def send(src, dst, ss, rs, device):
            return pltpu.make_async_remote_copy(
                src_ref=src,
                dst_ref=dst,
                send_sem=ss,
                recv_sem=rs,
                device_id=device,
                device_id_type=MESH,
            )

        def block_loads(src, src_layers, pad, pad_layers, sem):
            return [
                pltpu.make_async_copy(
                    src.at[(*src_layers, slice(None), slice(u * TC, (u + 1) * TC))],
                    pad.at[(*pad_layers, u + 1, slice(row0, row1))],
                    in_sem.at[sem],
                )
                for u in range(tile_cols)
            ]

        both = (slice(top - 1, layers),)
        rest = (slice(0, top - 1),)
        all_layers = (slice(0, layers),)
        first_loads = block_loads(temp, both, tpad, both, 0) + block_loads(cond, (), kpad, (), 1)
        rim_loads = block_loads(temp, rest, tpad, rest, 2) + block_loads(
            adj, all_layers, apad, all_layers, 3
        )
        loads = [None] * 4 + [
            pltpu.make_async_copy(grad, gin, in_sem.at[4]),
            pltpu.make_async_copy(obs, obs_v, in_sem.at[5]),
            pltpu.make_async_copy(map_in, map_v, in_sem.at[6]),
            pltpu.make_async_copy(weight_in, weight_v, in_sem.at[7]),
            pltpu.make_async_copy(frame_in, frame_v, in_sem.at[8]),
        ]
        for load in first_loads:
            load.start()

        barrier = pltpu.get_barrier_semaphore()
        greeted = [along(b % RING, b // RING) for b in others] + [partner] + list(sides)
        for device in greeted:
            pl.semaphore_signal(barrier, inc=1, device_id=device, device_id_type=MESH)

        for load in loads[6:] + rim_loads + loads[4:6]:
            load.start()

        inside = (slice(1, tile_cols + 1), slice(row0, row1))
        wait_bytes(tpad.at[(*both, *inside)], in_sem.at[0])
        wait_bytes(kpad.at[inside], in_sem.at[1])
        first, last = row0, row1 - 1

        def across(pad, index, at):
            return jnp.concatenate(
                [pad[(*index, u, at, slice(None))] for u in range(1, tile_cols + 1)], axis=-1
            )

        def put_line(pad, index, at, value):
            for u in range(tile_cols):
                pad[(*index, u + 1, at, slice(None))] = value[..., u * TC : (u + 1) * TC]

        def edge_column(pad, index, side):
            u, at = ((1, 0), (tile_cols, TC - 1))[side]
            return pad[(*index, u, slice(row0, row1), slice(at, at + 1))]

        rim_lane = iota((rows, LANES), 1)
        for side, row in ((0, first), (1, last)):
            ns0_send[side, 0:1] = across(tpad, (top,), slice(row, row + 1))
            ns0_send[side, 1:2] = across(kpad, (), slice(row, row + 1))
        for side in range(2):
            ew0_send[side] = jnp.where(
                rim_lane == 0, edge_column(tpad, (top,), side), edge_column(kpad, (), side)
            )

        pl.semaphore_wait(barrier, len(greeted))

        def rim_copies(ns_s, ns_r, ew_s, ew_r, ss, rs):
            copies = []
            for i in range(4):
                src, dst = (ns_s, ns_r) if i < 2 else (ew_s, ew_r)
                copies.append(
                    pltpu.make_async_remote_copy(
                        src_ref=src.at[i % 2],
                        dst_ref=dst.at[1 - i % 2],
                        send_sem=ss.at[i // 2],
                        recv_sem=rs.at[i // 2],
                        device_id=sides[i],
                        device_id_type=MESH,
                    )
                )
            return copies

        rims0 = rim_copies(ns0_send, ns0_recv, ew0_send, ew0_recv, rim0_ss, rim0_rs)
        for copy in rims0:
            copy.start()

        for load in loads[6:]:
            load.wait()
        small[0:k_blocks, 0:tiles] = map_v[...].astype(F32)
        small[k_blocks : 2 * k_blocks, 0:tiles] = weight_v[...]
        small[2 * k_blocks : 2 * k_blocks + 1, 0:tiles] = frame_v[...].astype(F32)
        columns_of = jnp.transpose(small[...])[0:tiles]
        weight = columns_of[:, k_blocks : 2 * k_blocks]
        code = columns_of[:, 0:k_blocks].astype(jnp.int32)
        plate = code >> ((tiles * n_gy).bit_length() - 1)
        far = ((plate ^ gx) >> 2) & 1
        dz = ((plate >> 3) - gx_z) & 3
        dy = (plate - gx) & 3
        block = far * PLANE + dy * RING + dz
        wish = ((code & (tiles - 1)) + 1).astype(F32)
        lane = iota((tiles, LANES), 1)
        lane_slot = iota((tiles, n_slots), 1)
        lower = jnp.where(iota((tiles, tiles), 0) > iota((tiles, tiles), 1), 1.0, 0.0)
        hits = [jnp.where(block[:, k : k + 1] == lane, 1.0, 0.0) for k in range(k_blocks)]
        before = jnp.dot(lower, jnp.concatenate(hits, axis=1), preferred_element_type=F32)
        base = jnp.zeros((1, LANES), F32)
        wanted = jnp.zeros((tiles, n_slots), F32)
        weights = [jnp.zeros((tiles, n_slots), F32) for _ in range(2)]
        ranks = []
        for k in range(k_blocks):
            earlier = before[:, k * LANES : (k + 1) * LANES] + base
            base = base + jnp.sum(hits[k], axis=0, keepdims=True)
            ranks.append(jnp.sum(hits[k] * earlier, axis=1, keepdims=True).astype(jnp.int32))
            here = block[:, k : k + 1] * CAP + ranks[k] == lane_slot
            wanted = wanted + jnp.where(here, wish[:, k : k + 1], 0.0)
        asked = jnp.sum(wanted, axis=0, keepdims=True)
        for g in range(groups):
            for f in range(2):
                at = f * half + g * LANES
                req_send[g, f : f + 1] = asked[:, at : at + LANES]

        for b in others:
            send(
                req_send.at[b // per_group],
                req_recv.at[b],
                req_ss.at[0],
                req_rs.at[0],
                along(b % RING, b // RING),
            ).start()
        for k in range(k_blocks):
            col = slice(k, k + 1)
            for h, (dense, slot) in enumerate(((dz, dy), (dy, dz))):
                at = (dense * LANES + far * (LANES // 2) + slot * CAP)[:, col] + ranks[k]
                weights[h] = weights[h] + jnp.where(at == lane_slot, weight[:, col], 0.0)
        for h in range(2):
            for d in range(RING):
                wsend[h, d] = weights[h][:, d * LANES : (d + 1) * LANES]
            wblk[h, 0] = weights[h][:, 0:LANES]
            for d in range(1, RING):
                send(
                    wsend.at[h, d], wblk.at[h, d], w_ss.at[0], w_rs.at[0], dense_peer(h, d)
                ).start()
        req_recv[0] = req_send[0]

        has_north = jnp.where(gx > 0, 1.0, 0.0)
        has_south = jnp.where(gx < n_gx - 1, 1.0, 0.0)
        has_west = jnp.where(gy > 0, 1.0, 0.0)
        has_east = jnp.where(gy < n_gy - 1, 1.0, 0.0)

        def column_rims(pad, index, source, lane_at):
            for side, has, at in ((0, has_west, 0), (1, has_east, tile_cols + 1)):
                value = source[side, :, lane_at : lane_at + 1] * has
                pad[(*index, at, slice(row0, row1))] = jnp.broadcast_to(value, (rows, LANES))

        wait_bytes(ns0_recv, rim0_rs.at[0])
        wait_bytes(ew0_recv, rim0_rs.at[1])
        above, below = slice(first - 1, first), slice(last + 1, last + 2)
        put_line(kpad, (), above, ns0_recv[0, 1:2] * has_north)
        put_line(kpad, (), below, ns0_recv[1, 1:2] * has_south)
        column_rims(kpad, (), ew0_recv, 1)
        put_line(tpad, (top,), above, ns0_recv[0, 0:1] * has_north)
        put_line(tpad, (top,), below, ns0_recv[1, 0:1] * has_south)
        column_rims(tpad, (top,), ew0_recv, 0)

        strip_lane = iota((TR, TC), 1)

        def around(pad, index, r):
            a, b = row0 + r * TR, row0 + (r + 1) * TR
            blocks = [pad[(*index, u, slice(a, b), slice(None))] for u in range(tile_cols + 2)]
            inside = blocks[1:-1]
            eastward = [pltpu.roll(x, TC - 1, 1) for x in inside] + blocks[-1:]
            westward = blocks[:1] + [pltpu.roll(x, 1, 1) for x in inside]
            e = [
                jnp.where(strip_lane == TC - 1, eastward[u + 1], eastward[u])
                for u in range(tile_cols)
            ]
            w = [
                jnp.where(strip_lane == 0, westward[u], westward[u + 1]) for u in range(tile_cols)
            ]
            return (
                jnp.concatenate(inside, axis=1),
                jnp.concatenate(e, axis=1),
                jnp.concatenate(w, axis=1),
                across(pad, index, slice(a - 1, b - 1)),
                across(pad, index, slice(a + 1, b + 1)),
            )

        for r in range(strips):
            kc, ke, kw, kn, ks = around(kpad, (), r)
            strip = slice(r * TR, (r + 1) * TR)
            faces = [0.5 * RATE_PLANE * (kc + other) for other in (ke, kw, kn, ks)]
            for i in range(4):
                coef[i, strip] = faces[i]
            tc, te, tw, tn, ts = around(tpad, (top,), r)
            under = across(tpad, (top - 1,), slice(row0 + r * TR, row0 + (r + 1) * TR))
            value = tc + RATE_VERTICAL * (under - tc)
            for face, other in zip(faces, (te, tw, tn, ts)):
                value = value + face * (other - tc)
            for u in range(tile_cols):
                tiles3[r * tile_cols + u] = value[:, u * TC : (u + 1) * TC]

        x_copies = []
        for i in range(2):
            for rr in range(TR // 2):
                x_send[i, :, rr * TC : (rr + 1) * TC] = tiles3[:, i * (TR // 2) + rr, :]
            copy = send(x_send.at[i], x_recv.at[i], x_ss.at[i], x_rs.at[i], partner)
            copy.start()
            x_copies.append(copy)

        wait_bytes(req_recv.at[1:PLANE], req_rs.at[0])
        group_lane = iota((per_group, LANES), 1) // CAP
        group_row = iota((per_group, LANES), 0)
        tile_row = iota((tiles, LANES), 0).astype(F32)
        def make_picks(f):
            picks = []
            for g in range(groups):
                block = req_recv[g * per_group : (g + 1) * per_group, f, :]
                line = jnp.sum(
                    jnp.where(group_lane == group_row, block, 0.0), axis=0, keepdims=True
                )
                picks.append(jnp.where(line - 1.0 == tile_row, 1.0, 0.0))
            pick = jnp.concatenate(picks, axis=1)
            onehot[:, f * half : (f + 1) * half] = pick
            turned = jnp.transpose(jnp.concatenate([pick, pick], axis=0)).astype(BF16)
            lhs1[f * half : (f + 1) * half] = turned

        make_picks(0)

        def plane_rows(ref, c, f, d):
            return ref.at[0, c // 2, f, d] if c % 2 == 0 else ref.at[1, c // 2, f, :, d]

        def near_rows(ref, h, d):
            return ref.at[0, :, 0, d] if h == 0 else ref.at[1, :, 0, :, d]

        slots1 = {}
        for d in range(1, RING):
            for c in range(n_chunks):
                slots1[c, 1, d] = send(
                    plane_rows(send1, c, 1, d),
                    recv1.at[c % 2, c // 2, :, 1, d],
                    s1_ss.at[0],
                    s1_rs.at[c],
                    slot_peer(c % 2, -d),
                )
            for h in range(2):
                slots1[h, 0, d] = send(
                    near_rows(send1, h, d),
                    recv1.at[h, :, :, 0, d],
                    s1_ss.at[0],
                    s1_rs.at[n_chunks + h],
                    slot_peer(h, -d),
                )

        def columns(c, count=1):
            return slice(c * wide, (c + count) * wide)

        def pack_tiles(f, pair, source):
            for i, piece in enumerate(two_parts(source)):
                rhs[i * tiles : (i + 1) * tiles, columns(pair, 2)] = piece
            for c in (pair, pair + 1):
                packed = jnp.dot(
                    lhs1[f * half : (f + 1) * half],
                    rhs[:, columns(c)],
                    preferred_element_type=F32,
                )
                send1[c % 2, c // 2, f] = packed.reshape(RING, RING, CAP, wide)
                if f == 1:
                    for d in FARTHEST_FIRST:
                        slots1[c, f, d].start()
                recv1[c % 2, c // 2, :, f, 0] = send1[c % 2, c // 2, f, 0] if c % 2 == 0 else send1[c % 2, c // 2, f, :, 0]

        for pair in (0, 2):
            pack_tiles(0, pair, x_send[pair // 2])
        for d in FARTHEST_FIRST:
            for h in range(2):
                slots1[h, 0, d].start()
        make_picks(1)

        wait_bytes(tpad.at[(*rest, *inside)], in_sem.at[2])
        wait_bytes(apad.at[(*all_layers, *inside)], in_sem.at[3])
        for side, row in ((0, first), (1, last)):
            for u in range(tile_cols):
                at = slice(u * TC, (u + 1) * TC)
                ns_send[side, 0:top, at] = tpad[0:top, u + 1, row, :]
                ns_send[side, layers : layers + top, at] = apad[0:top, u + 1, row, :]
        for side in range(2):
            packed = jnp.zeros((rows, LANES), F32)
            for l in range(top):
                packed = jnp.where(rim_lane == l, edge_column(tpad, (l,), side), packed)
                packed = jnp.where(
                    rim_lane == layers + l, edge_column(apad, (l,), side), packed
                )
            ew_send[side] = packed
        rims = rim_copies(ns_send, ns_recv, ew_send, ew_recv, rim_ss, rim_rs)
        for copy in rims:
            copy.start()

        wait_bytes(wblk.at[:, 1:RING], w_rs.at[0])
        for h in range(2):
            for d in range(RING):
                for i, piece in enumerate(two_parts(wblk[h, d])):
                    wcat[h, d, i * tiles : (i + 1) * tiles] = jnp.concatenate(
                        [piece, piece], axis=1
                    )

        for pair in (0, 2):
            x_copies[pair // 2].wait_recv()
            pack_tiles(1, pair, x_recv[pair // 2])

        for h in range(2):
            for d in range(RING):
                parts_of = jnp.concatenate(two_parts(wblk[h, d]), axis=0).astype(F32)
                turned = jnp.transpose(parts_of).astype(BF16)
                lhs2[h, d, :, 0 : 2 * tiles] = turned
                lhs2[h, d, :, 2 * tiles : 4 * tiles] = turned

        edge = jnp.zeros((rows, LANES), F32)
        apad[top, 0, row0:row1] = edge
        apad[top, tile_cols + 1, row0:row1] = edge
        put_line(apad, (top,), above, jnp.zeros((1, cols), F32))
        put_line(apad, (top,), below, jnp.zeros((1, cols), F32))

        wait_bytes(ns_recv, rim_rs.at[0])
        wait_bytes(ew_recv, rim_rs.at[1])
        for l in range(top):
            column_rims(tpad, (l,), ew_recv, l)
            column_rims(apad, (l,), ew_recv, layers + l)
        for side, has, at in ((0, has_north, first - 1), (1, has_south, last + 1)):
            for u in range(tile_cols):
                cut = slice(u * TC, (u + 1) * TC)
                tpad[0:top, u + 1, at, :] = ns_recv[side, 0:top, cut] * has
                apad[0:top, u + 1, at, :] = ns_recv[side, layers : layers + top, cut] * has

        def layer_step(l, r, total):
            strip = slice(r * TR, (r + 1) * TR)
            tc, *t_near = around(tpad, (l,), r)
            ac, *a_near = around(apad, (l,), r)
            flow = jnp.zeros_like(ac)
            for i in range(4):
                step = a_near[i] - ac
                flow = flow + coef[i, strip] * step
                total = total + (t_near[i] - tc) * step
            return ac + flow, ac, total

        def inner_layers(r):
            strip = slice(r * TR, (r + 1) * TR)
            inner = slice(row0 + r * TR, row0 + (r + 1) * TR)

            def body(l, total):
                value, ac, total = layer_step(l, r, total)
                over = across(apad, (l + 1,), inner)
                under = across(apad, (jnp.maximum(l - 1, 0),), inner)
                outv[l, strip] = value + RATE_VERTICAL * ((over - ac) + (under - ac))
                return total

            gacc[strip] = lax.fori_loop(0, top, body, jnp.zeros((TR, cols), F32))

        for r in range(0, 2):
            inner_layers(r)

        loads[4].wait()
        loads[5].wait()
        frame = columns_of[:, 2 * k_blocks : 2 * k_blocks + 1].astype(jnp.int32)
        for c in range(n_chunks):
            seen = jnp.zeros((tiles, wide), F32)
            for f in range(frames):
                seen = jnp.where(frame == f, obs_v[f, :, columns(c)], seen)
            mis[c] = -seen

        def weigh(c, d):
            both = jnp.dot(
                wcat[c % 2, d],
                jnp.concatenate(two_parts(recv1[c % 2, c // 2, d].reshape(LANES, wide)), axis=0),
                preferred_element_type=F32,
            )
            return both[0:tiles] + both[tiles : 2 * tiles]

        parts, spread = {}, {}
        for c in range(n_chunks):
            for d in range(1, RING):
                parts[c, d] = send(
                    part.at[c, d],
                    part_recv.at[c, d],
                    p_ss.at[0],
                    p_rs.at[c],
                    dense_peer(c % 2, -d),
                )
                spread[c, d] = send(
                    mis.at[c], mis_recv.at[c, d], m_ss.at[0], m_rs.at[c], dense_peer(c % 2, d)
                )
        for c in range(n_chunks):
            if c < 2:
                wait_bytes(recv1.at[c, :, 0 : RING - 1, 0], s1_rs.at[n_chunks + c])
            wait_bytes(recv1.at[c % 2, c // 2, 0 : RING - 1, 1], s1_rs.at[c])
            for d in FARTHEST_FIRST:
                part[c, d] = weigh(c, d)
                parts[c, d].start()
            mis[c] += weigh(c, 0)

        inner_layers(2)

        for c in range(n_chunks):
            wait_bytes(part_recv.at[c, 1:RING], p_rs.at[c])
            mis[c] += part_recv[c, 1] + (part_recv[c, 2] + part_recv[c, 3])
            for d in FARTHEST_FIRST:
                spread[c, d].start()
            misfit_out[:, columns(c)] = mis[c]

        inner_layers(3)

        slots2 = {}
        for d in range(1, RING):
            for c in range(n_chunks):
                slots2[c, 1, d] = send(
                    send2.at[c % 2, c // 2, :, 1, d],
                    plane_rows(recv2, c, 1, d),
                    s2_ss.at[0],
                    s2_rs.at[c],
                    slot_peer(c % 2, d),
                )
            for h in range(2):
                slots2[h, 0, d] = send(
                    send2.at[h, :, :, 0, d],
                    near_rows(recv2, h, d),
                    s2_ss.at[0],
                    s2_rs.at[n_chunks + h],
                    slot_peer(h, d),
                )
        for c in range(n_chunks):
            wait_bytes(mis_recv.at[c, 1:RING], m_rs.at[c])
            for d in range(RING):
                mh, ml = two_parts(mis_recv[c, d] if d else mis[c])
                packed = jnp.dot(
                    lhs2[c % 2, d],
                    jnp.concatenate([mh, mh, ml, ml], axis=0),
                    preferred_element_type=F32,
                )
                send2[c % 2, c // 2, d] = packed.reshape(2, RING, CAP, wide)
            for d in FARTHEST_FIRST:
                slots2[c, 1, d].start()
        for d in FARTHEST_FIRST:
            for h in range(2):
                slots2[h, 0, d].start()
        for c in range(n_chunks):
            for f in range(2):
                if c % 2 == 0:
                    recv2[c % 2, c // 2, f, 0] = send2[c % 2, c // 2, :, f, 0]
                else:
                    recv2[c % 2, c // 2, f, :, 0] = send2[c % 2, c // 2, :, f, 0]

        for r in range(4, strips):
            inner_layers(r)
        for like, sem in (
            (ns0_recv, rim0_ss.at[0]),
            (ew0_recv, rim0_ss.at[1]),
            (ns_recv, rim_ss.at[0]),
            (ew_recv, rim_ss.at[1]),
            (req_recv.at[1:PLANE], req_ss.at[0]),
            (wblk.at[:, 1:RING], w_ss.at[0]),
            (recv1.at[:, :, 0 : RING - 1], s1_ss.at[0]),
            (part.at[:, 1:RING], p_ss.at[0]),
            (part.at[:, 1:RING], m_ss.at[0]),
        ):
            wait_bytes(like, sem)
        for copy in x_copies:
            copy.wait_send()

        def gathered(c, f):
            if f == 1:
                wait_bytes(recv2.at[c % 2, c // 2, 1, 0 : RING - 1], s2_rs.at[c])
            elif c < 2:
                wait_bytes(recv2.at[c, :, 0, 0 : RING - 1], s2_rs.at[n_chunks + c])
            pick = onehot[:, f * half : (f + 1) * half].astype(BF16)
            return jnp.dot(
                jnp.concatenate([pick, pick], axis=1),
                jnp.concatenate(two_parts(recv2[c % 2, c // 2, f].reshape(half, wide)), axis=0),
                preferred_element_type=F32,
            )

        xa_copies = []
        for c in range(n_chunks):
            xa_send[c] = gathered(c, 1)
            copy = send(xa_send.at[c], xa_recv.at[c], x_ss.at[2 + c], x_rs.at[2 + c], partner)
            copy.start()
            xa_copies.append(copy)
        sums = [gathered(c, 0) for c in range(n_chunks)]
        for copy in xa_copies:
            copy.wait_recv()
        added = jnp.concatenate([sums[c] + xa_recv[c] for c in range(n_chunks)], axis=1)
        for rr in range(TR):
            tiles3[:, rr, :] = added[:, rr * TC : (rr + 1) * TC]
        for r in range(strips):
            strip = slice(r * TR, (r + 1) * TR)
            inner = slice(row0 + r * TR, row0 + (r + 1) * TR)
            extra = jnp.concatenate(
                [tiles3[r * tile_cols + u] for u in range(tile_cols)], axis=1
            )
            put_line(apad, (top,), inner, across(apad, (top,), inner) + extra)
            outv[top - 1, strip] += RATE_VERTICAL * extra

        for side, row in ((0, first), (1, last)):
            ns2_send[side] = across(apad, (top,), slice(row, row + 1))
        for side in range(2):
            ew2_send[side] = jnp.broadcast_to(edge_column(apad, (top,), side), (rows, LANES))
        rims2 = rim_copies(ns2_send, ns2_recv, ew2_send, ew2_recv, rim2_ss, rim2_rs)
        for copy in rims2:
            copy.start()
        for r in range(strips):
            strip = slice(r * TR, (r + 1) * TR)
            inner = slice(row0 + r * TR, row0 + (r + 1) * TR)
            value, ac, total = layer_step(top, r, gacc[strip])
            under = across(apad, (top - 1,), inner)
            outv[top, strip] = value + RATE_VERTICAL * (under - ac)
            gradv[strip] = gin[strip] - (0.5 * RATE_PLANE) * total
        wait_bytes(recv2.at[:, :, :, 0 : RING - 1], s2_ss.at[0])
        for copy in xa_copies:
            copy.wait_send()

        wait_bytes(ns2_recv, rim2_rs.at[0])
        wait_bytes(ew2_recv, rim2_rs.at[1])
        for side, has, row, beyond in ((0, has_north, 0, first - 1), (1, has_south, rows - 1, last + 1)):
            at = slice(row, row + 1)
            rim = ns2_recv[side] * has
            slope = across(tpad, (top,), slice(beyond, beyond + 1)) - across(
                tpad, (top,), slice(row0 + row, row0 + row + 1)
            )
            outv[top, at] += coef[2 + side, at] * rim
            gradv[at] -= (0.5 * RATE_PLANE) * slope * rim
        for side, has, face, inside, beyond, edge_lane in (
            (0, has_west, 1, 1, 0, 0),
            (1, has_east, 0, tile_cols, tile_cols + 1, TC - 1),
        ):
            at = slice((inside - 1) * TC, inside * TC)
            rim = jnp.where(rim_lane == edge_lane, ew2_recv[side] * has, 0.0)
            slope = tpad[top, beyond, row0:row1] - tpad[top, inside, row0:row1]
            outv[top, :, at] += coef[face, :, at] * rim
            gradv[:, at] -= (0.5 * RATE_PLANE) * slope * rim

        wait_bytes(ns2_recv, rim2_ss.at[0])
        wait_bytes(ew2_recv, rim2_ss.at[1])

    dma = pltpu.SemaphoreType.DMA

    def vmem(*shape, dtype=F32):
        return pltpu.VMEM(shape, dtype)

    def pair(*shape):
        return [vmem(*shape), vmem(*shape)]

    tile = TR * TC
    scratch = [
        vmem(layers, tile_cols + 2, rows + 2 * TR, TC),
        vmem(layers, tile_cols + 2, rows + 2 * TR, TC),
        vmem(tile_cols + 2, rows + 2 * TR, TC),
        vmem(rows, cols),
        vmem(frames, tiles, tile),
        vmem(4, rows, cols),
        vmem(rows, cols),
        vmem(k_blocks, tiles, dtype=jnp.int32),
        vmem(k_blocks, tiles),
        vmem(1, tiles, dtype=jnp.int32),
        *pair(2, 2, cols),
        *pair(2, rows, LANES),
        *pair(2, 2 * layers, cols),
        *pair(2, rows, LANES),
        *pair(2, 1, cols),
        *pair(2, rows, LANES),
        vmem(2 * TR, LANES),
        vmem(groups, 8, LANES),
        vmem(PLANE, 8, LANES),
        vmem(tiles, TR, TC),
        vmem(tiles, n_slots),
        vmem(n_slots, 2 * tiles, dtype=BF16),
        vmem(2 * tiles, tile, dtype=BF16),
        *pair(2, RING, tiles, LANES),
        vmem(2, RING, 2 * tiles, 4 * tiles, dtype=BF16),
        vmem(2, RING, LANES, 4 * tiles, dtype=BF16),
        *pair(2, tiles, tile // 2),
        *pair(n_chunks, tiles, wide),
        vmem(2, n_chunks // 2, 2, RING, RING, CAP, wide),
        vmem(2, n_chunks // 2, RING, 2, RING, CAP, wide),
        *pair(n_chunks, RING, tiles, wide),
        vmem(n_chunks, tiles, wide),
        vmem(n_chunks, RING, tiles, wide),
        vmem(2, n_chunks // 2, RING, 2, RING, CAP, wide),
        vmem(2, n_chunks // 2, 2, RING, RING, CAP, wide),
        dma((9,)),
        *[dma((2,)) for _ in range(6)],
        dma((2 + n_chunks,)), dma((2 + n_chunks,)),
        dma((1,)), dma((1,)),
        dma((1,)), dma((1,)),
        dma((1,)), dma((2 + n_chunks,)),
        dma((1,)), dma((n_chunks,)),
        dma((1,)), dma((n_chunks,)),
        dma((1,)), dma((2 + n_chunks,)),
    ]
    in_hbm = pl.BlockSpec(memory_space=pltpu.HBM)
    in_vmem = pl.BlockSpec(memory_space=pltpu.VMEM)
    return pl.pallas_call(
        kernel,
        out_shape=(
            jax.ShapeDtypeStruct((tiles, tile), F32),
            jax.ShapeDtypeStruct((layers, rows, cols), F32),
            jax.ShapeDtypeStruct((rows, cols), F32),
        ),
        in_specs=[in_hbm] * 8,
        out_specs=[in_vmem] * 3,
        scratch_shapes=scratch,
        compiler_params=pltpu.CompilerParams(
            collective_id=0, has_side_effects=True, vmem_limit_bytes=48 * 1024 * 1024
        ),
    )


def write_out(results):
    count = len(results)

    def kernel(*refs):
        copies = [
            pltpu.make_async_copy(refs[i], refs[count + i], refs[-1].at[i]) for i in range(count)
        ]
        for copy in copies:
            copy.start()
        for copy in copies:
            copy.wait()

    return pl.pallas_call(
        kernel,
        out_shape=tuple(jax.ShapeDtypeStruct(x.shape, x.dtype) for x in results),
        in_specs=[pl.BlockSpec(memory_space=pltpu.VMEM)] * count,
        out_specs=[pl.BlockSpec(memory_space=pl.ANY)] * count,
        scratch_shapes=[pltpu.SemaphoreType.DMA((count,))],
        compiler_params=pltpu.CompilerParams(vmem_limit_bytes=8 * 1024 * 1024),
    )(*results)


def solution(mesh):
    n_gx, n_gy = mesh.shape["gx"], mesh.shape["gy"]

    def local(temp, cond, adj, grad, obs, frame_index, source_map, source_weight):
        layers, rows, cols = temp.shape
        call = make_kernel(n_gx, n_gy, layers, rows, cols, obs.shape[0], source_map.shape[1])
        operands = (
            temp, cond, adj, grad, obs, frame_index[None, :], source_map.T, source_weight.T
        )
        results = call(*(pltpu.with_memory_space_constraint(x, pltpu.HBM) for x in operands))
        return write_out(results)

    placed = (
        P(None, "gx", "gy"),
        P("gx", "gy"),
        P(None, "gx", "gy"),
        P("gx", "gy"),
        P(None, ("gx", "gy"), None),
        P(("gx", "gy")),
        P(("gx", "gy"), None),
        P(("gx", "gy"), None),
    )
    return jax.shard_map(
        local,
        mesh=mesh,
        in_specs=placed,
        out_specs=(P(("gx", "gy"), None), P(None, "gx", "gy"), P("gx", "gy")),
        check_vma=False,
    )
```

```python
import jax
import jax.numpy as jnp
from jax import lax
from jax.experimental import pallas as pl
from jax.experimental.pallas import tpu as pltpu
from jax.sharding import PartitionSpec as P

TR = 8
TC = 128
CAP = 16
LANES = 128
RATE_PLANE = 0.2
RATE_VERTICAL = 0.08
MESH = pl.DeviceIdType.MESH
F32 = jnp.float32
BF16 = jnp.bfloat16


def iota(shape, dim):
    return lax.broadcasted_iota(jnp.int32, shape, dim)


def two_parts(x):
    hi = x.astype(BF16)
    lo = (x - hi.astype(F32)).astype(BF16)
    return hi, lo


RING = 4
PLANE = RING * RING
FARTHEST_FIRST = (2, 1, 3)


def make_kernel(n_gx, n_gy, layers, rows, cols, frames, k_blocks):
    tiles = (rows // TR) * (cols // TC)
    half = PLANE * CAP
    n_slots = 2 * half
    row0, row1 = TR, TR + rows
    strips = rows // TR
    tile_cols = cols // TC
    top = layers - 1
    per_group = LANES // CAP
    groups = PLANE // per_group
    others = range(1, PLANE)
    n_chunks = 4
    wide = cols // n_chunks

    def kernel(
        temp, cond, adj, grad, obs, frame_in, map_in, weight_in,
        misfit_out, outv, gradv,
        tpad, apad, kpad, gin, obs_v, coef, gacc, map_v, weight_v, frame_v,
        ns0_send, ns0_recv, ew0_send, ew0_recv,
        ns_send, ns_recv, ew_send, ew_recv,
        ns2_send, ns2_recv, ew2_send, ew2_recv,
        small, req_send, req_recv, tiles3, onehot, lhs1, rhs,
        wsend, wblk, wcat, lhs2,
        x_send, x_recv, xa_send, xa_recv,
        send1, recv1, part, part_recv, mis, mis_recv, send2, recv2,
        in_sem,
        rim0_ss, rim0_rs, rim_ss, rim_rs, rim2_ss, rim2_rs, x_ss, x_rs,
        req_ss, req_rs, w_ss, w_rs, s1_ss, s1_rs, p_ss, p_rs, m_ss, m_rs, s2_ss, s2_rs,
    ):
        gx = lax.axis_index("gx")
        gy = lax.axis_index("gy")
        gx_y = lax.rem(gx, RING)
        gx_x = lax.rem(gx // RING, 2)
        gx_z = gx // (2 * RING)
        north, south = lax.rem(gx + n_gx - 1, n_gx), lax.rem(gx + 1, n_gx)
        west, east = lax.rem(gy + n_gy - 1, n_gy), lax.rem(gy + 1, n_gy)
        sides = ({"gx": north}, {"gx": south}, {"gy": west}, {"gy": east})
        partner = {"gx": gx + RING - 2 * RING * gx_x}

        def along(dz, dy):
            z = lax.rem(gx_z + dz % RING, RING)
            y = lax.rem(gx_y + dy % RING, RING)
            return {"gx": z * (2 * RING) + gx_x * RING + y}

        def slot_peer(h, d):
            return along(0, d) if h == 0 else along(d, 0)

        def dense_peer(h, d):
            return along(d, 0) if h == 0 else along(0, d)

        def wait_bytes(like, sem):
            pltpu.make_async_copy(like, like, sem).wait()

        def send(src, dst, ss, rs, device):
            return pltpu.make_async_remote_copy(
                src_ref=src,
                dst_ref=dst,
                send_sem=ss,
                recv_sem=rs,
                device_id=device,
                device_id_type=MESH,
            )

        def block_loads(src, src_layers, pad, pad_layers, sem):
            return [
                pltpu.make_async_copy(
                    src.at[(*src_layers, slice(None), slice(u * TC, (u + 1) * TC))],
                    pad.at[(*pad_layers, u + 1, slice(row0, row1))],
                    in_sem.at[sem],
                )
                for u in range(tile_cols)
            ]

        both = (slice(top - 1, layers),)
        rest = (slice(0, top - 1),)
        all_layers = (slice(0, layers),)
        first_loads = block_loads(temp, both, tpad, both, 0) + block_loads(cond, (), kpad, (), 1)
        rim_loads = block_loads(temp, rest, tpad, rest, 2) + block_loads(
            adj, all_layers, apad, all_layers, 3
        )
        loads = [None] * 4 + [
            pltpu.make_async_copy(grad, gin, in_sem.at[4]),
            pltpu.make_async_copy(obs, obs_v, in_sem.at[5]),
            pltpu.make_async_copy(map_in, map_v, in_sem.at[6]),
            pltpu.make_async_copy(weight_in, weight_v, in_sem.at[7]),
            pltpu.make_async_copy(frame_in, frame_v, in_sem.at[8]),
        ]
        for load in first_loads:
            load.start()

        barrier = pltpu.get_barrier_semaphore()
        greeted = [along(b % RING, b // RING) for b in others] + [partner] + list(sides)
        for device in greeted:
            pl.semaphore_signal(barrier, inc=1, device_id=device, device_id_type=MESH)

        for load in loads[6:] + rim_loads + loads[4:6]:
            load.start()

        inside = (slice(1, tile_cols + 1), slice(row0, row1))
        wait_bytes(tpad.at[(*both, *inside)], in_sem.at[0])
        wait_bytes(kpad.at[inside], in_sem.at[1])
        first, last = row0, row1 - 1

        def across(pad, index, at):
            return jnp.concatenate(
                [pad[(*index, u, at, slice(None))] for u in range(1, tile_cols + 1)], axis=-1
            )

        def put_line(pad, index, at, value):
            for u in range(tile_cols):
                pad[(*index, u + 1, at, slice(None))] = value[..., u * TC : (u + 1) * TC]

        def edge_column(pad, index, side):
            u, at = ((1, 0), (tile_cols, TC - 1))[side]
            return pad[(*index, u, slice(row0, row1), slice(at, at + 1))]

        rim_lane = iota((rows, LANES), 1)
        for side, row in ((0, first), (1, last)):
            ns0_send[side, 0:1] = across(tpad, (top,), slice(row, row + 1))
            ns0_send[side, 1:2] = across(kpad, (), slice(row, row + 1))
        for side in range(2):
            ew0_send[side] = jnp.where(
                rim_lane == 0, edge_column(tpad, (top,), side), edge_column(kpad, (), side)
            )

        pl.semaphore_wait(barrier, len(greeted))

        def rim_copies(ns_s, ns_r, ew_s, ew_r, ss, rs):
            copies = []
            for i in range(4):
                src, dst = (ns_s, ns_r) if i < 2 else (ew_s, ew_r)
                copies.append(
                    pltpu.make_async_remote_copy(
                        src_ref=src.at[i % 2],
                        dst_ref=dst.at[1 - i % 2],
                        send_sem=ss.at[i // 2],
                        recv_sem=rs.at[i // 2],
                        device_id=sides[i],
                        device_id_type=MESH,
                    )
                )
            return copies

        rims0 = rim_copies(ns0_send, ns0_recv, ew0_send, ew0_recv, rim0_ss, rim0_rs)
        for copy in rims0:
            copy.start()

        for load in loads[6:]:
            load.wait()
        small[0:k_blocks, 0:tiles] = map_v[...].astype(F32)
        small[k_blocks : 2 * k_blocks, 0:tiles] = weight_v[...]
        small[2 * k_blocks : 2 * k_blocks + 1, 0:tiles] = frame_v[...].astype(F32)
        columns_of = jnp.transpose(small[...])[0:tiles]
        weight = columns_of[:, k_blocks : 2 * k_blocks]
        code = columns_of[:, 0:k_blocks].astype(jnp.int32)
        plate = code >> ((tiles * n_gy).bit_length() - 1)
        far = ((plate ^ gx) >> 2) & 1
        dz = ((plate >> 3) - gx_z) & 3
        dy = (plate - gx) & 3
        block = far * PLANE + dy * RING + dz
        wish = ((code & (tiles - 1)) + 1).astype(F32)
        lane = iota((tiles, LANES), 1)
        lane_slot = iota((tiles, n_slots), 1)
        lower = jnp.where(iota((tiles, tiles), 0) > iota((tiles, tiles), 1), 1.0, 0.0)
        hits = [jnp.where(block[:, k : k + 1] == lane, 1.0, 0.0) for k in range(k_blocks)]
        before = jnp.dot(lower, jnp.concatenate(hits, axis=1), preferred_element_type=F32)
        base = jnp.zeros((1, LANES), F32)
        wanted = jnp.zeros((tiles, n_slots), F32)
        weights = [jnp.zeros((tiles, n_slots), F32) for _ in range(2)]
        ranks = []
        for k in range(k_blocks):
            earlier = before[:, k * LANES : (k + 1) * LANES] + base
            base = base + jnp.sum(hits[k], axis=0, keepdims=True)
            ranks.append(jnp.sum(hits[k] * earlier, axis=1, keepdims=True).astype(jnp.int32))
            here = block[:, k : k + 1] * CAP + ranks[k] == lane_slot
            wanted = wanted + jnp.where(here, wish[:, k : k + 1], 0.0)
        asked = jnp.sum(wanted, axis=0, keepdims=True)
        for g in range(groups):
            for f in range(2):
                at = f * half + g * LANES
                req_send[g, f : f + 1] = asked[:, at : at + LANES]

        for b in others:
            send(
                req_send.at[b // per_group],
                req_recv.at[b],
                req_ss.at[0],
                req_rs.at[0],
                along(b % RING, b // RING),
            ).start()
        for k in range(k_blocks):
            col = slice(k, k + 1)
            for h, (dense, slot) in enumerate(((dz, dy), (dy, dz))):
                at = (dense * LANES + far * (LANES // 2) + slot * CAP)[:, col] + ranks[k]
                weights[h] = weights[h] + jnp.where(at == lane_slot, weight[:, col], 0.0)
        for h in range(2):
            for d in range(RING):
                wsend[h, d] = weights[h][:, d * LANES : (d + 1) * LANES]
            wblk[h, 0] = weights[h][:, 0:LANES]
            for d in range(1, RING):
                send(
                    wsend.at[h, d], wblk.at[h, d], w_ss.at[0], w_rs.at[0], dense_peer(h, d)
                ).start()
        req_recv[0] = req_send[0]

        has_north = jnp.where(gx > 0, 1.0, 0.0)
        has_south = jnp.where(gx < n_gx - 1, 1.0, 0.0)
        has_west = jnp.where(gy > 0, 1.0, 0.0)
        has_east = jnp.where(gy < n_gy - 1, 1.0, 0.0)

        def column_rims(pad, index, source, lane_at):
            for side, has, at in ((0, has_west, 0), (1, has_east, tile_cols + 1)):
                value = source[side, :, lane_at : lane_at + 1] * has
                pad[(*index, at, slice(row0, row1))] = jnp.broadcast_to(value, (rows, LANES))

        wait_bytes(ns0_recv, rim0_rs.at[0])
        wait_bytes(ew0_recv, rim0_rs.at[1])
        above, below = slice(first - 1, first), slice(last + 1, last + 2)
        put_line(kpad, (), above, ns0_recv[0, 1:2] * has_north)
        put_line(kpad, (), below, ns0_recv[1, 1:2] * has_south)
        column_rims(kpad, (), ew0_recv, 1)
        put_line(tpad, (top,), above, ns0_recv[0, 0:1] * has_north)
        put_line(tpad, (top,), below, ns0_recv[1, 0:1] * has_south)
        column_rims(tpad, (top,), ew0_recv, 0)

        strip_lane = iota((TR, TC), 1)

        def around(pad, index, r):
            a, b = row0 + r * TR, row0 + (r + 1) * TR
            blocks = [pad[(*index, u, slice(a, b), slice(None))] for u in range(tile_cols + 2)]
            inside = blocks[1:-1]
            eastward = [pltpu.roll(x, TC - 1, 1) for x in inside] + blocks[-1:]
            westward = blocks[:1] + [pltpu.roll(x, 1, 1) for x in inside]
            e = [
                jnp.where(strip_lane == TC - 1, eastward[u + 1], eastward[u])
                for u in range(tile_cols)
            ]
            w = [
                jnp.where(strip_lane == 0, westward[u], westward[u + 1]) for u in range(tile_cols)
            ]
            return (
                jnp.concatenate(inside, axis=1),
                jnp.concatenate(e, axis=1),
                jnp.concatenate(w, axis=1),
                across(pad, index, slice(a - 1, b - 1)),
                across(pad, index, slice(a + 1, b + 1)),
            )

        for r in range(strips):
            kc, ke, kw, kn, ks = around(kpad, (), r)
            strip = slice(r * TR, (r + 1) * TR)
            faces = [0.5 * RATE_PLANE * (kc + other) for other in (ke, kw, kn, ks)]
            for i in range(4):
                coef[i, strip] = faces[i]
            tc, te, tw, tn, ts = around(tpad, (top,), r)
            under = across(tpad, (top - 1,), slice(row0 + r * TR, row0 + (r + 1) * TR))
            value = tc + RATE_VERTICAL * (under - tc)
            for face, other in zip(faces, (te, tw, tn, ts)):
                value = value + face * (other - tc)
            for u in range(tile_cols):
                tiles3[r * tile_cols + u] = value[:, u * TC : (u + 1) * TC]

        x_copies = []
        for i in range(2):
            for rr in range(TR // 2):
                x_send[i, :, rr * TC : (rr + 1) * TC] = tiles3[:, i * (TR // 2) + rr, :]
            copy = send(x_send.at[i], x_recv.at[i], x_ss.at[i], x_rs.at[i], partner)
            copy.start()
            x_copies.append(copy)

        wait_bytes(req_recv.at[1:PLANE], req_rs.at[0])
        group_lane = iota((per_group, LANES), 1) // CAP
        group_row = iota((per_group, LANES), 0)
        tile_row = iota((tiles, LANES), 0).astype(F32)
        def make_picks(f):
            picks = []
            for g in range(groups):
                block = req_recv[g * per_group : (g + 1) * per_group, f, :]
                line = jnp.sum(
                    jnp.where(group_lane == group_row, block, 0.0), axis=0, keepdims=True
                )
                picks.append(jnp.where(line - 1.0 == tile_row, 1.0, 0.0))
            pick = jnp.concatenate(picks, axis=1)
            onehot[:, f * half : (f + 1) * half] = pick
            turned = jnp.transpose(jnp.concatenate([pick, pick], axis=0)).astype(BF16)
            lhs1[f * half : (f + 1) * half] = turned

        make_picks(0)

        def plane_rows(ref, c, f, d):
            return ref.at[0, c // 2, f, d] if c % 2 == 0 else ref.at[1, c // 2, f, :, d]

        def near_rows(ref, h, d):
            return ref.at[0, :, 0, d] if h == 0 else ref.at[1, :, 0, :, d]

        slots1 = {}
        for d in range(1, RING):
            for c in range(n_chunks):
                slots1[c, 1, d] = send(
                    plane_rows(send1, c, 1, d),
                    recv1.at[c % 2, c // 2, :, 1, d],
                    s1_ss.at[0],
                    s1_rs.at[c],
                    slot_peer(c % 2, -d),
                )
            for h in range(2):
                slots1[h, 0, d] = send(
                    near_rows(send1, h, d),
                    recv1.at[h, :, :, 0, d],
                    s1_ss.at[0],
                    s1_rs.at[n_chunks + h],
                    slot_peer(h, -d),
                )

        def columns(c, count=1):
            return slice(c * wide, (c + count) * wide)

        def pack_tiles(f, pair, source):
            for i, piece in enumerate(two_parts(source)):
                rhs[i * tiles : (i + 1) * tiles, columns(pair, 2)] = piece
            for c in (pair, pair + 1):
                packed = jnp.dot(
                    lhs1[f * half : (f + 1) * half],
                    rhs[:, columns(c)],
                    preferred_element_type=F32,
                )
                send1[c % 2, c // 2, f] = packed.reshape(RING, RING, CAP, wide)
                if f == 1:
                    for d in FARTHEST_FIRST:
                        slots1[c, f, d].start()
                recv1[c % 2, c // 2, :, f, 0] = send1[c % 2, c // 2, f, 0] if c % 2 == 0 else send1[c % 2, c // 2, f, :, 0]

        for pair in (0, 2):
            pack_tiles(0, pair, x_send[pair // 2])
        for d in FARTHEST_FIRST:
            for h in range(2):
                slots1[h, 0, d].start()
        make_picks(1)

        wait_bytes(tpad.at[(*rest, *inside)], in_sem.at[2])
        wait_bytes(apad.at[(*all_layers, *inside)], in_sem.at[3])
        for side, row in ((0, first), (1, last)):
            for u in range(tile_cols):
                at = slice(u * TC, (u + 1) * TC)
                ns_send[side, 0:top, at] = tpad[0:top, u + 1, row, :]
                ns_send[side, layers : layers + top, at] = apad[0:top, u + 1, row, :]
        for side in range(2):
            packed = jnp.zeros((rows, LANES), F32)
            for l in range(top):
                packed = jnp.where(rim_lane == l, edge_column(tpad, (l,), side), packed)
                packed = jnp.where(
                    rim_lane == layers + l, edge_column(apad, (l,), side), packed
                )
            ew_send[side] = packed
        rims = rim_copies(ns_send, ns_recv, ew_send, ew_recv, rim_ss, rim_rs)
        for copy in rims:
            copy.start()

        wait_bytes(wblk.at[:, 1:RING], w_rs.at[0])
        for h in range(2):
            for d in range(RING):
                for i, piece in enumerate(two_parts(wblk[h, d])):
                    wcat[h, d, i * tiles : (i + 1) * tiles] = jnp.concatenate(
                        [piece, piece], axis=1
                    )

        x_copies[0].wait_recv()
        pack_tiles(1, 0, x_recv[0])

        for h in range(2):
            for d in range(RING):
                parts_of = jnp.concatenate(two_parts(wblk[h, d]), axis=0).astype(F32)
                turned = jnp.transpose(parts_of).astype(BF16)
                lhs2[h, d, :, 0 : 2 * tiles] = turned
                lhs2[h, d, :, 2 * tiles : 4 * tiles] = turned

        edge = jnp.zeros((rows, LANES), F32)
        apad[top, 0, row0:row1] = edge
        apad[top, tile_cols + 1, row0:row1] = edge
        put_line(apad, (top,), above, jnp.zeros((1, cols), F32))
        put_line(apad, (top,), below, jnp.zeros((1, cols), F32))

        wait_bytes(ns_recv, rim_rs.at[0])
        wait_bytes(ew_recv, rim_rs.at[1])
        for l in range(top):
            column_rims(tpad, (l,), ew_recv, l)
            column_rims(apad, (l,), ew_recv, layers + l)
        for side, has, at in ((0, has_north, first - 1), (1, has_south, last + 1)):
            for u in range(tile_cols):
                cut = slice(u * TC, (u + 1) * TC)
                tpad[0:top, u + 1, at, :] = ns_recv[side, 0:top, cut] * has
                apad[0:top, u + 1, at, :] = ns_recv[side, layers : layers + top, cut] * has

        loads[4].wait()
        loads[5].wait()
        frame = columns_of[:, 2 * k_blocks : 2 * k_blocks + 1].astype(jnp.int32)
        for c in range(n_chunks):
            seen = jnp.zeros((tiles, wide), F32)
            for f in range(frames):
                seen = jnp.where(frame == f, obs_v[f, :, columns(c)], seen)
            mis[c] = -seen

        x_copies[1].wait_recv()
        pack_tiles(1, 2, x_recv[1])

        def layer_step(l, r, total):
            strip = slice(r * TR, (r + 1) * TR)
            tc, *t_near = around(tpad, (l,), r)
            ac, *a_near = around(apad, (l,), r)
            flow = jnp.zeros_like(ac)
            for i in range(4):
                step = a_near[i] - ac
                flow = flow + coef[i, strip] * step
                total = total + (t_near[i] - tc) * step
            return ac + flow, ac, total

        def inner_layers(r):
            strip = slice(r * TR, (r + 1) * TR)
            inner = slice(row0 + r * TR, row0 + (r + 1) * TR)

            def body(l, total):
                value, ac, total = layer_step(l, r, total)
                over = across(apad, (l + 1,), inner)
                under = across(apad, (jnp.maximum(l - 1, 0),), inner)
                outv[l, strip] = value + RATE_VERTICAL * ((over - ac) + (under - ac))
                return total

            gacc[strip] = lax.fori_loop(0, top, body, jnp.zeros((TR, cols), F32))

        inner_layers(0)

        def weigh(c, d):
            both = jnp.dot(
                wcat[c % 2, d],
                jnp.concatenate(two_parts(recv1[c % 2, c // 2, d].reshape(LANES, wide)), axis=0),
                preferred_element_type=F32,
            )
            return both[0:tiles] + both[tiles : 2 * tiles]

        parts, spread = {}, {}
        for c in range(n_chunks):
            for d in range(1, RING):
                parts[c, d] = send(
                    part.at[c, d],
                    part_recv.at[c, d],
                    p_ss.at[0],
                    p_rs.at[c],
                    dense_peer(c % 2, -d),
                )
                spread[c, d] = send(
                    mis.at[c], mis_recv.at[c, d], m_ss.at[0], m_rs.at[c], dense_peer(c % 2, d)
                )
        for c in range(n_chunks):
            if c < 2:
                wait_bytes(recv1.at[c, :, 0 : RING - 1, 0], s1_rs.at[n_chunks + c])
            wait_bytes(recv1.at[c % 2, c // 2, 0 : RING - 1, 1], s1_rs.at[c])
            for d in FARTHEST_FIRST:
                part[c, d] = weigh(c, d)
                parts[c, d].start()
            mis[c] += weigh(c, 0)

        for c in range(n_chunks):
            wait_bytes(part_recv.at[c, 1:RING], p_rs.at[c])
            mis[c] += part_recv[c, 1] + (part_recv[c, 2] + part_recv[c, 3])
            for d in FARTHEST_FIRST:
                spread[c, d].start()
            misfit_out[:, columns(c)] = mis[c]
            if c % 2 == 1:
                inner_layers(1 + c // 2)

        slots2 = {}
        for d in range(1, RING):
            for c in range(n_chunks):
                slots2[c, 1, d] = send(
                    send2.at[c % 2, c // 2, :, 1, d],
                    plane_rows(recv2, c, 1, d),
                    s2_ss.at[0],
                    s2_rs.at[c],
                    slot_peer(c % 2, d),
                )
            for h in range(2):
                slots2[h, 0, d] = send(
                    send2.at[h, :, :, 0, d],
                    near_rows(recv2, h, d),
                    s2_ss.at[0],
                    s2_rs.at[n_chunks + h],
                    slot_peer(h, d),
                )
        for c in range(n_chunks):
            wait_bytes(mis_recv.at[c, 1:RING], m_rs.at[c])
            for d in range(RING):
                mh, ml = two_parts(mis_recv[c, d] if d else mis[c])
                packed = jnp.dot(
                    lhs2[c % 2, d],
                    jnp.concatenate([mh, mh, ml, ml], axis=0),
                    preferred_element_type=F32,
                )
                send2[c % 2, c // 2, d] = packed.reshape(2, RING, CAP, wide)
            for d in FARTHEST_FIRST:
                slots2[c, 1, d].start()
        for d in FARTHEST_FIRST:
            for h in range(2):
                slots2[h, 0, d].start()
        for c in range(n_chunks):
            for f in range(2):
                if c % 2 == 0:
                    recv2[c % 2, c // 2, f, 0] = send2[c % 2, c // 2, :, f, 0]
                else:
                    recv2[c % 2, c // 2, f, :, 0] = send2[c % 2, c // 2, :, f, 0]

        inner_layers(3)
        for like, sem in (
            (ns0_recv, rim0_ss.at[0]),
            (ew0_recv, rim0_ss.at[1]),
            (ns_recv, rim_ss.at[0]),
            (ew_recv, rim_ss.at[1]),
            (req_recv.at[1:PLANE], req_ss.at[0]),
            (wblk.at[:, 1:RING], w_ss.at[0]),
            (recv1.at[:, :, 0 : RING - 1], s1_ss.at[0]),
            (part.at[:, 1:RING], p_ss.at[0]),
            (part.at[:, 1:RING], m_ss.at[0]),
        ):
            wait_bytes(like, sem)
        for copy in x_copies:
            copy.wait_send()

        def gathered(c, f):
            if f == 1:
                wait_bytes(recv2.at[c % 2, c // 2, 1, 0 : RING - 1], s2_rs.at[c])
            elif c < 2:
                wait_bytes(recv2.at[c, :, 0, 0 : RING - 1], s2_rs.at[n_chunks + c])
            pick = onehot[:, f * half : (f + 1) * half].astype(BF16)
            return jnp.dot(
                jnp.concatenate([pick, pick], axis=1),
                jnp.concatenate(two_parts(recv2[c % 2, c // 2, f].reshape(half, wide)), axis=0),
                preferred_element_type=F32,
            )

        xa_copies = []
        for c in range(n_chunks):
            xa_send[c] = gathered(c, 1)
            copy = send(xa_send.at[c], xa_recv.at[c], x_ss.at[2 + c], x_rs.at[2 + c], partner)
            copy.start()
            xa_copies.append(copy)
            if c % 2 == 1:
                for r in range(3 + c, 5 + c):
                    inner_layers(r)
        sums = [gathered(c, 0) for c in range(n_chunks)]
        for copy in xa_copies:
            copy.wait_recv()
        added = jnp.concatenate([sums[c] + xa_recv[c] for c in range(n_chunks)], axis=1)
        for rr in range(TR):
            tiles3[:, rr, :] = added[:, rr * TC : (rr + 1) * TC]
        for r in range(strips):
            strip = slice(r * TR, (r + 1) * TR)
            inner = slice(row0 + r * TR, row0 + (r + 1) * TR)
            extra = jnp.concatenate(
                [tiles3[r * tile_cols + u] for u in range(tile_cols)], axis=1
            )
            put_line(apad, (top,), inner, across(apad, (top,), inner) + extra)
            outv[top - 1, strip] += RATE_VERTICAL * extra

        for side, row in ((0, first), (1, last)):
            ns2_send[side] = across(apad, (top,), slice(row, row + 1))
        for side in range(2):
            ew2_send[side] = jnp.broadcast_to(edge_column(apad, (top,), side), (rows, LANES))
        rims2 = rim_copies(ns2_send, ns2_recv, ew2_send, ew2_recv, rim2_ss, rim2_rs)
        for copy in rims2:
            copy.start()
        for r in range(strips):
            strip = slice(r * TR, (r + 1) * TR)
            inner = slice(row0 + r * TR, row0 + (r + 1) * TR)
            value, ac, total = layer_step(top, r, gacc[strip])
            under = across(apad, (top - 1,), inner)
            outv[top, strip] = value + RATE_VERTICAL * (under - ac)
            gradv[strip] = gin[strip] - (0.5 * RATE_PLANE) * total
        wait_bytes(recv2.at[:, :, :, 0 : RING - 1], s2_ss.at[0])
        for copy in xa_copies:
            copy.wait_send()

        wait_bytes(ns2_recv, rim2_rs.at[0])
        wait_bytes(ew2_recv, rim2_rs.at[1])
        for side, has, row, beyond in ((0, has_north, 0, first - 1), (1, has_south, rows - 1, last + 1)):
            at = slice(row, row + 1)
            rim = ns2_recv[side] * has
            slope = across(tpad, (top,), slice(beyond, beyond + 1)) - across(
                tpad, (top,), slice(row0 + row, row0 + row + 1)
            )
            outv[top, at] += coef[2 + side, at] * rim
            gradv[at] -= (0.5 * RATE_PLANE) * slope * rim
        for side, has, face, inside, beyond, edge_lane in (
            (0, has_west, 1, 1, 0, 0),
            (1, has_east, 0, tile_cols, tile_cols + 1, TC - 1),
        ):
            at = slice((inside - 1) * TC, inside * TC)
            rim = jnp.where(rim_lane == edge_lane, ew2_recv[side] * has, 0.0)
            slope = tpad[top, beyond, row0:row1] - tpad[top, inside, row0:row1]
            outv[top, :, at] += coef[face, :, at] * rim
            gradv[:, at] -= (0.5 * RATE_PLANE) * slope * rim

        wait_bytes(ns2_recv, rim2_ss.at[0])
        wait_bytes(ew2_recv, rim2_ss.at[1])

    dma = pltpu.SemaphoreType.DMA

    def vmem(*shape, dtype=F32):
        return pltpu.VMEM(shape, dtype)

    def pair(*shape):
        return [vmem(*shape), vmem(*shape)]

    tile = TR * TC
    scratch = [
        vmem(layers, tile_cols + 2, rows + 2 * TR, TC),
        vmem(layers, tile_cols + 2, rows + 2 * TR, TC),
        vmem(tile_cols + 2, rows + 2 * TR, TC),
        vmem(rows, cols),
        vmem(frames, tiles, tile),
        vmem(4, rows, cols),
        vmem(rows, cols),
        vmem(k_blocks, tiles, dtype=jnp.int32),
        vmem(k_blocks, tiles),
        vmem(1, tiles, dtype=jnp.int32),
        *pair(2, 2, cols),
        *pair(2, rows, LANES),
        *pair(2, 2 * layers, cols),
        *pair(2, rows, LANES),
        *pair(2, 1, cols),
        *pair(2, rows, LANES),
        vmem(2 * TR, LANES),
        vmem(groups, 8, LANES),
        vmem(PLANE, 8, LANES),
        vmem(tiles, TR, TC),
        vmem(tiles, n_slots),
        vmem(n_slots, 2 * tiles, dtype=BF16),
        vmem(2 * tiles, tile, dtype=BF16),
        *pair(2, RING, tiles, LANES),
        vmem(2, RING, 2 * tiles, 4 * tiles, dtype=BF16),
        vmem(2, RING, LANES, 4 * tiles, dtype=BF16),
        *pair(2, tiles, tile // 2),
        *pair(n_chunks, tiles, wide),
        vmem(2, n_chunks // 2, 2, RING, RING, CAP, wide),
        vmem(2, n_chunks // 2, RING, 2, RING, CAP, wide),
        *pair(n_chunks, RING, tiles, wide),
        vmem(n_chunks, tiles, wide),
        vmem(n_chunks, RING, tiles, wide),
        vmem(2, n_chunks // 2, RING, 2, RING, CAP, wide),
        vmem(2, n_chunks // 2, 2, RING, RING, CAP, wide),
        dma((9,)),
        *[dma((2,)) for _ in range(6)],
        dma((2 + n_chunks,)), dma((2 + n_chunks,)),
        dma((1,)), dma((1,)),
        dma((1,)), dma((1,)),
        dma((1,)), dma((2 + n_chunks,)),
        dma((1,)), dma((n_chunks,)),
        dma((1,)), dma((n_chunks,)),
        dma((1,)), dma((2 + n_chunks,)),
    ]
    in_hbm = pl.BlockSpec(memory_space=pltpu.HBM)
    in_vmem = pl.BlockSpec(memory_space=pltpu.VMEM)
    return pl.pallas_call(
        kernel,
        out_shape=(
            jax.ShapeDtypeStruct((tiles, tile), F32),
            jax.ShapeDtypeStruct((layers, rows, cols), F32),
            jax.ShapeDtypeStruct((rows, cols), F32),
        ),
        in_specs=[in_hbm] * 8,
        out_specs=[in_vmem] * 3,
        scratch_shapes=scratch,
        compiler_params=pltpu.CompilerParams(
            collective_id=0, has_side_effects=True, vmem_limit_bytes=48 * 1024 * 1024
        ),
    )


def write_out(results):
    count = len(results)
    layers = results[1].shape[0]

    def kernel(*refs):
        misfit, adjoint, grad, misfit_out, adjoint_out, grad_out, sems = refs
        pairs = [(misfit, misfit_out), (grad, grad_out)]
        pairs += [(adjoint.at[l], adjoint_out.at[l]) for l in range(layers)]
        copies = [
            pltpu.make_async_copy(src, dst, sems.at[i]) for i, (src, dst) in enumerate(pairs)
        ]
        for copy in copies:
            copy.start()
        for copy in copies:
            copy.wait()

    return pl.pallas_call(
        kernel,
        out_shape=tuple(jax.ShapeDtypeStruct(x.shape, x.dtype) for x in results),
        in_specs=[pl.BlockSpec(memory_space=pltpu.VMEM)] * count,
        out_specs=[pl.BlockSpec(memory_space=pl.ANY)] * count,
        scratch_shapes=[pltpu.SemaphoreType.DMA((layers + 2,))],
        compiler_params=pltpu.CompilerParams(vmem_limit_bytes=8 * 1024 * 1024),
    )(*results)


def solution(mesh):
    n_gx, n_gy = mesh.shape["gx"], mesh.shape["gy"]

    def local(temp, cond, adj, grad, obs, frame_index, source_map, source_weight):
        layers, rows, cols = temp.shape
        call = make_kernel(n_gx, n_gy, layers, rows, cols, obs.shape[0], source_map.shape[1])
        operands = (
            temp, cond, adj, grad, obs, frame_index[None, :], source_map.T, source_weight.T
        )
        results = call(*(pltpu.with_memory_space_constraint(x, pltpu.HBM) for x in operands))
        return write_out(results)

    placed = (
        P(None, "gx", "gy"),
        P("gx", "gy"),
        P(None, "gx", "gy"),
        P("gx", "gy"),
        P(None, ("gx", "gy"), None),
        P(("gx", "gy")),
        P(("gx", "gy"), None),
        P(("gx", "gy"), None),
    )
    return jax.shard_map(
        local,
        mesh=mesh,
        in_specs=placed,
        out_specs=(P(("gx", "gy"), None), P(None, "gx", "gy"), P("gx", "gy")),
        check_vma=False,
    )
```

```python
import jax
import jax.numpy as jnp
from jax import lax
from jax.experimental import pallas as pl
from jax.experimental.pallas import tpu as pltpu
from jax.sharding import PartitionSpec as P

TR = 8
TC = 128
CAP = 16
LANES = 128
RATE_PLANE = 0.2
RATE_VERTICAL = 0.08
MESH = pl.DeviceIdType.MESH
F32 = jnp.float32
BF16 = jnp.bfloat16


def iota(shape, dim):
    return lax.broadcasted_iota(jnp.int32, shape, dim)


def two_parts(x):
    hi = x.astype(BF16)
    lo = (x - hi.astype(F32)).astype(BF16)
    return hi, lo


RING = 4
PLANE = RING * RING
FARTHEST_FIRST = (2, 1, 3)


def make_kernel(n_gx, n_gy, layers, rows, cols, frames, k_blocks):
    tiles = (rows // TR) * (cols // TC)
    half = PLANE * CAP
    n_slots = 2 * half
    row0, row1 = TR, TR + rows
    strips = rows // TR
    tile_cols = cols // TC
    top = layers - 1
    per_group = LANES // CAP
    groups = PLANE // per_group
    others = range(1, PLANE)
    n_chunks = 4
    wide = cols // n_chunks

    def kernel(
        temp, cond, adj, grad, obs, frame_in, map_in, weight_in,
        misfit_out, outv, gradv,
        tpad, apad, kpad, gin, obs_v, coef, gacc, map_v, weight_v, frame_v,
        ns0_send, ns0_recv, ew0_send, ew0_recv,
        ns_send, ns_recv, ew_send, ew_recv,
        ns2_send, ns2_recv, ew2_send, ew2_recv,
        small, req_send, req_recv, tiles3, onehot, lhs1, rhs,
        wsend, wblk, wcat, lhs2,
        x_send, x_recv, xa_send, xa_recv,
        send1, recv1, part, part_recv, mis, mis_recv, send2, recv2,
        in_sem,
        rim0_ss, rim0_rs, rim_ss, rim_rs, rim2_ss, rim2_rs, x_ss, x_rs,
        req_ss, req_rs, w_ss, w_rs, s1_ss, s1_rs, p_ss, p_rs, m_ss, m_rs, s2_ss, s2_rs,
    ):
        gx = lax.axis_index("gx")
        gy = lax.axis_index("gy")
        gx_y = lax.rem(gx, RING)
        gx_x = lax.rem(gx // RING, 2)
        gx_z = gx // (2 * RING)
        north, south = lax.rem(gx + n_gx - 1, n_gx), lax.rem(gx + 1, n_gx)
        west, east = lax.rem(gy + n_gy - 1, n_gy), lax.rem(gy + 1, n_gy)
        sides = ({"gx": north}, {"gx": south}, {"gy": west}, {"gy": east})
        partner = {"gx": gx + RING - 2 * RING * gx_x}

        def along(dz, dy):
            z = lax.rem(gx_z + dz % RING, RING)
            y = lax.rem(gx_y + dy % RING, RING)
            return {"gx": z * (2 * RING) + gx_x * RING + y}

        def slot_peer(h, d):
            return along(0, d) if h == 0 else along(d, 0)

        def dense_peer(h, d):
            return along(d, 0) if h == 0 else along(0, d)

        def wait_bytes(like, sem):
            pltpu.make_async_copy(like, like, sem).wait()

        def send(src, dst, ss, rs, device):
            return pltpu.make_async_remote_copy(
                src_ref=src,
                dst_ref=dst,
                send_sem=ss,
                recv_sem=rs,
                device_id=device,
                device_id_type=MESH,
            )

        def block_loads(src, src_layers, pad, pad_layers, sem):
            return [
                pltpu.make_async_copy(
                    src.at[(*src_layers, slice(None), slice(u * TC, (u + 1) * TC))],
                    pad.at[(*pad_layers, u + 1, slice(row0, row1))],
                    in_sem.at[sem],
                )
                for u in range(tile_cols)
            ]

        both = (slice(top - 1, layers),)
        rest = (slice(0, top - 1),)
        all_layers = (slice(0, layers),)
        first_loads = block_loads(temp, both, tpad, both, 0) + block_loads(cond, (), kpad, (), 1)
        rim_loads = block_loads(temp, rest, tpad, rest, 2) + block_loads(
            adj, all_layers, apad, all_layers, 3
        )
        loads = [None] * 4 + [
            pltpu.make_async_copy(grad, gin, in_sem.at[4]),
            pltpu.make_async_copy(obs, obs_v, in_sem.at[5]),
            pltpu.make_async_copy(map_in, map_v, in_sem.at[6]),
            pltpu.make_async_copy(weight_in, weight_v, in_sem.at[7]),
            pltpu.make_async_copy(frame_in, frame_v, in_sem.at[8]),
        ]
        for load in first_loads:
            load.start()

        barrier = pltpu.get_barrier_semaphore()
        greeted = [along(b % RING, b // RING) for b in others] + [partner] + list(sides)
        for device in greeted:
            pl.semaphore_signal(barrier, inc=1, device_id=device, device_id_type=MESH)

        for load in loads[6:] + rim_loads + loads[4:6]:
            load.start()

        inside = (slice(1, tile_cols + 1), slice(row0, row1))
        wait_bytes(tpad.at[(*both, *inside)], in_sem.at[0])
        wait_bytes(kpad.at[inside], in_sem.at[1])
        first, last = row0, row1 - 1

        def across(pad, index, at):
            return jnp.concatenate(
                [pad[(*index, u, at, slice(None))] for u in range(1, tile_cols + 1)], axis=-1
            )

        def put_line(pad, index, at, value):
            for u in range(tile_cols):
                pad[(*index, u + 1, at, slice(None))] = value[..., u * TC : (u + 1) * TC]

        def edge_column(pad, index, side):
            u, at = ((1, 0), (tile_cols, TC - 1))[side]
            return pad[(*index, u, slice(row0, row1), slice(at, at + 1))]

        rim_lane = iota((rows, LANES), 1)
        for side, row in ((0, first), (1, last)):
            ns0_send[side, 0:1] = across(tpad, (top,), slice(row, row + 1))
            ns0_send[side, 1:2] = across(kpad, (), slice(row, row + 1))
        for side in range(2):
            ew0_send[side] = jnp.where(
                rim_lane == 0, edge_column(tpad, (top,), side), edge_column(kpad, (), side)
            )

        pl.semaphore_wait(barrier, len(greeted))

        def rim_copies(ns_s, ns_r, ew_s, ew_r, ss, rs):
            copies = []
            for i in range(4):
                src, dst = (ns_s, ns_r) if i < 2 else (ew_s, ew_r)
                copies.append(
                    pltpu.make_async_remote_copy(
                        src_ref=src.at[i % 2],
                        dst_ref=dst.at[1 - i % 2],
                        send_sem=ss.at[i // 2],
                        recv_sem=rs.at[i // 2],
                        device_id=sides[i],
                        device_id_type=MESH,
                    )
                )
            return copies

        rims0 = rim_copies(ns0_send, ns0_recv, ew0_send, ew0_recv, rim0_ss, rim0_rs)
        for copy in rims0:
            copy.start()

        for load in loads[6:]:
            load.wait()
        small[0:k_blocks, 0:tiles] = map_v[...].astype(F32)
        small[k_blocks : 2 * k_blocks, 0:tiles] = weight_v[...]
        small[2 * k_blocks : 2 * k_blocks + 1, 0:tiles] = frame_v[...].astype(F32)
        columns_of = jnp.transpose(small[...])[0:tiles]
        weight = columns_of[:, k_blocks : 2 * k_blocks]
        code = columns_of[:, 0:k_blocks].astype(jnp.int32)
        plate = code >> ((tiles * n_gy).bit_length() - 1)
        far = ((plate ^ gx) >> 2) & 1
        dz = ((plate >> 3) - gx_z) & 3
        dy = (plate - gx) & 3
        block = far * PLANE + dy * RING + dz
        wish = ((code & (tiles - 1)) + 1).astype(F32)
        lane = iota((tiles, LANES), 1)
        lane_slot = iota((tiles, n_slots), 1)
        lower = jnp.where(iota((tiles, tiles), 0) > iota((tiles, tiles), 1), 1.0, 0.0)
        hits = [jnp.where(block[:, k : k + 1] == lane, 1.0, 0.0) for k in range(k_blocks)]
        before = jnp.dot(lower, jnp.concatenate(hits, axis=1), preferred_element_type=F32)
        base = jnp.zeros((1, LANES), F32)
        wanted = jnp.zeros((tiles, n_slots), F32)
        weights = [jnp.zeros((tiles, n_slots), F32) for _ in range(2)]
        ranks = []
        for k in range(k_blocks):
            earlier = before[:, k * LANES : (k + 1) * LANES] + base
            base = base + jnp.sum(hits[k], axis=0, keepdims=True)
            ranks.append(jnp.sum(hits[k] * earlier, axis=1, keepdims=True).astype(jnp.int32))
            here = block[:, k : k + 1] * CAP + ranks[k] == lane_slot
            wanted = wanted + jnp.where(here, wish[:, k : k + 1], 0.0)
        asked = jnp.sum(wanted, axis=0, keepdims=True)
        for g in range(groups):
            for f in range(2):
                at = f * half + g * LANES
                req_send[g, f : f + 1] = asked[:, at : at + LANES]

        for b in others:
            send(
                req_send.at[b // per_group],
                req_recv.at[b],
                req_ss.at[0],
                req_rs.at[0],
                along(b % RING, b // RING),
            ).start()
        for k in range(k_blocks):
            col = slice(k, k + 1)
            for h, (dense, slot) in enumerate(((dz, dy), (dy, dz))):
                at = (dense * LANES + far * (LANES // 2) + slot * CAP)[:, col] + ranks[k]
                weights[h] = weights[h] + jnp.where(at == lane_slot, weight[:, col], 0.0)
        for h in range(2):
            for d in range(RING):
                wsend[h, d] = weights[h][:, d * LANES : (d + 1) * LANES]
            wblk[h, 0] = weights[h][:, 0:LANES]
            for d in range(1, RING):
                send(
                    wsend.at[h, d], wblk.at[h, d], w_ss.at[0], w_rs.at[0], dense_peer(h, d)
                ).start()
        req_recv[0] = req_send[0]

        has_north = jnp.where(gx > 0, 1.0, 0.0)
        has_south = jnp.where(gx < n_gx - 1, 1.0, 0.0)
        has_west = jnp.where(gy > 0, 1.0, 0.0)
        has_east = jnp.where(gy < n_gy - 1, 1.0, 0.0)

        def column_rims(pad, index, source, lane_at):
            for side, has, at in ((0, has_west, 0), (1, has_east, tile_cols + 1)):
                value = source[side, :, lane_at : lane_at + 1] * has
                pad[(*index, at, slice(row0, row1))] = jnp.broadcast_to(value, (rows, LANES))

        wait_bytes(ns0_recv, rim0_rs.at[0])
        wait_bytes(ew0_recv, rim0_rs.at[1])
        above, below = slice(first - 1, first), slice(last + 1, last + 2)
        put_line(kpad, (), above, ns0_recv[0, 1:2] * has_north)
        put_line(kpad, (), below, ns0_recv[1, 1:2] * has_south)
        column_rims(kpad, (), ew0_recv, 1)
        put_line(tpad, (top,), above, ns0_recv[0, 0:1] * has_north)
        put_line(tpad, (top,), below, ns0_recv[1, 0:1] * has_south)
        column_rims(tpad, (top,), ew0_recv, 0)

        strip_lane = iota((TR, TC), 1)

        def around(pad, index, r):
            a, b = row0 + r * TR, row0 + (r + 1) * TR
            blocks = [pad[(*index, u, slice(a, b), slice(None))] for u in range(tile_cols + 2)]
            inside = blocks[1:-1]
            eastward = [pltpu.roll(x, TC - 1, 1) for x in inside] + blocks[-1:]
            westward = blocks[:1] + [pltpu.roll(x, 1, 1) for x in inside]
            e = [
                jnp.where(strip_lane == TC - 1, eastward[u + 1], eastward[u])
                for u in range(tile_cols)
            ]
            w = [
                jnp.where(strip_lane == 0, westward[u], westward[u + 1]) for u in range(tile_cols)
            ]
            return (
                jnp.concatenate(inside, axis=1),
                jnp.concatenate(e, axis=1),
                jnp.concatenate(w, axis=1),
                across(pad, index, slice(a - 1, b - 1)),
                across(pad, index, slice(a + 1, b + 1)),
            )

        for r in range(strips):
            kc, ke, kw, kn, ks = around(kpad, (), r)
            strip = slice(r * TR, (r + 1) * TR)
            faces = [0.5 * RATE_PLANE * (kc + other) for other in (ke, kw, kn, ks)]
            for i in range(4):
                coef[i, strip] = faces[i]
            tc, te, tw, tn, ts = around(tpad, (top,), r)
            under = across(tpad, (top - 1,), slice(row0 + r * TR, row0 + (r + 1) * TR))
            value = tc + RATE_VERTICAL * (under - tc)
            for face, other in zip(faces, (te, tw, tn, ts)):
                value = value + face * (other - tc)
            for u in range(tile_cols):
                tiles3[r * tile_cols + u] = value[:, u * TC : (u + 1) * TC]

        x_copies = []
        for i in range(2):
            for rr in range(TR // 2):
                x_send[i, :, rr * TC : (rr + 1) * TC] = tiles3[:, i * (TR // 2) + rr, :]
            copy = send(x_send.at[i], x_recv.at[i], x_ss.at[i], x_rs.at[i], partner)
            copy.start()
            x_copies.append(copy)

        wait_bytes(req_recv.at[1:PLANE], req_rs.at[0])
        group_lane = iota((per_group, LANES), 1) // CAP
        group_row = iota((per_group, LANES), 0)
        tile_row = iota((tiles, LANES), 0).astype(F32)
        def make_picks(f):
            picks = []
            for g in range(groups):
                block = req_recv[g * per_group : (g + 1) * per_group, f, :]
                line = jnp.sum(
                    jnp.where(group_lane == group_row, block, 0.0), axis=0, keepdims=True
                )
                picks.append(jnp.where(line - 1.0 == tile_row, 1.0, 0.0))
            pick = jnp.concatenate(picks, axis=1)
            onehot[:, f * half : (f + 1) * half] = pick
            turned = jnp.transpose(jnp.concatenate([pick, pick], axis=0)).astype(BF16)
            lhs1[f * half : (f + 1) * half] = turned

        make_picks(0)

        def plane_rows(ref, c, f, d):
            return ref.at[0, c // 2, f, d] if c % 2 == 0 else ref.at[1, c // 2, f, :, d]

        def near_rows(ref, h, d):
            return ref.at[0, :, 0, d] if h == 0 else ref.at[1, :, 0, :, d]

        slots1 = {}
        for d in range(1, RING):
            for c in range(n_chunks):
                slots1[c, 1, d] = send(
                    plane_rows(send1, c, 1, d),
                    recv1.at[c % 2, c // 2, :, 1, d],
                    s1_ss.at[0],
                    s1_rs.at[c],
                    slot_peer(c % 2, -d),
                )
            for h in range(2):
                slots1[h, 0, d] = send(
                    near_rows(send1, h, d),
                    recv1.at[h, :, :, 0, d],
                    s1_ss.at[0],
                    s1_rs.at[n_chunks + h],
                    slot_peer(h, -d),
                )

        def columns(c, count=1):
            return slice(c * wide, (c + count) * wide)

        def pack_tiles(f, pair, source):
            for i, piece in enumerate(two_parts(source)):
                rhs[i * tiles : (i + 1) * tiles, columns(pair, 2)] = piece
            for c in (pair, pair + 1):
                packed = jnp.dot(
                    lhs1[f * half : (f + 1) * half],
                    rhs[:, columns(c)],
                    preferred_element_type=F32,
                )
                send1[c % 2, c // 2, f] = packed.reshape(RING, RING, CAP, wide)
                if f == 1:
                    for d in FARTHEST_FIRST:
                        slots1[c, f, d].start()
                recv1[c % 2, c // 2, :, f, 0] = send1[c % 2, c // 2, f, 0] if c % 2 == 0 else send1[c % 2, c // 2, f, :, 0]

        for pair in (0, 2):
            pack_tiles(0, pair, x_send[pair // 2])
        for d in FARTHEST_FIRST:
            for h in range(2):
                slots1[h, 0, d].start()
        make_picks(1)

        wait_bytes(tpad.at[(*rest, *inside)], in_sem.at[2])
        wait_bytes(apad.at[(*all_layers, *inside)], in_sem.at[3])
        for side, row in ((0, first), (1, last)):
            for u in range(tile_cols):
                at = slice(u * TC, (u + 1) * TC)
                ns_send[side, 0:top, at] = tpad[0:top, u + 1, row, :]
                ns_send[side, layers : layers + top, at] = apad[0:top, u + 1, row, :]
        for side in range(2):
            packed = jnp.zeros((rows, LANES), F32)
            for l in range(top):
                packed = jnp.where(rim_lane == l, edge_column(tpad, (l,), side), packed)
                packed = jnp.where(
                    rim_lane == layers + l, edge_column(apad, (l,), side), packed
                )
            ew_send[side] = packed
        rims = rim_copies(ns_send, ns_recv, ew_send, ew_recv, rim_ss, rim_rs)
        for copy in rims:
            copy.start()

        wait_bytes(wblk.at[:, 1:RING], w_rs.at[0])
        for h in range(2):
            for d in range(RING):
                for i, piece in enumerate(two_parts(wblk[h, d])):
                    wcat[h, d, i * tiles : (i + 1) * tiles] = jnp.concatenate(
                        [piece, piece], axis=1
                    )

        for pair in (0, 2):
            x_copies[pair // 2].wait_recv()
            pack_tiles(1, pair, x_recv[pair // 2])

        for h in range(2):
            for d in range(RING):
                parts_of = jnp.concatenate(two_parts(wblk[h, d]), axis=0).astype(F32)
                turned = jnp.transpose(parts_of).astype(BF16)
                lhs2[h, d, :, 0 : 2 * tiles] = turned
                lhs2[h, d, :, 2 * tiles : 4 * tiles] = turned

        edge = jnp.zeros((rows, LANES), F32)
        apad[top, 0, row0:row1] = edge
        apad[top, tile_cols + 1, row0:row1] = edge
        put_line(apad, (top,), above, jnp.zeros((1, cols), F32))
        put_line(apad, (top,), below, jnp.zeros((1, cols), F32))

        wait_bytes(ns_recv, rim_rs.at[0])
        wait_bytes(ew_recv, rim_rs.at[1])
        for l in range(top):
            column_rims(tpad, (l,), ew_recv, l)
            column_rims(apad, (l,), ew_recv, layers + l)
        for side, has, at in ((0, has_north, first - 1), (1, has_south, last + 1)):
            for u in range(tile_cols):
                cut = slice(u * TC, (u + 1) * TC)
                tpad[0:top, u + 1, at, :] = ns_recv[side, 0:top, cut] * has
                apad[0:top, u + 1, at, :] = ns_recv[side, layers : layers + top, cut] * has

        def layer_step(l, r, total):
            strip = slice(r * TR, (r + 1) * TR)
            tc, *t_near = around(tpad, (l,), r)
            ac, *a_near = around(apad, (l,), r)
            flow = jnp.zeros_like(ac)
            for i in range(4):
                step = a_near[i] - ac
                flow = flow + coef[i, strip] * step
                total = total + (t_near[i] - tc) * step
            return ac + flow, ac, total

        def inner_layers(r):
            strip = slice(r * TR, (r + 1) * TR)
            inner = slice(row0 + r * TR, row0 + (r + 1) * TR)

            def body(l, total):
                value, ac, total = layer_step(l, r, total)
                over = across(apad, (l + 1,), inner)
                under = across(apad, (jnp.maximum(l - 1, 0),), inner)
                outv[l, strip] = value + RATE_VERTICAL * ((over - ac) + (under - ac))
                return total

            gacc[strip] = lax.fori_loop(0, top, body, jnp.zeros((TR, cols), F32))

        for r in range(0, 4):
            inner_layers(r)

        loads[4].wait()
        loads[5].wait()
        frame = columns_of[:, 2 * k_blocks : 2 * k_blocks + 1].astype(jnp.int32)
        for c in range(n_chunks):
            seen = jnp.zeros((tiles, wide), F32)
            for f in range(frames):
                seen = jnp.where(frame == f, obs_v[f, :, columns(c)], seen)
            mis[c] = -seen

        def weigh(c, d):
            both = jnp.dot(
                wcat[c % 2, d],
                jnp.concatenate(two_parts(recv1[c % 2, c // 2, d].reshape(LANES, wide)), axis=0),
                preferred_element_type=F32,
            )
            return both[0:tiles] + both[tiles : 2 * tiles]

        parts, spread = {}, {}
        for c in range(n_chunks):
            for d in range(1, RING):
                parts[c, d] = send(
                    part.at[c, d],
                    part_recv.at[c, d],
                    p_ss.at[0],
                    p_rs.at[c],
                    dense_peer(c % 2, -d),
                )
                spread[c, d] = send(
                    mis.at[c], mis_recv.at[c, d], m_ss.at[0], m_rs.at[c], dense_peer(c % 2, d)
                )
        for c in range(n_chunks):
            if c < 2:
                wait_bytes(recv1.at[c, :, 0 : RING - 1, 0], s1_rs.at[n_chunks + c])
            wait_bytes(recv1.at[c % 2, c // 2, 0 : RING - 1, 1], s1_rs.at[c])
            for d in FARTHEST_FIRST:
                part[c, d] = weigh(c, d)
                parts[c, d].start()
            mis[c] += weigh(c, 0)

        inner_layers(4)

        for c in range(n_chunks):
            wait_bytes(part_recv.at[c, 1:RING], p_rs.at[c])
            mis[c] += part_recv[c, 1] + (part_recv[c, 2] + part_recv[c, 3])
            for d in FARTHEST_FIRST:
                spread[c, d].start()
            misfit_out[:, columns(c)] = mis[c]

        inner_layers(5)

        slots2 = {}
        for d in range(1, RING):
            for c in range(n_chunks):
                slots2[c, 1, d] = send(
                    send2.at[c % 2, c // 2, :, 1, d],
                    plane_rows(recv2, c, 1, d),
                    s2_ss.at[0],
                    s2_rs.at[c],
                    slot_peer(c % 2, d),
                )
            for h in range(2):
                slots2[h, 0, d] = send(
                    send2.at[h, :, :, 0, d],
                    near_rows(recv2, h, d),
                    s2_ss.at[0],
                    s2_rs.at[n_chunks + h],
                    slot_peer(h, d),
                )
        for c in range(n_chunks):
            wait_bytes(mis_recv.at[c, 1:RING], m_rs.at[c])
            for d in range(RING):
                mh, ml = two_parts(mis_recv[c, d] if d else mis[c])
                packed = jnp.dot(
                    lhs2[c % 2, d],
                    jnp.concatenate([mh, mh, ml, ml], axis=0),
                    preferred_element_type=F32,
                )
                send2[c % 2, c // 2, d] = packed.reshape(2, RING, CAP, wide)
            for d in FARTHEST_FIRST:
                slots2[c, 1, d].start()
        for d in FARTHEST_FIRST:
            for h in range(2):
                slots2[h, 0, d].start()
        for c in range(n_chunks):
            for f in range(2):
                if c % 2 == 0:
                    recv2[c % 2, c // 2, f, 0] = send2[c % 2, c // 2, :, f, 0]
                else:
                    recv2[c % 2, c // 2, f, :, 0] = send2[c % 2, c // 2, :, f, 0]

        for r in range(6, strips):
            inner_layers(r)
        for like, sem in (
            (ns0_recv, rim0_ss.at[0]),
            (ew0_recv, rim0_ss.at[1]),
            (ns_recv, rim_ss.at[0]),
            (ew_recv, rim_ss.at[1]),
            (req_recv.at[1:PLANE], req_ss.at[0]),
            (wblk.at[:, 1:RING], w_ss.at[0]),
            (recv1.at[:, :, 0 : RING - 1], s1_ss.at[0]),
            (part.at[:, 1:RING], p_ss.at[0]),
            (part.at[:, 1:RING], m_ss.at[0]),
        ):
            wait_bytes(like, sem)
        for copy in x_copies:
            copy.wait_send()

        def gathered(c, f):
            if f == 1:
                wait_bytes(recv2.at[c % 2, c // 2, 1, 0 : RING - 1], s2_rs.at[c])
            elif c < 2:
                wait_bytes(recv2.at[c, :, 0, 0 : RING - 1], s2_rs.at[n_chunks + c])
            pick = onehot[:, f * half : (f + 1) * half].astype(BF16)
            return jnp.dot(
                jnp.concatenate([pick, pick], axis=1),
                jnp.concatenate(two_parts(recv2[c % 2, c // 2, f].reshape(half, wide)), axis=0),
                preferred_element_type=F32,
            )

        xa_copies = []
        for c in range(n_chunks):
            xa_send[c] = gathered(c, 1)
            copy = send(xa_send.at[c], xa_recv.at[c], x_ss.at[2 + c], x_rs.at[2 + c], partner)
            copy.start()
            xa_copies.append(copy)
        sums = [gathered(c, 0) for c in range(n_chunks)]
        for copy in xa_copies:
            copy.wait_recv()
        added = jnp.concatenate([sums[c] + xa_recv[c] for c in range(n_chunks)], axis=1)
        for rr in range(TR):
            tiles3[:, rr, :] = added[:, rr * TC : (rr + 1) * TC]
        for r in range(strips):
            strip = slice(r * TR, (r + 1) * TR)
            inner = slice(row0 + r * TR, row0 + (r + 1) * TR)
            extra = jnp.concatenate(
                [tiles3[r * tile_cols + u] for u in range(tile_cols)], axis=1
            )
            put_line(apad, (top,), inner, across(apad, (top,), inner) + extra)
            outv[top - 1, strip] += RATE_VERTICAL * extra

        for side, row in ((0, first), (1, last)):
            ns2_send[side] = across(apad, (top,), slice(row, row + 1))
        for side in range(2):
            ew2_send[side] = jnp.broadcast_to(edge_column(apad, (top,), side), (rows, LANES))
        rims2 = rim_copies(ns2_send, ns2_recv, ew2_send, ew2_recv, rim2_ss, rim2_rs)
        for copy in rims2:
            copy.start()
        for r in range(strips):
            strip = slice(r * TR, (r + 1) * TR)
            inner = slice(row0 + r * TR, row0 + (r + 1) * TR)
            value, ac, total = layer_step(top, r, gacc[strip])
            under = across(apad, (top - 1,), inner)
            outv[top, strip] = value + RATE_VERTICAL * (under - ac)
            gradv[strip] = gin[strip] - (0.5 * RATE_PLANE) * total
        wait_bytes(recv2.at[:, :, :, 0 : RING - 1], s2_ss.at[0])
        for copy in xa_copies:
            copy.wait_send()

        wait_bytes(ns2_recv, rim2_rs.at[0])
        wait_bytes(ew2_recv, rim2_rs.at[1])
        for side, has, row, beyond in ((0, has_north, 0, first - 1), (1, has_south, rows - 1, last + 1)):
            at = slice(row, row + 1)
            rim = ns2_recv[side] * has
            slope = across(tpad, (top,), slice(beyond, beyond + 1)) - across(
                tpad, (top,), slice(row0 + row, row0 + row + 1)
            )
            outv[top, at] += coef[2 + side, at] * rim
            gradv[at] -= (0.5 * RATE_PLANE) * slope * rim
        for side, has, face, inside, beyond, edge_lane in (
            (0, has_west, 1, 1, 0, 0),
            (1, has_east, 0, tile_cols, tile_cols + 1, TC - 1),
        ):
            at = slice((inside - 1) * TC, inside * TC)
            rim = jnp.where(rim_lane == edge_lane, ew2_recv[side] * has, 0.0)
            slope = tpad[top, beyond, row0:row1] - tpad[top, inside, row0:row1]
            outv[top, :, at] += coef[face, :, at] * rim
            gradv[:, at] -= (0.5 * RATE_PLANE) * slope * rim

        wait_bytes(ns2_recv, rim2_ss.at[0])
        wait_bytes(ew2_recv, rim2_ss.at[1])

    dma = pltpu.SemaphoreType.DMA

    def vmem(*shape, dtype=F32):
        return pltpu.VMEM(shape, dtype)

    def pair(*shape):
        return [vmem(*shape), vmem(*shape)]

    tile = TR * TC
    scratch = [
        vmem(layers, tile_cols + 2, rows + 2 * TR, TC),
        vmem(layers, tile_cols + 2, rows + 2 * TR, TC),
        vmem(tile_cols + 2, rows + 2 * TR, TC),
        vmem(rows, cols),
        vmem(frames, tiles, tile),
        vmem(4, rows, cols),
        vmem(rows, cols),
        vmem(k_blocks, tiles, dtype=jnp.int32),
        vmem(k_blocks, tiles),
        vmem(1, tiles, dtype=jnp.int32),
        *pair(2, 2, cols),
        *pair(2, rows, LANES),
        *pair(2, 2 * layers, cols),
        *pair(2, rows, LANES),
        *pair(2, 1, cols),
        *pair(2, rows, LANES),
        vmem(2 * TR, LANES),
        vmem(groups, 8, LANES),
        vmem(PLANE, 8, LANES),
        vmem(tiles, TR, TC),
        vmem(tiles, n_slots),
        vmem(n_slots, 2 * tiles, dtype=BF16),
        vmem(2 * tiles, tile, dtype=BF16),
        *pair(2, RING, tiles, LANES),
        vmem(2, RING, 2 * tiles, 4 * tiles, dtype=BF16),
        vmem(2, RING, LANES, 4 * tiles, dtype=BF16),
        *pair(2, tiles, tile // 2),
        *pair(n_chunks, tiles, wide),
        vmem(2, n_chunks // 2, 2, RING, RING, CAP, wide),
        vmem(2, n_chunks // 2, RING, 2, RING, CAP, wide),
        *pair(n_chunks, RING, tiles, wide),
        vmem(n_chunks, tiles, wide),
        vmem(n_chunks, RING, tiles, wide),
        vmem(2, n_chunks // 2, RING, 2, RING, CAP, wide),
        vmem(2, n_chunks // 2, 2, RING, RING, CAP, wide),
        dma((9,)),
        *[dma((2,)) for _ in range(6)],
        dma((2 + n_chunks,)), dma((2 + n_chunks,)),
        dma((1,)), dma((1,)),
        dma((1,)), dma((1,)),
        dma((1,)), dma((2 + n_chunks,)),
        dma((1,)), dma((n_chunks,)),
        dma((1,)), dma((n_chunks,)),
        dma((1,)), dma((2 + n_chunks,)),
    ]
    in_hbm = pl.BlockSpec(memory_space=pltpu.HBM)
    in_vmem = pl.BlockSpec(memory_space=pltpu.VMEM)
    return pl.pallas_call(
        kernel,
        out_shape=(
            jax.ShapeDtypeStruct((tiles, tile), F32),
            jax.ShapeDtypeStruct((layers, rows, cols), F32),
            jax.ShapeDtypeStruct((rows, cols), F32),
        ),
        in_specs=[in_hbm] * 8,
        out_specs=[in_vmem] * 3,
        scratch_shapes=scratch,
        compiler_params=pltpu.CompilerParams(
            collective_id=0, has_side_effects=True, vmem_limit_bytes=48 * 1024 * 1024
        ),
    )


def write_out(results):
    count = len(results)

    def kernel(*refs):
        copies = [
            pltpu.make_async_copy(refs[i], refs[count + i], refs[-1].at[i]) for i in range(count)
        ]
        for copy in copies:
            copy.start()
        for copy in copies:
            copy.wait()

    return pl.pallas_call(
        kernel,
        out_shape=tuple(jax.ShapeDtypeStruct(x.shape, x.dtype) for x in results),
        in_specs=[pl.BlockSpec(memory_space=pltpu.VMEM)] * count,
        out_specs=[pl.BlockSpec(memory_space=pl.ANY)] * count,
        scratch_shapes=[pltpu.SemaphoreType.DMA((count,))],
        compiler_params=pltpu.CompilerParams(vmem_limit_bytes=8 * 1024 * 1024),
    )(*results)


def solution(mesh):
    n_gx, n_gy = mesh.shape["gx"], mesh.shape["gy"]

    def local(temp, cond, adj, grad, obs, frame_index, source_map, source_weight):
        layers, rows, cols = temp.shape
        call = make_kernel(n_gx, n_gy, layers, rows, cols, obs.shape[0], source_map.shape[1])
        operands = (
            temp, cond, adj, grad, obs, frame_index[None, :], source_map.T, source_weight.T
        )
        results = call(*(pltpu.with_memory_space_constraint(x, pltpu.HBM) for x in operands))
        return write_out(results)

    placed = (
        P(None, "gx", "gy"),
        P("gx", "gy"),
        P(None, "gx", "gy"),
        P("gx", "gy"),
        P(None, ("gx", "gy"), None),
        P(("gx", "gy")),
        P(("gx", "gy"), None),
        P(("gx", "gy"), None),
    )
    return jax.shard_map(
        local,
        mesh=mesh,
        in_specs=placed,
        out_specs=(P(("gx", "gy"), None), P(None, "gx", "gy"), P("gx", "gy")),
        check_vma=False,
    )
```

```python
import jax
import jax.numpy as jnp
from jax import lax
from jax.experimental import pallas as pl
from jax.experimental.pallas import tpu as pltpu
from jax.sharding import PartitionSpec as P

TR = 8
TC = 128
CAP = 16
LANES = 128
RATE_PLANE = 0.2
RATE_VERTICAL = 0.08
MESH = pl.DeviceIdType.MESH
F32 = jnp.float32
BF16 = jnp.bfloat16


def iota(shape, dim):
    return lax.broadcasted_iota(jnp.int32, shape, dim)


def two_parts(x):
    hi = x.astype(BF16)
    lo = (x - hi.astype(F32)).astype(BF16)
    return hi, lo


RING = 4
PLANE = RING * RING
FARTHEST_FIRST = (2, 1, 3)


def make_kernel(n_gx, n_gy, layers, rows, cols, frames, k_blocks):
    tiles = (rows // TR) * (cols // TC)
    half = PLANE * CAP
    n_slots = 2 * half
    row0, row1 = TR, TR + rows
    strips = rows // TR
    tile_cols = cols // TC
    top = layers - 1
    per_group = LANES // CAP
    groups = PLANE // per_group
    others = range(1, PLANE)
    n_chunks = 4
    wide = cols // n_chunks

    def kernel(
        temp, cond, adj, grad, obs, frame_in, map_in, weight_in,
        misfit_out, outv, gradv,
        tpad, apad, kpad, gin, obs_v, coef, gacc, map_v, weight_v, frame_v,
        ns0_send, ns0_recv, ew0_send, ew0_recv,
        ns_send, ns_recv, ew_send, ew_recv,
        ns2_send, ns2_recv, ew2_send, ew2_recv,
        small, req_send, req_recv, tiles3, onehot, lhs1, rhs,
        wsend, wblk, wcol, wcat, lhs2,
        x_send, x_recv, xa_send, xa_recv,
        send1, recv1, part, part_recv, mis, mis_recv, send2, recv2,
        in_sem,
        rim0_ss, rim0_rs, rim_ss, rim_rs, rim2_ss, rim2_rs, x_ss, x_rs,
        req_ss, req_rs, w_ss, w_rs, s1_ss, s1_rs, p_ss, p_rs, m_ss, m_rs, s2_ss, s2_rs,
    ):
        gx = lax.axis_index("gx")
        gy = lax.axis_index("gy")
        gx_y = lax.rem(gx, RING)
        gx_x = lax.rem(gx // RING, 2)
        gx_z = gx // (2 * RING)
        north, south = lax.rem(gx + n_gx - 1, n_gx), lax.rem(gx + 1, n_gx)
        west, east = lax.rem(gy + n_gy - 1, n_gy), lax.rem(gy + 1, n_gy)
        sides = ({"gx": north}, {"gx": south}, {"gy": west}, {"gy": east})
        partner = {"gx": gx + RING - 2 * RING * gx_x}

        def along(dz, dy):
            z = lax.rem(gx_z + dz % RING, RING)
            y = lax.rem(gx_y + dy % RING, RING)
            return {"gx": z * (2 * RING) + gx_x * RING + y}

        def slot_peer(h, d):
            return along(0, d) if h == 0 else along(d, 0)

        def dense_peer(h, d):
            return along(d, 0) if h == 0 else along(0, d)

        def wait_bytes(like, sem):
            pltpu.make_async_copy(like, like, sem).wait()

        def send(src, dst, ss, rs, device):
            return pltpu.make_async_remote_copy(
                src_ref=src,
                dst_ref=dst,
                send_sem=ss,
                recv_sem=rs,
                device_id=device,
                device_id_type=MESH,
            )

        def block_loads(src, src_layers, pad, pad_layers, sem):
            return [
                pltpu.make_async_copy(
                    src.at[(*src_layers, slice(None), slice(u * TC, (u + 1) * TC))],
                    pad.at[(*pad_layers, u + 1, slice(row0, row1))],
                    in_sem.at[sem],
                )
                for u in range(tile_cols)
            ]

        both = (slice(top - 1, layers),)
        rest = (slice(0, top - 1),)
        all_layers = (slice(0, layers),)
        first_loads = block_loads(temp, both, tpad, both, 0) + block_loads(cond, (), kpad, (), 1)
        rim_loads = block_loads(temp, rest, tpad, rest, 2) + block_loads(
            adj, all_layers, apad, all_layers, 3
        )
        loads = [None] * 4 + [
            pltpu.make_async_copy(grad, gin, in_sem.at[4]),
            pltpu.make_async_copy(obs, obs_v, in_sem.at[5]),
            pltpu.make_async_copy(map_in, map_v, in_sem.at[6]),
            pltpu.make_async_copy(weight_in, weight_v, in_sem.at[7]),
            pltpu.make_async_copy(frame_in, frame_v, in_sem.at[8]),
        ]
        for load in first_loads:
            load.start()

        barrier = pltpu.get_barrier_semaphore()
        greeted = [along(b % RING, b // RING) for b in others] + [partner] + list(sides)
        for device in greeted:
            pl.semaphore_signal(barrier, inc=1, device_id=device, device_id_type=MESH)

        for load in loads[6:] + rim_loads + loads[4:6]:
            load.start()

        inside = (slice(1, tile_cols + 1), slice(row0, row1))
        wait_bytes(tpad.at[(*both, *inside)], in_sem.at[0])
        wait_bytes(kpad.at[inside], in_sem.at[1])
        first, last = row0, row1 - 1

        def across(pad, index, at):
            return jnp.concatenate(
                [pad[(*index, u, at, slice(None))] for u in range(1, tile_cols + 1)], axis=-1
            )

        def put_line(pad, index, at, value):
            for u in range(tile_cols):
                pad[(*index, u + 1, at, slice(None))] = value[..., u * TC : (u + 1) * TC]

        def edge_column(pad, index, side):
            u, at = ((1, 0), (tile_cols, TC - 1))[side]
            return pad[(*index, u, slice(row0, row1), slice(at, at + 1))]

        rim_lane = iota((rows, LANES), 1)
        for side, row in ((0, first), (1, last)):
            ns0_send[side, 0:1] = across(tpad, (top,), slice(row, row + 1))
            ns0_send[side, 1:2] = across(kpad, (), slice(row, row + 1))
        for side in range(2):
            ew0_send[side] = jnp.where(
                rim_lane == 0, edge_column(tpad, (top,), side), edge_column(kpad, (), side)
            )

        pl.semaphore_wait(barrier, len(greeted))

        def rim_copies(ns_s, ns_r, ew_s, ew_r, ss, rs):
            copies = []
            for i in range(4):
                src, dst = (ns_s, ns_r) if i < 2 else (ew_s, ew_r)
                copies.append(
                    pltpu.make_async_remote_copy(
                        src_ref=src.at[i % 2],
                        dst_ref=dst.at[1 - i % 2],
                        send_sem=ss.at[i // 2],
                        recv_sem=rs.at[i // 2],
                        device_id=sides[i],
                        device_id_type=MESH,
                    )
                )
            return copies

        rims0 = rim_copies(ns0_send, ns0_recv, ew0_send, ew0_recv, rim0_ss, rim0_rs)
        for copy in rims0:
            copy.start()

        for load in loads[6:]:
            load.wait()
        small[0:k_blocks, 0:tiles] = map_v[...].astype(F32)
        small[k_blocks : 2 * k_blocks, 0:tiles] = weight_v[...]
        small[2 * k_blocks : 2 * k_blocks + 1, 0:tiles] = frame_v[...].astype(F32)
        columns_of = jnp.transpose(small[...])[0:tiles]
        weight = columns_of[:, k_blocks : 2 * k_blocks]
        code = columns_of[:, 0:k_blocks].astype(jnp.int32)
        plate = code >> ((tiles * n_gy).bit_length() - 1)
        far = ((plate ^ gx) >> 2) & 1
        dz = ((plate >> 3) - gx_z) & 3
        dy = (plate - gx) & 3
        block = far * PLANE + dy * RING + dz
        wish = ((code & (tiles - 1)) + 1).astype(F32)
        lane = iota((tiles, LANES), 1)
        lane_slot = iota((tiles, n_slots), 1)
        lower = jnp.where(iota((tiles, tiles), 0) > iota((tiles, tiles), 1), 1.0, 0.0)
        hits = [jnp.where(block[:, k : k + 1] == lane, 1.0, 0.0) for k in range(k_blocks)]
        before = jnp.dot(lower, jnp.concatenate(hits, axis=1), preferred_element_type=F32)
        base = jnp.zeros((1, LANES), F32)
        wanted = jnp.zeros((tiles, n_slots), F32)
        weights = [jnp.zeros((tiles, n_slots), F32) for _ in range(2)]
        ranks = []
        for k in range(k_blocks):
            earlier = before[:, k * LANES : (k + 1) * LANES] + base
            base = base + jnp.sum(hits[k], axis=0, keepdims=True)
            ranks.append(jnp.sum(hits[k] * earlier, axis=1, keepdims=True).astype(jnp.int32))
            here = block[:, k : k + 1] * CAP + ranks[k] == lane_slot
            wanted = wanted + jnp.where(here, wish[:, k : k + 1], 0.0)
        asked = jnp.sum(wanted, axis=0, keepdims=True)
        for g in range(groups):
            for f in range(2):
                at = f * half + g * LANES
                req_send[g, f : f + 1] = asked[:, at : at + LANES]

        for b in others:
            send(
                req_send.at[b // per_group],
                req_recv.at[b],
                req_ss.at[0],
                req_rs.at[0],
                along(b % RING, b // RING),
            ).start()
        for k in range(k_blocks):
            col = slice(k, k + 1)
            for h, (dense, slot) in enumerate(((dz, dy), (dy, dz))):
                at = (dense * LANES + far * (LANES // 2) + slot * CAP)[:, col] + ranks[k]
                weights[h] = weights[h] + jnp.where(at == lane_slot, weight[:, col], 0.0)
        for h in range(2):
            for d in range(RING):
                wsend[h, d] = weights[h][:, d * LANES : (d + 1) * LANES]
            wblk[h, 0] = weights[h][:, 0:LANES]
            for d in range(1, RING):
                send(
                    wsend.at[h, d], wblk.at[h, d], w_ss.at[0], w_rs.at[0], dense_peer(h, d)
                ).start()
        req_recv[0] = req_send[0]

        has_north = jnp.where(gx > 0, 1.0, 0.0)
        has_south = jnp.where(gx < n_gx - 1, 1.0, 0.0)
        has_west = jnp.where(gy > 0, 1.0, 0.0)
        has_east = jnp.where(gy < n_gy - 1, 1.0, 0.0)

        def column_rims(pad, index, source, lane_at):
            for side, has, at in ((0, has_west, 0), (1, has_east, tile_cols + 1)):
                value = source[side, :, lane_at : lane_at + 1] * has
                pad[(*index, at, slice(row0, row1))] = jnp.broadcast_to(value, (rows, LANES))

        wait_bytes(ns0_recv, rim0_rs.at[0])
        wait_bytes(ew0_recv, rim0_rs.at[1])
        above, below = slice(first - 1, first), slice(last + 1, last + 2)
        put_line(kpad, (), above, ns0_recv[0, 1:2] * has_north)
        put_line(kpad, (), below, ns0_recv[1, 1:2] * has_south)
        column_rims(kpad, (), ew0_recv, 1)
        put_line(tpad, (top,), above, ns0_recv[0, 0:1] * has_north)
        put_line(tpad, (top,), below, ns0_recv[1, 0:1] * has_south)
        column_rims(tpad, (top,), ew0_recv, 0)

        strip_lane = iota((TR, TC), 1)

        def around(pad, index, r):
            a, b = row0 + r * TR, row0 + (r + 1) * TR
            blocks = [pad[(*index, u, slice(a, b), slice(None))] for u in range(tile_cols + 2)]
            inside = blocks[1:-1]
            eastward = [pltpu.roll(x, TC - 1, 1) for x in inside] + blocks[-1:]
            westward = blocks[:1] + [pltpu.roll(x, 1, 1) for x in inside]
            e = [
                jnp.where(strip_lane == TC - 1, eastward[u + 1], eastward[u])
                for u in range(tile_cols)
            ]
            w = [
                jnp.where(strip_lane == 0, westward[u], westward[u + 1]) for u in range(tile_cols)
            ]
            return (
                jnp.concatenate(inside, axis=1),
                jnp.concatenate(e, axis=1),
                jnp.concatenate(w, axis=1),
                across(pad, index, slice(a - 1, b - 1)),
                across(pad, index, slice(a + 1, b + 1)),
            )

        for r in range(strips):
            kc, ke, kw, kn, ks = around(kpad, (), r)
            strip = slice(r * TR, (r + 1) * TR)
            faces = [0.5 * RATE_PLANE * (kc + other) for other in (ke, kw, kn, ks)]
            for i in range(4):
                coef[i, strip] = faces[i]
            tc, te, tw, tn, ts = around(tpad, (top,), r)
            under = across(tpad, (top - 1,), slice(row0 + r * TR, row0 + (r + 1) * TR))
            value = tc + RATE_VERTICAL * (under - tc)
            for face, other in zip(faces, (te, tw, tn, ts)):
                value = value + face * (other - tc)
            for u in range(tile_cols):
                tiles3[r * tile_cols + u] = value[:, u * TC : (u + 1) * TC]

        x_copies = []
        for i in range(2):
            for rr in range(TR // 2):
                x_send[i, :, rr * TC : (rr + 1) * TC] = tiles3[:, i * (TR // 2) + rr, :]
            copy = send(x_send.at[i], x_recv.at[i], x_ss.at[i], x_rs.at[i], partner)
            copy.start()
            x_copies.append(copy)

        wait_bytes(req_recv.at[1:PLANE], req_rs.at[0])
        group_lane = iota((per_group, LANES), 1) // CAP
        group_row = iota((per_group, LANES), 0)
        tile_row = iota((tiles, LANES), 0).astype(F32)
        def make_picks(f):
            picks = []
            for g in range(groups):
                block = req_recv[g * per_group : (g + 1) * per_group, f, :]
                line = jnp.sum(
                    jnp.where(group_lane == group_row, block, 0.0), axis=0, keepdims=True
                )
                picks.append(jnp.where(line - 1.0 == tile_row, 1.0, 0.0))
            pick = jnp.concatenate(picks, axis=1)
            onehot[:, f * half : (f + 1) * half] = pick
            turned = jnp.transpose(jnp.concatenate([pick, pick], axis=0)).astype(BF16)
            lhs1[f * half : (f + 1) * half] = turned

        make_picks(0)

        def plane_rows(ref, c, f, d):
            return ref.at[0, c // 2, f, d] if c % 2 == 0 else ref.at[1, c // 2, f, :, d]

        def near_rows(ref, h, d):
            return ref.at[0, :, 0, d] if h == 0 else ref.at[1, :, 0, :, d]

        slots1 = {}
        for d in range(1, RING):
            for c in range(n_chunks):
                slots1[c, 1, d] = send(
                    plane_rows(send1, c, 1, d),
                    recv1.at[c % 2, c // 2, :, 1, d],
                    s1_ss.at[0],
                    s1_rs.at[c],
                    slot_peer(c % 2, -d),
                )
            for h in range(2):
                slots1[h, 0, d] = send(
                    near_rows(send1, h, d),
                    recv1.at[h, :, :, 0, d],
                    s1_ss.at[0],
                    s1_rs.at[n_chunks + h],
                    slot_peer(h, -d),
                )

        def columns(c, count=1):
            return slice(c * wide, (c + count) * wide)

        def pack_tiles(f, pair, source):
            for i, piece in enumerate(two_parts(source)):
                rhs[i * tiles : (i + 1) * tiles, columns(pair, 2)] = piece
            for c in (pair, pair + 1):
                packed = jnp.dot(
                    lhs1[f * half : (f + 1) * half],
                    rhs[:, columns(c)],
                    preferred_element_type=F32,
                )
                send1[c % 2, c // 2, f] = packed.reshape(RING, RING, CAP, wide)
                if f == 1:
                    for d in FARTHEST_FIRST:
                        slots1[c, f, d].start()
                recv1[c % 2, c // 2, :, f, 0] = send1[c % 2, c // 2, f, 0] if c % 2 == 0 else send1[c % 2, c // 2, f, :, 0]

        for pair in (0, 2):
            pack_tiles(0, pair, x_send[pair // 2])
        for d in FARTHEST_FIRST:
            for h in range(2):
                slots1[h, 0, d].start()
        make_picks(1)

        wait_bytes(tpad.at[(*rest, *inside)], in_sem.at[2])
        wait_bytes(apad.at[(*all_layers, *inside)], in_sem.at[3])
        for side, row in ((0, first), (1, last)):
            for u in range(tile_cols):
                at = slice(u * TC, (u + 1) * TC)
                ns_send[side, 0:top, at] = tpad[0:top, u + 1, row, :]
                ns_send[side, layers : layers + top, at] = apad[0:top, u + 1, row, :]
        for side in range(2):
            packed = jnp.zeros((rows, LANES), F32)
            for l in range(top):
                packed = jnp.where(rim_lane == l, edge_column(tpad, (l,), side), packed)
                packed = jnp.where(
                    rim_lane == layers + l, edge_column(apad, (l,), side), packed
                )
            ew_send[side] = packed
        rims = rim_copies(ns_send, ns_recv, ew_send, ew_recv, rim_ss, rim_rs)
        for copy in rims:
            copy.start()

        wait_bytes(wblk.at[:, 1:RING], w_rs.at[0])
        for pair in (0, 2):
            x_copies[pair // 2].wait_recv()
            pack_tiles(1, pair, x_recv[pair // 2])

        for h in range(2):
            for d in range(RING):
                parts_of = jnp.concatenate(two_parts(wblk[h, d]), axis=0).astype(F32)
                turned = jnp.transpose(parts_of).astype(BF16)
                lhs2[h, d, :, 0 : 2 * tiles] = turned
                lhs2[h, d, :, 2 * tiles : 4 * tiles] = turned
                slot_weight = jnp.sum(wblk[h, d], axis=0, keepdims=True)
                wcol[h, d] = jnp.transpose(jnp.broadcast_to(slot_weight, (LANES, LANES)))
                hit = jnp.where(wblk[h, d] != 0.0, 1.0, 0.0).astype(BF16)
                for f in range(2):
                    piece = hit[:, f * tiles : (f + 1) * tiles]
                    wcat[h, d, f] = jnp.concatenate([piece, piece], axis=1)

        edge = jnp.zeros((rows, LANES), F32)
        apad[top, 0, row0:row1] = edge
        apad[top, tile_cols + 1, row0:row1] = edge
        put_line(apad, (top,), above, jnp.zeros((1, cols), F32))
        put_line(apad, (top,), below, jnp.zeros((1, cols), F32))

        wait_bytes(ns_recv, rim_rs.at[0])
        wait_bytes(ew_recv, rim_rs.at[1])
        for l in range(top):
            column_rims(tpad, (l,), ew_recv, l)
            column_rims(apad, (l,), ew_recv, layers + l)
        for side, has, at in ((0, has_north, first - 1), (1, has_south, last + 1)):
            for u in range(tile_cols):
                cut = slice(u * TC, (u + 1) * TC)
                tpad[0:top, u + 1, at, :] = ns_recv[side, 0:top, cut] * has
                apad[0:top, u + 1, at, :] = ns_recv[side, layers : layers + top, cut] * has

        def layer_step(l, r, total):
            strip = slice(r * TR, (r + 1) * TR)
            tc, *t_near = around(tpad, (l,), r)
            ac, *a_near = around(apad, (l,), r)
            flow = jnp.zeros_like(ac)
            for i in range(4):
                step = a_near[i] - ac
                flow = flow + coef[i, strip] * step
                total = total + (t_near[i] - tc) * step
            return ac + flow, ac, total

        def inner_layers(r):
            strip = slice(r * TR, (r + 1) * TR)
            inner = slice(row0 + r * TR, row0 + (r + 1) * TR)

            def body(l, total):
                value, ac, total = layer_step(l, r, total)
                over = across(apad, (l + 1,), inner)
                under = across(apad, (jnp.maximum(l - 1, 0),), inner)
                outv[l, strip] = value + RATE_VERTICAL * ((over - ac) + (under - ac))
                return total

            gacc[strip] = lax.fori_loop(0, top, body, jnp.zeros((TR, cols), F32))

        for r in range(0, 2):
            inner_layers(r)

        loads[4].wait()
        loads[5].wait()
        frame = columns_of[:, 2 * k_blocks : 2 * k_blocks + 1].astype(jnp.int32)
        for c in range(n_chunks):
            seen = jnp.zeros((tiles, wide), F32)
            for f in range(frames):
                seen = jnp.where(frame == f, obs_v[f, :, columns(c)], seen)
            mis[c] = -seen

        def weigh(c, d, f):
            scale = wcol[c % 2, d, f * tiles : (f + 1) * tiles]
            value = recv1[c % 2, c // 2, d, f].reshape(tiles, wide)
            value = value * jnp.concatenate([scale] * (wide // LANES), axis=1)
            return jnp.dot(
                wcat[c % 2, d, f],
                jnp.concatenate(two_parts(value), axis=0),
                preferred_element_type=F32,
            )

        parts, spread = {}, {}
        for c in range(n_chunks):
            for d in range(1, RING):
                parts[c, d] = send(
                    part.at[c, d],
                    part_recv.at[c, d],
                    p_ss.at[0],
                    p_rs.at[c],
                    dense_peer(c % 2, -d),
                )
                spread[c, d] = send(
                    mis.at[c], mis_recv.at[c, d], m_ss.at[0], m_rs.at[c], dense_peer(c % 2, d)
                )
        for c in range(n_chunks):
            if c < 2:
                wait_bytes(recv1.at[c, :, 0 : RING - 1, 0], s1_rs.at[n_chunks + c])
            for d in range(1, RING):
                part[c, d] = weigh(c, d, 0)
            mis[c] += weigh(c, 0, 0)
        for c in range(n_chunks):
            wait_bytes(recv1.at[c % 2, c // 2, 0 : RING - 1, 1], s1_rs.at[c])
            for d in FARTHEST_FIRST:
                part[c, d] += weigh(c, d, 1)
                parts[c, d].start()
            mis[c] += weigh(c, 0, 1)

        inner_layers(2)

        for c in range(n_chunks):
            wait_bytes(part_recv.at[c, 1:RING], p_rs.at[c])
            mis[c] += part_recv[c, 1] + (part_recv[c, 2] + part_recv[c, 3])
            for d in FARTHEST_FIRST:
                spread[c, d].start()
            misfit_out[:, columns(c)] = mis[c]

        inner_layers(3)

        slots2 = {}
        for d in range(1, RING):
            for c in range(n_chunks):
                slots2[c, 1, d] = send(
                    send2.at[c % 2, c // 2, :, 1, d],
                    plane_rows(recv2, c, 1, d),
                    s2_ss.at[0],
                    s2_rs.at[c],
                    slot_peer(c % 2, d),
                )
            for h in range(2):
                slots2[h, 0, d] = send(
                    send2.at[h, :, :, 0, d],
                    near_rows(recv2, h, d),
                    s2_ss.at[0],
                    s2_rs.at[n_chunks + h],
                    slot_peer(h, d),
                )
        for c in range(n_chunks):
            wait_bytes(mis_recv.at[c, 1:RING], m_rs.at[c])
            for d in range(RING):
                mh, ml = two_parts(mis_recv[c, d] if d else mis[c])
                packed = jnp.dot(
                    lhs2[c % 2, d],
                    jnp.concatenate([mh, mh, ml, ml], axis=0),
                    preferred_element_type=F32,
                )
                send2[c % 2, c // 2, d] = packed.reshape(2, RING, CAP, wide)
            for d in FARTHEST_FIRST:
                slots2[c, 1, d].start()
        for d in FARTHEST_FIRST:
            for h in range(2):
                slots2[h, 0, d].start()
        for c in range(n_chunks):
            for f in range(2):
                if c % 2 == 0:
                    recv2[c % 2, c // 2, f, 0] = send2[c % 2, c // 2, :, f, 0]
                else:
                    recv2[c % 2, c // 2, f, :, 0] = send2[c % 2, c // 2, :, f, 0]

        for r in range(4, strips):
            inner_layers(r)
        for like, sem in (
            (ns0_recv, rim0_ss.at[0]),
            (ew0_recv, rim0_ss.at[1]),
            (ns_recv, rim_ss.at[0]),
            (ew_recv, rim_ss.at[1]),
            (req_recv.at[1:PLANE], req_ss.at[0]),
            (wblk.at[:, 1:RING], w_ss.at[0]),
            (recv1.at[:, :, 0 : RING - 1], s1_ss.at[0]),
            (part.at[:, 1:RING], p_ss.at[0]),
            (part.at[:, 1:RING], m_ss.at[0]),
        ):
            wait_bytes(like, sem)
        for copy in x_copies:
            copy.wait_send()

        def gathered(c, f):
            if f == 1:
                wait_bytes(recv2.at[c % 2, c // 2, 1, 0 : RING - 1], s2_rs.at[c])
            elif c < 2:
                wait_bytes(recv2.at[c, :, 0, 0 : RING - 1], s2_rs.at[n_chunks + c])
            pick = onehot[:, f * half : (f + 1) * half].astype(BF16)
            return jnp.dot(
                jnp.concatenate([pick, pick], axis=1),
                jnp.concatenate(two_parts(recv2[c % 2, c // 2, f].reshape(half, wide)), axis=0),
                preferred_element_type=F32,
            )

        xa_copies = []
        for c in range(n_chunks):
            xa_send[c] = gathered(c, 1)
            copy = send(xa_send.at[c], xa_recv.at[c], x_ss.at[2 + c], x_rs.at[2 + c], partner)
            copy.start()
            xa_copies.append(copy)
        sums = [gathered(c, 0) for c in range(n_chunks)]
        for copy in xa_copies:
            copy.wait_recv()
        added = jnp.concatenate([sums[c] + xa_recv[c] for c in range(n_chunks)], axis=1)
        for rr in range(TR):
            tiles3[:, rr, :] = added[:, rr * TC : (rr + 1) * TC]
        for r in range(strips):
            strip = slice(r * TR, (r + 1) * TR)
            inner = slice(row0 + r * TR, row0 + (r + 1) * TR)
            extra = jnp.concatenate(
                [tiles3[r * tile_cols + u] for u in range(tile_cols)], axis=1
            )
            put_line(apad, (top,), inner, across(apad, (top,), inner) + extra)
            outv[top - 1, strip] += RATE_VERTICAL * extra

        for side, row in ((0, first), (1, last)):
            ns2_send[side] = across(apad, (top,), slice(row, row + 1))
        for side in range(2):
            ew2_send[side] = jnp.broadcast_to(edge_column(apad, (top,), side), (rows, LANES))
        rims2 = rim_copies(ns2_send, ns2_recv, ew2_send, ew2_recv, rim2_ss, rim2_rs)
        for copy in rims2:
            copy.start()
        for r in range(strips):
            strip = slice(r * TR, (r + 1) * TR)
            inner = slice(row0 + r * TR, row0 + (r + 1) * TR)
            value, ac, total = layer_step(top, r, gacc[strip])
            under = across(apad, (top - 1,), inner)
            outv[top, strip] = value + RATE_VERTICAL * (under - ac)
            gradv[strip] = gin[strip] - (0.5 * RATE_PLANE) * total
        wait_bytes(recv2.at[:, :, :, 0 : RING - 1], s2_ss.at[0])
        for copy in xa_copies:
            copy.wait_send()

        wait_bytes(ns2_recv, rim2_rs.at[0])
        wait_bytes(ew2_recv, rim2_rs.at[1])
        for side, has, row, beyond in ((0, has_north, 0, first - 1), (1, has_south, rows - 1, last + 1)):
            at = slice(row, row + 1)
            rim = ns2_recv[side] * has
            slope = across(tpad, (top,), slice(beyond, beyond + 1)) - across(
                tpad, (top,), slice(row0 + row, row0 + row + 1)
            )
            outv[top, at] += coef[2 + side, at] * rim
            gradv[at] -= (0.5 * RATE_PLANE) * slope * rim
        for side, has, face, inside, beyond, edge_lane in (
            (0, has_west, 1, 1, 0, 0),
            (1, has_east, 0, tile_cols, tile_cols + 1, TC - 1),
        ):
            at = slice((inside - 1) * TC, inside * TC)
            rim = jnp.where(rim_lane == edge_lane, ew2_recv[side] * has, 0.0)
            slope = tpad[top, beyond, row0:row1] - tpad[top, inside, row0:row1]
            outv[top, :, at] += coef[face, :, at] * rim
            gradv[:, at] -= (0.5 * RATE_PLANE) * slope * rim

        wait_bytes(ns2_recv, rim2_ss.at[0])
        wait_bytes(ew2_recv, rim2_ss.at[1])

    dma = pltpu.SemaphoreType.DMA

    def vmem(*shape, dtype=F32):
        return pltpu.VMEM(shape, dtype)

    def pair(*shape):
        return [vmem(*shape), vmem(*shape)]

    tile = TR * TC
    scratch = [
        vmem(layers, tile_cols + 2, rows + 2 * TR, TC),
        vmem(layers, tile_cols + 2, rows + 2 * TR, TC),
        vmem(tile_cols + 2, rows + 2 * TR, TC),
        vmem(rows, cols),
        vmem(frames, tiles, tile),
        vmem(4, rows, cols),
        vmem(rows, cols),
        vmem(k_blocks, tiles, dtype=jnp.int32),
        vmem(k_blocks, tiles),
        vmem(1, tiles, dtype=jnp.int32),
        *pair(2, 2, cols),
        *pair(2, rows, LANES),
        *pair(2, 2 * layers, cols),
        *pair(2, rows, LANES),
        *pair(2, 1, cols),
        *pair(2, rows, LANES),
        vmem(2 * TR, LANES),
        vmem(groups, 8, LANES),
        vmem(PLANE, 8, LANES),
        vmem(tiles, TR, TC),
        vmem(tiles, n_slots),
        vmem(n_slots, 2 * tiles, dtype=BF16),
        vmem(2 * tiles, tile, dtype=BF16),
        *pair(2, RING, tiles, LANES),
        vmem(2, RING, LANES, LANES),
        vmem(2, RING, 2, tiles, 2 * tiles, dtype=BF16),
        vmem(2, RING, LANES, 4 * tiles, dtype=BF16),
        *pair(2, tiles, tile // 2),
        *pair(n_chunks, tiles, wide),
        vmem(2, n_chunks // 2, 2, RING, RING, CAP, wide),
        vmem(2, n_chunks // 2, RING, 2, RING, CAP, wide),
        *pair(n_chunks, RING, tiles, wide),
        vmem(n_chunks, tiles, wide),
        vmem(n_chunks, RING, tiles, wide),
        vmem(2, n_chunks // 2, RING, 2, RING, CAP, wide),
        vmem(2, n_chunks // 2, 2, RING, RING, CAP, wide),
        dma((9,)),
        *[dma((2,)) for _ in range(6)],
        dma((2 + n_chunks,)), dma((2 + n_chunks,)),
        dma((1,)), dma((1,)),
        dma((1,)), dma((1,)),
        dma((1,)), dma((2 + n_chunks,)),
        dma((1,)), dma((n_chunks,)),
        dma((1,)), dma((n_chunks,)),
        dma((1,)), dma((2 + n_chunks,)),
    ]
    in_hbm = pl.BlockSpec(memory_space=pltpu.HBM)
    in_vmem = pl.BlockSpec(memory_space=pltpu.VMEM)
    return pl.pallas_call(
        kernel,
        out_shape=(
            jax.ShapeDtypeStruct((tiles, tile), F32),
            jax.ShapeDtypeStruct((layers, rows, cols), F32),
            jax.ShapeDtypeStruct((rows, cols), F32),
        ),
        in_specs=[in_hbm] * 8,
        out_specs=[in_vmem] * 3,
        scratch_shapes=scratch,
        compiler_params=pltpu.CompilerParams(
            collective_id=0, has_side_effects=True, vmem_limit_bytes=48 * 1024 * 1024
        ),
    )


def write_out(results):
    count = len(results)

    def kernel(*refs):
        copies = [
            pltpu.make_async_copy(refs[i], refs[count + i], refs[-1].at[i]) for i in range(count)
        ]
        for copy in copies:
            copy.start()
        for copy in copies:
            copy.wait()

    return pl.pallas_call(
        kernel,
        out_shape=tuple(jax.ShapeDtypeStruct(x.shape, x.dtype) for x in results),
        in_specs=[pl.BlockSpec(memory_space=pltpu.VMEM)] * count,
        out_specs=[pl.BlockSpec(memory_space=pl.ANY)] * count,
        scratch_shapes=[pltpu.SemaphoreType.DMA((count,))],
        compiler_params=pltpu.CompilerParams(vmem_limit_bytes=8 * 1024 * 1024),
    )(*results)


def solution(mesh):
    n_gx, n_gy = mesh.shape["gx"], mesh.shape["gy"]

    def local(temp, cond, adj, grad, obs, frame_index, source_map, source_weight):
        layers, rows, cols = temp.shape
        call = make_kernel(n_gx, n_gy, layers, rows, cols, obs.shape[0], source_map.shape[1])
        operands = (
            temp, cond, adj, grad, obs, frame_index[None, :], source_map.T, source_weight.T
        )
        results = call(*(pltpu.with_memory_space_constraint(x, pltpu.HBM) for x in operands))
        return write_out(results)

    placed = (
        P(None, "gx", "gy"),
        P("gx", "gy"),
        P(None, "gx", "gy"),
        P("gx", "gy"),
        P(None, ("gx", "gy"), None),
        P(("gx", "gy")),
        P(("gx", "gy"), None),
        P(("gx", "gy"), None),
    )
    return jax.shard_map(
        local,
        mesh=mesh,
        in_specs=placed,
        out_specs=(P(("gx", "gy"), None), P(None, "gx", "gy"), P("gx", "gy")),
        check_vma=False,
    )
```

```python
import jax
import jax.numpy as jnp
from jax import lax
from jax.experimental import pallas as pl
from jax.experimental.pallas import tpu as pltpu
from jax.sharding import PartitionSpec as P

TR = 8
TC = 128
CAP = 16
LANES = 128
RATE_PLANE = 0.2
RATE_VERTICAL = 0.08
MESH = pl.DeviceIdType.MESH
F32 = jnp.float32
BF16 = jnp.bfloat16


def iota(shape, dim):
    return lax.broadcasted_iota(jnp.int32, shape, dim)


def two_parts(x):
    hi = x.astype(BF16)
    lo = (x - hi.astype(F32)).astype(BF16)
    return hi, lo


RING = 4
PLANE = RING * RING
FARTHEST_FIRST = (2, 1, 3)


def make_kernel(n_gx, n_gy, layers, rows, cols, frames, k_blocks):
    tiles = (rows // TR) * (cols // TC)
    half = PLANE * CAP
    n_slots = 2 * half
    row0, row1 = TR, TR + rows
    strips = rows // TR
    tile_cols = cols // TC
    top = layers - 1
    per_group = LANES // CAP
    groups = PLANE // per_group
    others = range(1, PLANE)
    n_chunks = 4
    wide = cols // n_chunks

    def kernel(
        temp, cond, adj, grad, obs, frame_in, map_in, weight_in,
        misfit_out, outv, gradv,
        tpad, apad, kpad, gin, obs_v, coef, gacc, map_v, weight_v, frame_v,
        ns0_send, ns0_recv, ew0_send, ew0_recv,
        ns_send, ns_recv, ew_send, ew_recv,
        ns2_send, ns2_recv, ew2_send, ew2_recv,
        small, req_send, req_recv, tiles3, onehot, lhs1, rhs,
        wsend, wblk, wcat, lhs2,
        x_send, x_recv, xa_send, xa_recv,
        send1, recv1, part, part_recv, mis, mis_recv, send2, recv2,
        in_sem,
        rim0_ss, rim0_rs, rim_ss, rim_rs, rim2_ss, rim2_rs, x_ss, x_rs,
        req_ss, req_rs, w_ss, w_rs, s1_ss, s1_rs, p_ss, p_rs, m_ss, m_rs, s2_ss, s2_rs,
    ):
        gx = lax.axis_index("gx")
        gy = lax.axis_index("gy")
        gx_y = lax.rem(gx, RING)
        gx_x = lax.rem(gx // RING, 2)
        gx_z = gx // (2 * RING)
        north, south = lax.rem(gx + n_gx - 1, n_gx), lax.rem(gx + 1, n_gx)
        west, east = lax.rem(gy + n_gy - 1, n_gy), lax.rem(gy + 1, n_gy)
        sides = ({"gx": north}, {"gx": south}, {"gy": west}, {"gy": east})
        partner = {"gx": gx + RING - 2 * RING * gx_x}

        def along(dz, dy):
            z = lax.rem(gx_z + dz % RING, RING)
            y = lax.rem(gx_y + dy % RING, RING)
            return {"gx": z * (2 * RING) + gx_x * RING + y}

        def slot_peer(h, d):
            return along(0, d) if h == 0 else along(d, 0)

        def dense_peer(h, d):
            return along(d, 0) if h == 0 else along(0, d)

        def wait_bytes(like, sem):
            pltpu.make_async_copy(like, like, sem).wait()

        def send(src, dst, ss, rs, device):
            return pltpu.make_async_remote_copy(
                src_ref=src,
                dst_ref=dst,
                send_sem=ss,
                recv_sem=rs,
                device_id=device,
                device_id_type=MESH,
            )

        def block_loads(src, src_layers, pad, pad_layers, sem):
            return [
                pltpu.make_async_copy(
                    src.at[(*src_layers, slice(None), slice(u * TC, (u + 1) * TC))],
                    pad.at[(*pad_layers, u + 1, slice(row0, row1))],
                    in_sem.at[sem],
                )
                for u in range(tile_cols)
            ]

        both = (slice(top - 1, layers),)
        rest = (slice(0, top - 1),)
        all_layers = (slice(0, layers),)
        first_loads = block_loads(temp, both, tpad, both, 0) + block_loads(cond, (), kpad, (), 1)
        rim_loads = block_loads(temp, rest, tpad, rest, 2) + block_loads(
            adj, all_layers, apad, all_layers, 3
        )
        loads = [None] * 4 + [
            pltpu.make_async_copy(grad, gin, in_sem.at[4]),
            pltpu.make_async_copy(obs, obs_v, in_sem.at[5]),
            pltpu.make_async_copy(map_in, map_v, in_sem.at[6]),
            pltpu.make_async_copy(weight_in, weight_v, in_sem.at[7]),
            pltpu.make_async_copy(frame_in, frame_v, in_sem.at[8]),
        ]
        for load in first_loads:
            load.start()

        barrier = pltpu.get_barrier_semaphore()
        greeted = [along(b % RING, b // RING) for b in others] + [partner] + list(sides)
        for device in greeted:
            pl.semaphore_signal(barrier, inc=1, device_id=device, device_id_type=MESH)

        for load in loads[6:] + rim_loads + loads[4:6]:
            load.start()

        inside = (slice(1, tile_cols + 1), slice(row0, row1))
        wait_bytes(tpad.at[(*both, *inside)], in_sem.at[0])
        wait_bytes(kpad.at[inside], in_sem.at[1])
        first, last = row0, row1 - 1

        def across(pad, index, at):
            return jnp.concatenate(
                [pad[(*index, u, at, slice(None))] for u in range(1, tile_cols + 1)], axis=-1
            )

        def put_line(pad, index, at, value):
            for u in range(tile_cols):
                pad[(*index, u + 1, at, slice(None))] = value[..., u * TC : (u + 1) * TC]

        def edge_column(pad, index, side):
            u, at = ((1, 0), (tile_cols, TC - 1))[side]
            return pad[(*index, u, slice(row0, row1), slice(at, at + 1))]

        rim_lane = iota((rows, LANES), 1)
        for side, row in ((0, first), (1, last)):
            ns0_send[side, 0:1] = across(tpad, (top,), slice(row, row + 1))
            ns0_send[side, 1:2] = across(kpad, (), slice(row, row + 1))
        for side in range(2):
            ew0_send[side] = jnp.where(
                rim_lane == 0, edge_column(tpad, (top,), side), edge_column(kpad, (), side)
            )

        pl.semaphore_wait(barrier, len(greeted))

        def rim_copies(ns_s, ns_r, ew_s, ew_r, ss, rs):
            copies = []
            for i in range(4):
                src, dst = (ns_s, ns_r) if i < 2 else (ew_s, ew_r)
                copies.append(
                    pltpu.make_async_remote_copy(
                        src_ref=src.at[i % 2],
                        dst_ref=dst.at[1 - i % 2],
                        send_sem=ss.at[i // 2],
                        recv_sem=rs.at[i // 2],
                        device_id=sides[i],
                        device_id_type=MESH,
                    )
                )
            return copies

        rims0 = rim_copies(ns0_send, ns0_recv, ew0_send, ew0_recv, rim0_ss, rim0_rs)
        for copy in rims0:
            copy.start()

        for load in loads[6:]:
            load.wait()
        small[0:k_blocks, 0:tiles] = map_v[...].astype(F32)
        small[k_blocks : 2 * k_blocks, 0:tiles] = weight_v[...]
        small[2 * k_blocks : 2 * k_blocks + 1, 0:tiles] = frame_v[...].astype(F32)
        columns_of = jnp.transpose(small[...])[0:tiles]
        weight = columns_of[:, k_blocks : 2 * k_blocks]
        code = columns_of[:, 0:k_blocks].astype(jnp.int32)
        plate = code >> ((tiles * n_gy).bit_length() - 1)
        far = ((plate ^ gx) >> 2) & 1
        dz = ((plate >> 3) - gx_z) & 3
        dy = (plate - gx) & 3
        block = far * PLANE + dy * RING + dz
        wish = ((code & (tiles - 1)) + 1).astype(F32)
        lane = iota((tiles, LANES), 1)
        lane_slot = iota((tiles, n_slots), 1)
        lower = jnp.where(iota((tiles, tiles), 0) > iota((tiles, tiles), 1), 1.0, 0.0)
        hits = [jnp.where(block[:, k : k + 1] == lane, 1.0, 0.0) for k in range(k_blocks)]
        before = jnp.dot(lower, jnp.concatenate(hits, axis=1), preferred_element_type=F32)
        base = jnp.zeros((1, LANES), F32)
        wanted = jnp.zeros((tiles, n_slots), F32)
        weights = [jnp.zeros((tiles, n_slots), F32) for _ in range(2)]
        ranks = []
        for k in range(k_blocks):
            earlier = before[:, k * LANES : (k + 1) * LANES] + base
            base = base + jnp.sum(hits[k], axis=0, keepdims=True)
            ranks.append(jnp.sum(hits[k] * earlier, axis=1, keepdims=True).astype(jnp.int32))
            here = block[:, k : k + 1] * CAP + ranks[k] == lane_slot
            wanted = wanted + jnp.where(here, wish[:, k : k + 1], 0.0)
        asked = jnp.sum(wanted, axis=0, keepdims=True)
        for g in range(groups):
            for f in range(2):
                at = f * half + g * LANES
                req_send[g, f : f + 1] = asked[:, at : at + LANES]

        for b in others:
            send(
                req_send.at[b // per_group],
                req_recv.at[b],
                req_ss.at[0],
                req_rs.at[0],
                along(b % RING, b // RING),
            ).start()
        for k in range(k_blocks):
            col = slice(k, k + 1)
            for h, (dense, slot) in enumerate(((dz, dy), (dy, dz))):
                at = (dense * LANES + far * (LANES // 2) + slot * CAP)[:, col] + ranks[k]
                weights[h] = weights[h] + jnp.where(at == lane_slot, weight[:, col], 0.0)
        for h in range(2):
            for d in range(RING):
                wsend[h, d] = weights[h][:, d * LANES : (d + 1) * LANES]
            wblk[h, 0] = weights[h][:, 0:LANES]
            for d in range(1, RING):
                send(
                    wsend.at[h, d], wblk.at[h, d], w_ss.at[0], w_rs.at[0], dense_peer(h, d)
                ).start()
        req_recv[0] = req_send[0]

        has_north = jnp.where(gx > 0, 1.0, 0.0)
        has_south = jnp.where(gx < n_gx - 1, 1.0, 0.0)
        has_west = jnp.where(gy > 0, 1.0, 0.0)
        has_east = jnp.where(gy < n_gy - 1, 1.0, 0.0)

        def column_rims(pad, index, source, lane_at):
            for side, has, at in ((0, has_west, 0), (1, has_east, tile_cols + 1)):
                value = source[side, :, lane_at : lane_at + 1] * has
                pad[(*index, at, slice(row0, row1))] = jnp.broadcast_to(value, (rows, LANES))

        wait_bytes(ns0_recv, rim0_rs.at[0])
        wait_bytes(ew0_recv, rim0_rs.at[1])
        above, below = slice(first - 1, first), slice(last + 1, last + 2)
        put_line(kpad, (), above, ns0_recv[0, 1:2] * has_north)
        put_line(kpad, (), below, ns0_recv[1, 1:2] * has_south)
        column_rims(kpad, (), ew0_recv, 1)
        put_line(tpad, (top,), above, ns0_recv[0, 0:1] * has_north)
        put_line(tpad, (top,), below, ns0_recv[1, 0:1] * has_south)
        column_rims(tpad, (top,), ew0_recv, 0)

        strip_lane = iota((TR, TC), 1)

        def around(pad, index, r):
            a, b = row0 + r * TR, row0 + (r + 1) * TR
            blocks = [pad[(*index, u, slice(a, b), slice(None))] for u in range(tile_cols + 2)]
            inside = blocks[1:-1]
            eastward = [pltpu.roll(x, TC - 1, 1) for x in inside] + blocks[-1:]
            westward = blocks[:1] + [pltpu.roll(x, 1, 1) for x in inside]
            e = [
                jnp.where(strip_lane == TC - 1, eastward[u + 1], eastward[u])
                for u in range(tile_cols)
            ]
            w = [
                jnp.where(strip_lane == 0, westward[u], westward[u + 1]) for u in range(tile_cols)
            ]
            return (
                jnp.concatenate(inside, axis=1),
                jnp.concatenate(e, axis=1),
                jnp.concatenate(w, axis=1),
                across(pad, index, slice(a - 1, b - 1)),
                across(pad, index, slice(a + 1, b + 1)),
            )

        for r in range(strips):
            kc, ke, kw, kn, ks = around(kpad, (), r)
            strip = slice(r * TR, (r + 1) * TR)
            faces = [0.5 * RATE_PLANE * (kc + other) for other in (ke, kw, kn, ks)]
            for i in range(4):
                coef[i, strip] = faces[i]
            tc, te, tw, tn, ts = around(tpad, (top,), r)
            under = across(tpad, (top - 1,), slice(row0 + r * TR, row0 + (r + 1) * TR))
            value = tc + RATE_VERTICAL * (under - tc)
            for face, other in zip(faces, (te, tw, tn, ts)):
                value = value + face * (other - tc)
            for u in range(tile_cols):
                tiles3[r * tile_cols + u] = value[:, u * TC : (u + 1) * TC]

        x_copies = []
        per_chunk = wide // TC
        for i in range(n_chunks):
            for rr in range(per_chunk):
                x_send[i, :, rr * TC : (rr + 1) * TC] = tiles3[:, i * per_chunk + rr, :]
            copy = send(x_send.at[i], x_recv.at[i], x_ss.at[i], x_rs.at[i], partner)
            copy.start()
            x_copies.append(copy)

        wait_bytes(req_recv.at[1:PLANE], req_rs.at[0])
        group_lane = iota((per_group, LANES), 1) // CAP
        group_row = iota((per_group, LANES), 0)
        tile_row = iota((tiles, LANES), 0).astype(F32)
        def make_picks(f):
            picks = []
            for g in range(groups):
                block = req_recv[g * per_group : (g + 1) * per_group, f, :]
                line = jnp.sum(
                    jnp.where(group_lane == group_row, block, 0.0), axis=0, keepdims=True
                )
                picks.append(jnp.where(line - 1.0 == tile_row, 1.0, 0.0))
            pick = jnp.concatenate(picks, axis=1)
            onehot[:, f * half : (f + 1) * half] = pick
            turned = jnp.transpose(jnp.concatenate([pick, pick], axis=0)).astype(BF16)
            lhs1[f * half : (f + 1) * half] = turned

        make_picks(0)

        def plane_rows(ref, c, f, d):
            return ref.at[0, c // 2, f, d] if c % 2 == 0 else ref.at[1, c // 2, f, :, d]

        def near_rows(ref, h, d):
            return ref.at[0, :, 0, d] if h == 0 else ref.at[1, :, 0, :, d]

        slots1 = {}
        for d in range(1, RING):
            for c in range(n_chunks):
                slots1[c, 1, d] = send(
                    plane_rows(send1, c, 1, d),
                    recv1.at[c % 2, c // 2, :, 1, d],
                    s1_ss.at[0],
                    s1_rs.at[c],
                    slot_peer(c % 2, -d),
                )
            for h in range(2):
                slots1[h, 0, d] = send(
                    near_rows(send1, h, d),
                    recv1.at[h, :, :, 0, d],
                    s1_ss.at[0],
                    s1_rs.at[n_chunks + h],
                    slot_peer(h, -d),
                )

        def columns(c, count=1):
            return slice(c * wide, (c + count) * wide)

        def pack_tiles(f, c, source):
            for i, piece in enumerate(two_parts(source)):
                rhs[i * tiles : (i + 1) * tiles, columns(c)] = piece
            packed = jnp.dot(
                lhs1[f * half : (f + 1) * half],
                rhs[:, columns(c)],
                preferred_element_type=F32,
            )
            send1[c % 2, c // 2, f] = packed.reshape(RING, RING, CAP, wide)
            if f == 1:
                for d in FARTHEST_FIRST:
                    slots1[c, f, d].start()
            recv1[c % 2, c // 2, :, f, 0] = send1[c % 2, c // 2, f, 0] if c % 2 == 0 else send1[c % 2, c // 2, f, :, 0]

        for c in range(n_chunks):
            pack_tiles(0, c, x_send[c])
        for d in FARTHEST_FIRST:
            for h in range(2):
                slots1[h, 0, d].start()
        make_picks(1)

        wait_bytes(tpad.at[(*rest, *inside)], in_sem.at[2])
        wait_bytes(apad.at[(*all_layers, *inside)], in_sem.at[3])
        for side, row in ((0, first), (1, last)):
            for u in range(tile_cols):
                at = slice(u * TC, (u + 1) * TC)
                ns_send[side, 0:top, at] = tpad[0:top, u + 1, row, :]
                ns_send[side, layers : layers + top, at] = apad[0:top, u + 1, row, :]
        for side in range(2):
            packed = jnp.zeros((rows, LANES), F32)
            for l in range(top):
                packed = jnp.where(rim_lane == l, edge_column(tpad, (l,), side), packed)
                packed = jnp.where(
                    rim_lane == layers + l, edge_column(apad, (l,), side), packed
                )
            ew_send[side] = packed
        rims = rim_copies(ns_send, ns_recv, ew_send, ew_recv, rim_ss, rim_rs)
        for copy in rims:
            copy.start()

        wait_bytes(wblk.at[:, 1:RING], w_rs.at[0])
        for h in range(2):
            for d in range(RING):
                for i, piece in enumerate(two_parts(wblk[h, d])):
                    wcat[h, d, i * tiles : (i + 1) * tiles] = jnp.concatenate(
                        [piece, piece], axis=1
                    )

        for c in range(n_chunks):
            x_copies[c].wait_recv()
            pack_tiles(1, c, x_recv[c])

        for h in range(2):
            for d in range(RING):
                parts_of = jnp.concatenate(two_parts(wblk[h, d]), axis=0).astype(F32)
                turned = jnp.transpose(parts_of).astype(BF16)
                lhs2[h, d, :, 0 : 2 * tiles] = turned
                lhs2[h, d, :, 2 * tiles : 4 * tiles] = turned

        edge = jnp.zeros((rows, LANES), F32)
        apad[top, 0, row0:row1] = edge
        apad[top, tile_cols + 1, row0:row1] = edge
        put_line(apad, (top,), above, jnp.zeros((1, cols), F32))
        put_line(apad, (top,), below, jnp.zeros((1, cols), F32))

        wait_bytes(ns_recv, rim_rs.at[0])
        wait_bytes(ew_recv, rim_rs.at[1])
        for l in range(top):
            column_rims(tpad, (l,), ew_recv, l)
            column_rims(apad, (l,), ew_recv, layers + l)
        for side, has, at in ((0, has_north, first - 1), (1, has_south, last + 1)):
            for u in range(tile_cols):
                cut = slice(u * TC, (u + 1) * TC)
                tpad[0:top, u + 1, at, :] = ns_recv[side, 0:top, cut] * has
                apad[0:top, u + 1, at, :] = ns_recv[side, layers : layers + top, cut] * has

        def layer_step(l, r, total):
            strip = slice(r * TR, (r + 1) * TR)
            tc, *t_near = around(tpad, (l,), r)
            ac, *a_near = around(apad, (l,), r)
            flow = jnp.zeros_like(ac)
            for i in range(4):
                step = a_near[i] - ac
                flow = flow + coef[i, strip] * step
                total = total + (t_near[i] - tc) * step
            return ac + flow, ac, total

        def inner_layers(r):
            strip = slice(r * TR, (r + 1) * TR)
            inner = slice(row0 + r * TR, row0 + (r + 1) * TR)

            def body(l, total):
                value, ac, total = layer_step(l, r, total)
                over = across(apad, (l + 1,), inner)
                under = across(apad, (jnp.maximum(l - 1, 0),), inner)
                outv[l, strip] = value + RATE_VERTICAL * ((over - ac) + (under - ac))
                return total

            gacc[strip] = lax.fori_loop(0, top, body, jnp.zeros((TR, cols), F32))

        for r in range(0, 2):
            inner_layers(r)

        loads[4].wait()
        loads[5].wait()
        frame = columns_of[:, 2 * k_blocks : 2 * k_blocks + 1].astype(jnp.int32)
        for c in range(n_chunks):
            seen = jnp.zeros((tiles, wide), F32)
            for f in range(frames):
                seen = jnp.where(frame == f, obs_v[f, :, columns(c)], seen)
            mis[c] = -seen

        def weigh(c, d):
            both = jnp.dot(
                wcat[c % 2, d],
                jnp.concatenate(two_parts(recv1[c % 2, c // 2, d].reshape(LANES, wide)), axis=0),
                preferred_element_type=F32,
            )
            return both[0:tiles] + both[tiles : 2 * tiles]

        parts, spread = {}, {}
        for c in range(n_chunks):
            for d in range(1, RING):
                parts[c, d] = send(
                    part.at[c, d],
                    part_recv.at[c, d],
                    p_ss.at[0],
                    p_rs.at[c],
                    dense_peer(c % 2, -d),
                )
                spread[c, d] = send(
                    mis.at[c], mis_recv.at[c, d], m_ss.at[0], m_rs.at[c], dense_peer(c % 2, d)
                )
        for c in range(n_chunks):
            if c < 2:
                wait_bytes(recv1.at[c, :, 0 : RING - 1, 0], s1_rs.at[n_chunks + c])
            wait_bytes(recv1.at[c % 2, c // 2, 0 : RING - 1, 1], s1_rs.at[c])
            for d in FARTHEST_FIRST:
                part[c, d] = weigh(c, d)
                parts[c, d].start()
            mis[c] += weigh(c, 0)

        inner_layers(2)

        for c in range(n_chunks):
            wait_bytes(part_recv.at[c, 1:RING], p_rs.at[c])
            mis[c] += part_recv[c, 1] + (part_recv[c, 2] + part_recv[c, 3])
            for d in FARTHEST_FIRST:
                spread[c, d].start()
            misfit_out[:, columns(c)] = mis[c]

        inner_layers(3)

        slots2 = {}
        for d in range(1, RING):
            for c in range(n_chunks):
                slots2[c, 1, d] = send(
                    send2.at[c % 2, c // 2, :, 1, d],
                    plane_rows(recv2, c, 1, d),
                    s2_ss.at[0],
                    s2_rs.at[c],
                    slot_peer(c % 2, d),
                )
            for h in range(2):
                slots2[h, 0, d] = send(
                    send2.at[h, :, :, 0, d],
                    near_rows(recv2, h, d),
                    s2_ss.at[0],
                    s2_rs.at[n_chunks + h],
                    slot_peer(h, d),
                )
        for c in range(n_chunks):
            wait_bytes(mis_recv.at[c, 1:RING], m_rs.at[c])
            for d in range(RING):
                mh, ml = two_parts(mis_recv[c, d] if d else mis[c])
                packed = jnp.dot(
                    lhs2[c % 2, d],
                    jnp.concatenate([mh, mh, ml, ml], axis=0),
                    preferred_element_type=F32,
                )
                send2[c % 2, c // 2, d] = packed.reshape(2, RING, CAP, wide)
            for d in FARTHEST_FIRST:
                slots2[c, 1, d].start()
        for d in FARTHEST_FIRST:
            for h in range(2):
                slots2[h, 0, d].start()
        for c in range(n_chunks):
            for f in range(2):
                if c % 2 == 0:
                    recv2[c % 2, c // 2, f, 0] = send2[c % 2, c // 2, :, f, 0]
                else:
                    recv2[c % 2, c // 2, f, :, 0] = send2[c % 2, c // 2, :, f, 0]

        for r in range(4, strips):
            inner_layers(r)
        for like, sem in (
            (ns0_recv, rim0_ss.at[0]),
            (ew0_recv, rim0_ss.at[1]),
            (ns_recv, rim_ss.at[0]),
            (ew_recv, rim_ss.at[1]),
            (req_recv.at[1:PLANE], req_ss.at[0]),
            (wblk.at[:, 1:RING], w_ss.at[0]),
            (recv1.at[:, :, 0 : RING - 1], s1_ss.at[0]),
            (part.at[:, 1:RING], p_ss.at[0]),
            (part.at[:, 1:RING], m_ss.at[0]),
        ):
            wait_bytes(like, sem)
        for copy in x_copies:
            copy.wait_send()

        def gathered(c, f):
            if f == 1:
                wait_bytes(recv2.at[c % 2, c // 2, 1, 0 : RING - 1], s2_rs.at[c])
            elif c < 2:
                wait_bytes(recv2.at[c, :, 0, 0 : RING - 1], s2_rs.at[n_chunks + c])
            pick = onehot[:, f * half : (f + 1) * half].astype(BF16)
            return jnp.dot(
                jnp.concatenate([pick, pick], axis=1),
                jnp.concatenate(two_parts(recv2[c % 2, c // 2, f].reshape(half, wide)), axis=0),
                preferred_element_type=F32,
            )

        xa_copies = []
        for c in range(n_chunks):
            xa_send[c] = gathered(c, 1)
            copy = send(xa_send.at[c], xa_recv.at[c], x_ss.at[n_chunks + c], x_rs.at[n_chunks + c], partner)
            copy.start()
            xa_copies.append(copy)
        sums = [gathered(c, 0) for c in range(n_chunks)]
        for copy in xa_copies:
            copy.wait_recv()
        added = jnp.concatenate([sums[c] + xa_recv[c] for c in range(n_chunks)], axis=1)
        for rr in range(TR):
            tiles3[:, rr, :] = added[:, rr * TC : (rr + 1) * TC]
        for r in range(strips):
            strip = slice(r * TR, (r + 1) * TR)
            inner = slice(row0 + r * TR, row0 + (r + 1) * TR)
            extra = jnp.concatenate(
                [tiles3[r * tile_cols + u] for u in range(tile_cols)], axis=1
            )
            put_line(apad, (top,), inner, across(apad, (top,), inner) + extra)
            outv[top - 1, strip] += RATE_VERTICAL * extra

        for side, row in ((0, first), (1, last)):
            ns2_send[side] = across(apad, (top,), slice(row, row + 1))
        for side in range(2):
            ew2_send[side] = jnp.broadcast_to(edge_column(apad, (top,), side), (rows, LANES))
        rims2 = rim_copies(ns2_send, ns2_recv, ew2_send, ew2_recv, rim2_ss, rim2_rs)
        for copy in rims2:
            copy.start()
        for r in range(strips):
            strip = slice(r * TR, (r + 1) * TR)
            inner = slice(row0 + r * TR, row0 + (r + 1) * TR)
            value, ac, total = layer_step(top, r, gacc[strip])
            under = across(apad, (top - 1,), inner)
            outv[top, strip] = value + RATE_VERTICAL * (under - ac)
            gradv[strip] = gin[strip] - (0.5 * RATE_PLANE) * total
        wait_bytes(recv2.at[:, :, :, 0 : RING - 1], s2_ss.at[0])
        for copy in xa_copies:
            copy.wait_send()

        wait_bytes(ns2_recv, rim2_rs.at[0])
        wait_bytes(ew2_recv, rim2_rs.at[1])
        for side, has, row, beyond in ((0, has_north, 0, first - 1), (1, has_south, rows - 1, last + 1)):
            at = slice(row, row + 1)
            rim = ns2_recv[side] * has
            slope = across(tpad, (top,), slice(beyond, beyond + 1)) - across(
                tpad, (top,), slice(row0 + row, row0 + row + 1)
            )
            outv[top, at] += coef[2 + side, at] * rim
            gradv[at] -= (0.5 * RATE_PLANE) * slope * rim
        for side, has, face, inside, beyond, edge_lane in (
            (0, has_west, 1, 1, 0, 0),
            (1, has_east, 0, tile_cols, tile_cols + 1, TC - 1),
        ):
            at = slice((inside - 1) * TC, inside * TC)
            rim = jnp.where(rim_lane == edge_lane, ew2_recv[side] * has, 0.0)
            slope = tpad[top, beyond, row0:row1] - tpad[top, inside, row0:row1]
            outv[top, :, at] += coef[face, :, at] * rim
            gradv[:, at] -= (0.5 * RATE_PLANE) * slope * rim

        wait_bytes(ns2_recv, rim2_ss.at[0])
        wait_bytes(ew2_recv, rim2_ss.at[1])

    dma = pltpu.SemaphoreType.DMA

    def vmem(*shape, dtype=F32):
        return pltpu.VMEM(shape, dtype)

    def pair(*shape):
        return [vmem(*shape), vmem(*shape)]

    tile = TR * TC
    scratch = [
        vmem(layers, tile_cols + 2, rows + 2 * TR, TC),
        vmem(layers, tile_cols + 2, rows + 2 * TR, TC),
        vmem(tile_cols + 2, rows + 2 * TR, TC),
        vmem(rows, cols),
        vmem(frames, tiles, tile),
        vmem(4, rows, cols),
        vmem(rows, cols),
        vmem(k_blocks, tiles, dtype=jnp.int32),
        vmem(k_blocks, tiles),
        vmem(1, tiles, dtype=jnp.int32),
        *pair(2, 2, cols),
        *pair(2, rows, LANES),
        *pair(2, 2 * layers, cols),
        *pair(2, rows, LANES),
        *pair(2, 1, cols),
        *pair(2, rows, LANES),
        vmem(2 * TR, LANES),
        vmem(groups, 8, LANES),
        vmem(PLANE, 8, LANES),
        vmem(tiles, TR, TC),
        vmem(tiles, n_slots),
        vmem(n_slots, 2 * tiles, dtype=BF16),
        vmem(2 * tiles, tile, dtype=BF16),
        *pair(2, RING, tiles, LANES),
        vmem(2, RING, 2 * tiles, 4 * tiles, dtype=BF16),
        vmem(2, RING, LANES, 4 * tiles, dtype=BF16),
        *pair(n_chunks, tiles, wide),
        *pair(n_chunks, tiles, wide),
        vmem(2, n_chunks // 2, 2, RING, RING, CAP, wide),
        vmem(2, n_chunks // 2, RING, 2, RING, CAP, wide),
        *pair(n_chunks, RING, tiles, wide),
        vmem(n_chunks, tiles, wide),
        vmem(n_chunks, RING, tiles, wide),
        vmem(2, n_chunks // 2, RING, 2, RING, CAP, wide),
        vmem(2, n_chunks // 2, 2, RING, RING, CAP, wide),
        dma((9,)),
        *[dma((2,)) for _ in range(6)],
        dma((2 * n_chunks,)), dma((2 * n_chunks,)),
        dma((1,)), dma((1,)),
        dma((1,)), dma((1,)),
        dma((1,)), dma((2 + n_chunks,)),
        dma((1,)), dma((n_chunks,)),
        dma((1,)), dma((n_chunks,)),
        dma((1,)), dma((2 + n_chunks,)),
    ]
    in_hbm = pl.BlockSpec(memory_space=pltpu.HBM)
    in_vmem = pl.BlockSpec(memory_space=pltpu.VMEM)
    return pl.pallas_call(
        kernel,
        out_shape=(
            jax.ShapeDtypeStruct((tiles, tile), F32),
            jax.ShapeDtypeStruct((layers, rows, cols), F32),
            jax.ShapeDtypeStruct((rows, cols), F32),
        ),
        in_specs=[in_hbm] * 8,
        out_specs=[in_vmem] * 3,
        scratch_shapes=scratch,
        compiler_params=pltpu.CompilerParams(
            collective_id=0, has_side_effects=True, vmem_limit_bytes=48 * 1024 * 1024
        ),
    )


def write_out(results):
    count = len(results)

    def kernel(*refs):
        copies = [
            pltpu.make_async_copy(refs[i], refs[count + i], refs[-1].at[i]) for i in range(count)
        ]
        for copy in copies:
            copy.start()
        for copy in copies:
            copy.wait()

    return pl.pallas_call(
        kernel,
        out_shape=tuple(jax.ShapeDtypeStruct(x.shape, x.dtype) for x in results),
        in_specs=[pl.BlockSpec(memory_space=pltpu.VMEM)] * count,
        out_specs=[pl.BlockSpec(memory_space=pl.ANY)] * count,
        scratch_shapes=[pltpu.SemaphoreType.DMA((count,))],
        compiler_params=pltpu.CompilerParams(vmem_limit_bytes=8 * 1024 * 1024),
    )(*results)


def solution(mesh):
    n_gx, n_gy = mesh.shape["gx"], mesh.shape["gy"]

    def local(temp, cond, adj, grad, obs, frame_index, source_map, source_weight):
        layers, rows, cols = temp.shape
        call = make_kernel(n_gx, n_gy, layers, rows, cols, obs.shape[0], source_map.shape[1])
        operands = (
            temp, cond, adj, grad, obs, frame_index[None, :], source_map.T, source_weight.T
        )
        results = call(*(pltpu.with_memory_space_constraint(x, pltpu.HBM) for x in operands))
        return write_out(results)

    placed = (
        P(None, "gx", "gy"),
        P("gx", "gy"),
        P(None, "gx", "gy"),
        P("gx", "gy"),
        P(None, ("gx", "gy"), None),
        P(("gx", "gy")),
        P(("gx", "gy"), None),
        P(("gx", "gy"), None),
    )
    return jax.shard_map(
        local,
        mesh=mesh,
        in_specs=placed,
        out_specs=(P(("gx", "gy"), None), P(None, "gx", "gy"), P("gx", "gy")),
        check_vma=False,
    )
```
